256 devices in a mesh: lon: 8 (over x_hi, y), lat: 32 (over x_lo, z, core).
Axes of the slice: x: 4 (x_hi: 2, x_lo: 2; x = x_hi * 2 + x_lo), y: 4, z: 8, core: 2. Of those that a mesh axis runs over, the one named last changes fastest.
Arguments:
- tracer: float32 [8, 1536, 1024], P(None, 'lat', 'lon'), may hold values from -6 to 6
- salinity: float32 [8, 1536, 1024], P(None, 'lat', 'lon'), may hold values from -6 to 6
- zonal_vel: float32 [8, 1536, 1024], P(None, 'lat', 'lon'), may hold values from -4 to 4
- merid_vel: float32 [8, 1536, 1024], P(None, 'lat', 'lon'), may hold values from -4 to 4
- surface: float32 [1536, 1024], P('lat', 'lon'), may hold values from -6 to 6
- land_mask: int32 [8, 1536, 1024], P(None, 'lat', 'lon'), may hold values 0 or 1
- bottom_level: int32 [1536, 1024], P('lat', 'lon'), may hold values from 7 to 8
- tracer_adj: float32 [8, 1536, 1024], P(None, 'lat', 'lon'), may hold values from -6 to 6
- salinity_adj: float32 [8, 1536, 1024], P(None, 'lat', 'lon'), may hold values from -6 to 6
- zonal_adj: float32 [8, 1536, 1024], P(None, 'lat', 'lon'), may hold values from -6 to 6
- merid_adj: float32 [8, 1536, 1024], P(None, 'lat', 'lon'), may hold values from -6 to 6
- surface_adj: float32 [1536, 1024], P('lat', 'lon'), may hold values from -6 to 6
- stream_adj: float32 [1536, 1024], P('lat', 'lon'), may hold values from -0.625 to 0.625
Outputs:
- tracer_grad: float32 [8, 1536, 1024], P(None, 'lat', 'lon')
- salinity_grad: float32 [8, 1536, 1024], P(None, 'lat', 'lon')
- zonal_grad: float32 [8, 1536, 1024], P(None, 'lat', 'lon')
- merid_grad: float32 [8, 1536, 1024], P(None, 'lat', 'lon')
- surface_grad: float32 [1536, 1024], P('lat', 'lon')
The draws below stay inside these ranges and needn't reach their ends.
All inputs are finite; a program needn't handle non-finite values. No bound on the sum of `land_mask` on one device may be relied on, other than what follows from the above.
Results may differ from the reference program's by a relative error of at most 0.00002.
Values sent between devices are 32-bit elements; how exact they have to be, the bound alone decides.
A program may use at most 64 MiB of HBM per device.

```python
import jax
import jax.numpy as jnp
from jax import lax

LEVELS = 8
SUBCYCLES = 8
GRID_X = 1024
GRID_Y = 1536


def place_ends(result, stream_key, least, high):
    longest = result.shape.index(max(result.shape))
    spots = []
    for shift in (0, 1):
        where = [jax.random.randint(jax.random.fold_in(stream_key, axis), (), 0, length) for axis, length in enumerate(result.shape)]
        where[longest] = (where[longest] + shift) % result.shape[longest]
        spots.append(tuple(where))
    return result.at[spots[0]].set(least).at[spots[1]].set(high)


def block_levels(stream_key, extent, split, smallest, largest):
    def one(dim, shards_of):
        draws = jax.random.uniform(jax.random.fold_in(jax.random.fold_in(stream_key, 6), dim), (shards_of,), jnp.float32, smallest / len(split), largest / len(split))
        return jnp.repeat(jnp.exp(draws), extent[dim] // shards_of).reshape((-1,) + (1,) * (len(extent) - dim - 1))

    loudness = one(*split[0])
    for cut in split[1:]:
        loudness = loudness * one(*cut)
    return loudness


def bell_draw(stream_key, extent, width, most, split=(), kind=jnp.bfloat16):
    values = width * jax.random.normal(stream_key, extent, jnp.float32)
    if split:
        values = values * block_levels(stream_key, extent, split, -0.22, 0.18)
    return jnp.clip(values, -most, most).astype(kind)


def setup_inputs(seed: int = 0) -> dict:
    key_of = jax.random.split(jax.random.key(seed), 14)
    tracer = bell_draw(key_of[0], (LEVELS, GRID_Y, GRID_X), 1.0, 6.0, ((1, 32), (2, 8)), jnp.float32)
    salinity = bell_draw(key_of[1], (LEVELS, GRID_Y, GRID_X), 1.0, 6.0, ((1, 32), (2, 8)), jnp.float32)
    zonal_vel = bell_draw(key_of[2], (LEVELS, GRID_Y, GRID_X), 0.5, 4.0, ((1, 32), (2, 8)), jnp.float32)
    merid_vel = bell_draw(key_of[3], (LEVELS, GRID_Y, GRID_X), 0.5, 4.0, ((1, 32), (2, 8)), jnp.float32)
    surface = bell_draw(key_of[4], (GRID_Y, GRID_X), 1.0, 6.0, ((0, 32), (1, 8)), jnp.float32)
    land_mask = place_ends((jax.random.randint(key_of[5], (LEVELS, GRID_Y, GRID_X), 0, 64) < 63).astype(jnp.int32), jax.random.fold_in(key_of[5], 1), 0, 1)
    bottom_level = place_ends(jax.random.randint(key_of[6], (GRID_Y, GRID_X), LEVELS - 1, LEVELS + 1), jax.random.fold_in(key_of[6], 1), LEVELS - 1, LEVELS).astype(jnp.int32)
    tracer_adj = bell_draw(key_of[7], (LEVELS, GRID_Y, GRID_X), 1.0, 6.0, ((1, 32), (2, 8)), jnp.float32)
    salinity_adj = bell_draw(key_of[8], (LEVELS, GRID_Y, GRID_X), 1.0, 6.0, ((1, 32), (2, 8)), jnp.float32)
    zonal_adj = bell_draw(key_of[9], (LEVELS, GRID_Y, GRID_X), 1.0, 6.0, ((1, 32), (2, 8)), jnp.float32)
    merid_adj = bell_draw(key_of[10], (LEVELS, GRID_Y, GRID_X), 1.0, 6.0, ((1, 32), (2, 8)), jnp.float32)
    surface_adj = bell_draw(key_of[11], (GRID_Y, GRID_X), 1.0, 6.0, ((0, 32), (1, 8)), jnp.float32)
    stream_adj = bell_draw(key_of[12], (GRID_Y, GRID_X), 0.04, 0.625, ((0, 32), (1, 8)), jnp.float32)
    return dict(tracer=tracer, salinity=salinity, zonal_vel=zonal_vel, merid_vel=merid_vel, surface=surface, land_mask=land_mask, bottom_level=bottom_level, tracer_adj=tracer_adj, salinity_adj=salinity_adj, zonal_adj=zonal_adj, merid_adj=merid_adj, surface_adj=surface_adj, stream_adj=stream_adj)


ADVECT = 0.25
DIFFUSION = 0.1
HEAT_COEF = 0.5
SALT_COEF = 0.4
PRESS_COEF = 0.3
CORIOLIS = 0.3
DRAG_COEF = 0.5
DIVERGENCE = 0.5
SLOPE_COEF = 0.5
FRICTION = 0.05
THICK_COEF = 0.3

def roll_east(field):
    return jnp.roll(field, -1, axis=-1)

def roll_west(field):
    return jnp.roll(field, 1, axis=-1)

def shift_north(field):
    zeros = jnp.zeros_like(field[..., :1, :])
    return jnp.concatenate([field[..., 1:, :], zeros], axis=-2)

def shift_south(field):
    zeros = jnp.zeros_like(field[..., :1, :])
    return jnp.concatenate([zeros, field[..., :-1, :]], axis=-2)

def baroclinic(tracer, salinity, zonal_vel, merid_vel, wet, bottom, coriolis, east, west, north, south):
    levels = wet.shape[0]
    wet_east = wet * east(wet)
    wet_north = wet * north(wet)
    tracer = tracer * wet
    salinity = salinity * wet
    zonal_vel = zonal_vel * wet_east
    merid_vel = merid_vel * wet_north

    def advance(field):
        face_east = 7.0 / 12.0 * (field + east(field)) - 1.0 / 12.0 * (west(field) + east(east(field)))
        face_north = 7.0 / 12.0 * (field + north(field)) - 1.0 / 12.0 * (south(field) + north(north(field)))
        flux_east = ADVECT * zonal_vel * face_east - DIFFUSION * wet_east * (east(field) - field)
        flux_north = ADVECT * merid_vel * face_north - DIFFUSION * wet_north * (north(field) - field)
        return wet * (field - (flux_east - west(flux_east)) - (flux_north - south(flux_north)))
    tracer_new = advance(tracer)
    salt_new = advance(salinity)
    pressure = jnp.cumsum(wet * (SALT_COEF * salinity - HEAT_COEF * tracer), axis=0) / levels
    merid_at_u = 0.25 * (merid_vel + east(merid_vel) + south(merid_vel) + south(east(merid_vel)))
    zonal_at_v = 0.25 * (zonal_vel + west(zonal_vel) + north(zonal_vel) + north(west(zonal_vel)))
    zonal_new = wet_east * (zonal_vel + CORIOLIS * coriolis * merid_at_u - PRESS_COEF * (east(pressure) - pressure) - DRAG_COEF * bottom * zonal_vel)
    merid_new = wet_north * (merid_vel - CORIOLIS * coriolis * zonal_at_v - PRESS_COEF * (north(pressure) - pressure) - DRAG_COEF * bottom * merid_vel)
    return (tracer_new, salt_new, zonal_new, merid_new, zonal_vel, merid_vel)

def geometry_of(wet, east, north):
    levels = wet.shape[0]
    count_u = lax.optimization_barrier(jnp.sum(wet * east(wet), axis=0))
    count_v = lax.optimization_barrier(jnp.sum(wet * north(wet), axis=0))
    return jnp.stack([count_u / levels, count_v / levels, jnp.minimum(count_u, 1.0), jnp.minimum(count_v, 1.0), wet[0]])

def barotropic(state, forcing, geometry, east, west, north, south):
    surface, zonal_tr, merid_tr = (state[0], state[1], state[2])
    surface_new = geometry[4] * (surface - DIVERGENCE * (zonal_tr - west(zonal_tr) + (merid_tr - south(merid_tr))))
    surface_east = east(surface_new)
    surface_north = north(surface_new)
    thick_u = 1.0 + THICK_COEF * jnp.tanh(0.5 * (surface_new + surface_east))
    thick_v = 1.0 + THICK_COEF * jnp.tanh(0.5 * (surface_new + surface_north))
    zonal_new = geometry[2] * ((1.0 - FRICTION) * zonal_tr + forcing[0] - SLOPE_COEF * geometry[0] * thick_u * (surface_east - surface_new))
    merid_new = geometry[3] * ((1.0 - FRICTION) * merid_tr + forcing[1] - SLOPE_COEF * geometry[1] * thick_v * (surface_north - surface_new))
    return jnp.stack([surface_new, zonal_new, merid_new])

def finish(zonal_new, merid_new, zonal_fin, merid_fin, wet_east, wet_north, depth_u, depth_v):
    levels = zonal_new.shape[0]
    mean_u = lax.optimization_barrier(jnp.sum(zonal_new, axis=0)) / levels
    mean_v = lax.optimization_barrier(jnp.sum(merid_new, axis=0)) / levels
    zonal_out = zonal_new + wet_east * ((zonal_fin - mean_u) / jnp.maximum(depth_u, 1.0 / levels))
    merid_out = merid_new + wet_north * ((merid_fin - mean_v) / jnp.maximum(depth_v, 1.0 / levels))
    return (zonal_out, merid_out)

def reference(tracer, salinity, zonal_vel, merid_vel, surface, land_mask, bottom_level, tracer_adj, salinity_adj, zonal_adj, merid_adj, surface_adj, stream_adj):
    level_ids = jnp.arange(LEVELS, dtype=jnp.int32)[:, None, None]
    wet = jnp.where((land_mask > 0) & (level_ids < bottom_level[None]), 1.0, 0.0).astype(jnp.float32)
    bottom = jnp.where(level_ids == bottom_level[None] - 1, 1.0, 0.0).astype(jnp.float32)
    row_ids = jnp.arange(GRID_Y, dtype=jnp.int32).astype(jnp.float32)
    coriolis = -(1.0 + row_ids / GRID_Y)[:, None]
    geometry = geometry_of(wet, roll_east, shift_north)
    wet_east = wet * roll_east(wet)
    wet_north = wet * shift_north(wet)

    def forward(tracer, salinity, zonal_vel, merid_vel, surface):
        tracer_new, salt_new, zonal_new, merid_new, zonal_in, merid_in = baroclinic(tracer, salinity, zonal_vel, merid_vel, wet, bottom, coriolis, roll_east, roll_west, shift_north, shift_south)
        start_u = lax.optimization_barrier(jnp.sum(zonal_in, axis=0)) / LEVELS
        start_v = lax.optimization_barrier(jnp.sum(merid_in, axis=0)) / LEVELS
        force_u = (lax.optimization_barrier(jnp.sum(zonal_new, axis=0)) / LEVELS - start_u) / SUBCYCLES
        force_v = (lax.optimization_barrier(jnp.sum(merid_new, axis=0)) / LEVELS - start_v) / SUBCYCLES
        forcing = jnp.stack([force_u, force_v])
        state = jnp.stack([surface, start_u, start_v])
        for sub_step in range(SUBCYCLES):
            state = barotropic(state, forcing, geometry, roll_east, roll_west, shift_north, shift_south)
        zonal_out, merid_out = finish(zonal_new, merid_new, state[1], state[2], wet_east, wet_north, geometry[0], geometry[1])
        stream = jnp.cumsum(state[1], axis=0)
        return (tracer_new, salt_new, zonal_out, merid_out, state[0], stream)
    unused, pullback = jax.vjp(forward, tracer, salinity, zonal_vel, merid_vel, surface)
    return pullback((tracer_adj, salinity_adj, zonal_adj, merid_adj, surface_adj, stream_adj))
```

```python
import jax
import jax.numpy as jnp
from jax import lax
from jax.experimental import pallas as pl
from jax.experimental.pallas import tpu as pltpu
from jax.sharding import PartitionSpec as P

MESH = pl.DeviceIdType.MESH
F32 = jnp.float32
SUBCYCLES = 8
LEVELS = 8
ROWS = 48
LANES = 128
HALO = 16

ADVECT = 0.25
DIFFUSION = 0.1
HEAT_COEF = 0.5
SALT_COEF = 0.4
PRESS_COEF = 0.3
CORIOLIS = 0.3
DRAG_COEF = 0.5
DIVERGENCE = 0.5
SLOPE_COEF = 0.5
FRICTION = 0.05
THICK_COEF = 0.3

CT, CS, WU, WV, WET, AT, AS, WZ, WM = range(9)
OWN = slice(16, 64)
ZR = slice(16, 72)
MR = slice(8, 64)
TALL = 80
BODY = slice(8, 88)
MINE = slice(24, 72)
WIDE = 96
SF_H, SF_HADJ, SF_WT, SF_U, SF_V, SF_FU, SF_FV, SF_CU, SF_CV, SF_SU, SF_SV = range(11)
SIDES = ((1, 0), (-1, 0), (0, 1), (0, -1), (1, 1), (-1, 1), (1, -1), (-1, -1))


def roll(x, shift):
    return pltpu.roll(x, shift, axis=x.ndim - 1)


def lanes_of(rows):
    return lax.broadcasted_iota(jnp.int32, (rows, LANES), 1)


def pair_east(a, b):
    last = lanes_of(a.shape[0]) == LANES - 1
    ra, rb = roll(a, LANES - 1), roll(b, LANES - 1)
    return jnp.where(last, rb, ra), jnp.where(last, ra, rb)


def pair_west(a, b):
    first = lanes_of(a.shape[0]) == 0
    ra, rb = roll(a, 1), roll(b, 1)
    return jnp.where(first, rb, ra), jnp.where(first, ra, rb)


def kernel(
    nlon, nlat, inner,
    tracer, salinity, zonal, merid, surface, mask, bottom, tr_adj, sa_adj, zo_adj, me_adj, su_adj, st_adj,
    out_t, out_s, out_u, out_v, out_h,
    x, lm, bl, stv, c1, pw1, pe1, m1, rn, rs, got_s, got_n, tot, slot1, gsum, slot2, sfx,
    um0, umw, vm0, we, wew, wn, z1, z1w, mm1, mm1e, wne, tmp3, sut, svt,
    acc, acx, c2, pw2, pe2, m2, sa, sb, st, ou2, cd2, wt2, ff2, ga, gb, fg, tmpb, gg,
    in_sem, send_sem, recv_sem,
):
    lon, lat = lax.axis_index("lon"), lax.axis_index("lat")
    outer = nlat // inner

    def at(dlon, dlat):
        return (lax.rem(lon + dlon + nlon, nlon), lax.rem(lat + dlat + nlat, nlat))

    loads = []
    for src, dst in (
        (mask, lm), (bottom, bl), (st_adj, stv),
        (tracer, x.at[CT, :, OWN]), (salinity, x.at[CS, :, OWN]), (zonal, x.at[WU, :, OWN]), (merid, x.at[WV, :, OWN]),
        (tr_adj, x.at[AT, :, OWN]), (sa_adj, x.at[AS, :, OWN]), (zo_adj, x.at[WZ, :, OWN]), (me_adj, x.at[WM, :, OWN]),
        (surface, sa.at[SF_H, MINE]), (su_adj, sa.at[SF_HADJ, MINE]),
    ):
        copy = pltpu.make_async_copy(src, dst, in_sem.at[len(loads)])
        copy.start()
        loads.append(copy)

    gi, go = lax.rem(lat, inner), lat // inner
    mates = [(lon, go * inner + lax.rem(gi + d, inner)) for d in range(1, inner)]
    peers = [(lon, lax.rem(go + e, outer) * inner + gi) for e in range(1, outer)]
    around = [at(*side) for side in SIDES]

    barrier = pltpu.get_barrier_semaphore()
    for where in around + mates + peers:
        pl.semaphore_signal(barrier, inc=1, device_id=where, device_id_type=MESH)

    sent = []

    def send(src, dst, where):
        n = len(sent)
        copy = pltpu.make_async_remote_copy(
            src_ref=src, dst_ref=dst, send_sem=send_sem.at[n], recv_sem=recv_sem.at[n],
            device_id=where, device_id_type=MESH,
        )
        copy.start()
        sent.append(copy)
        return copy

    for copy in loads[:3]:
        copy.wait()
    pad = jnp.zeros((8, LANES), F32)
    tile_sum = stv[0:8]
    for r in range(1, ROWS // 8):
        tile_sum = tile_sum + stv[8 * r : 8 * r + 8]
    tot[...] = tile_sum
    pl.semaphore_wait(barrier, len(around) + len(mates) + len(peers))
    up1 = [send(tot, slot1.at[d - 1], mates[d - 1]) for d in range(1, inner)]

    for copy in loads[3:]:
        copy.wait()

    lane = lanes_of(ROWS)

    def mask_level(k, _):
        bottoms = bl[...]
        wet = jnp.where((lm[k] > 0) & (k < bottoms), 1.0, 0.0).astype(F32)
        packs = [c1[0], c1[1], c1[2]]
        for f in range(9):
            if f == WET:
                value = wet
            else:
                value = x[f, k, OWN] * wet
            x[f, k, OWN] = value
            here = lax.shift_right_logical(lane, 2) == 8 * (f % 4) + k
            packs[f // 4] = jnp.where(here, roll(value, 32 * (f % 4) + 4 * k + 2), packs[f // 4])
        for n in range(3):
            c1[n] = packs[n]
        return 0

    lax.fori_loop(0, LEVELS, mask_level, 0)

    def pack_rows(f, _):
        for k in range(LEVELS):
            rs[f, 2 * k : 2 * k + 2] = x[f, k, 16:18]
            rn[f, 2 * k : 2 * k + 2] = x[f, k, 62:64]
        return 0

    lax.fori_loop(0, 9, pack_rows, 0)
    sa[SF_WT, MINE] = x[WET, 0, OWN]
    pack = c1[2]
    for s, f in ((1, SF_H), (2, SF_HADJ), (3, SF_WT)):
        here = lax.shift_right_logical(lane, 5) == s
        pack = jnp.where(here, roll(sa[f, MINE], (32 * s + 16) % LANES), pack)
    c1[2] = pack

    LOW, HIGH = slice(0, 16), slice(32, 48)

    def exchange(c, pw, pe, first, last):
        return [
            send(c, pw.at[:, 16:64], around[0]),
            send(c, pe.at[:, 16:64], around[1]),
            send(sa.at[first:last, 56:72], sa.at[first:last, 8:24], around[2]),
            send(sa.at[first:last, 24:40], sa.at[first:last, 72:88], around[3]),
            send(c.at[:, HIGH], pw.at[:, 0:16], around[4]),
            send(c.at[:, HIGH], pe.at[:, 0:16], around[5]),
            send(c.at[:, LOW], pw.at[:, 64:80], around[6]),
            send(c.at[:, LOW], pe.at[:, 64:80], around[7]),
        ]

    phase1 = [send(rn, got_s, around[2]), send(rs, got_n, around[3])]
    phase1 += exchange(c1, pw1, pe1, 0, 3)

    sfx[0:48] = stv[...]
    for r in range(6):
        sfx[48 + 8 * r : 56 + 8 * r] = pad
    for step in (1, 2, 4, 8, 16, 32):
        moved = sfx[0:48] + sfx[step : step + 48]
        sfx[0:48] = moved
    for n in range(3):
        for p in range(2):
            st[n, p, 0:8] = pad
            st[n, p, 88:96] = pad
    for p in range(2):
        tmpb[p, 0:8] = pad
        tmpb[p, 88:96] = pad
    acc[...] = jnp.zeros_like(acc)
    acx[...] = jnp.zeros_like(acx)

    for copy in up1:
        copy.wait_recv()
    group = tot[...]
    above = jnp.zeros((8, LANES), F32)
    for d in range(1, inner):
        got = slot1[d - 1]
        group = group + got
        above = above + jnp.where(lax.rem(gi - d + inner, inner) > gi, got, 0.0)
    gsum[...] = group
    up2 = [send(gsum, slot2.at[e - 1], peers[e - 1]) for e in range(1, outer)]

    for copy in phase1:
        copy.wait_recv()
    south_here, north_here = lat > 0, lat < nlat - 1

    def unpack_rows(f, _):
        for k in range(LEVELS):
            x[f, k, 14:16] = jnp.where(south_here, got_s[f, 2 * k : 2 * k + 2], 0.0)
            x[f, k, 64:66] = jnp.where(north_here, got_n[f, 2 * k : 2 * k + 2], 0.0)
        return 0

    lax.fori_loop(0, 9, unpack_rows, 0)
    lane80 = lanes_of(80)
    rows80 = lax.broadcasted_iota(jnp.int32, (80, LANES), 0)
    inside = ((rows80 >= 16) | south_here) & ((rows80 < 64) | north_here)
    fine = (lane80 & 3) < 2
    coarse = (lane80 & 31) < 16
    for n in range(3):
        from_west = fine if n < 2 else jnp.where(lane80 < 32, fine.astype(jnp.int32), coarse.astype(jnp.int32)) > 0
        m1[n] = jnp.where(inside, jnp.where(from_west, pw1[n], pe1[n]), 0.0)

    def strip(f, k, rows):
        return roll(m1[f // 4, rows], 126 - 32 * (f % 4) - 4 * k)

    def shifted(value, rim, offset):
        ids = lanes_of(value.shape[0])
        if offset > 0:
            return roll(jnp.where(ids < offset, rim, value), LANES - offset)
        return roll(jnp.where(ids >= LANES + offset, rim, value), -offset)

    row_ids = lax.broadcasted_iota(jnp.int32, (64, LANES), 0) + (lat * ROWS - 8)
    cor = -(1.0 + row_ids.astype(F32) / (ROWS * nlat))

    EXT = slice(8, 72)

    def forward_level(k, _):
        wet = x[WET, k, EXT]
        wet_e = shifted(wet, strip(WET, k, EXT), 1)
        tmp3[EXT] = wet_e
        wet_n = x[WET, k, 9:73]
        east, north = wet * wet_e, wet * wet_n
        we[k, EXT] = east
        wn[k, EXT] = north
        wu, wv = x[WU, k, EXT], x[WV, k, EXT]
        u0 = wu * wet_e
        v0 = wv * wet_n
        uw = shifted(wu, strip(WU, k, EXT), -1) * wet
        ve = shifted(wv, strip(WV, k, EXT), 1) * tmp3[9:73]
        um0[k, EXT] = u0
        umw[k, EXT] = uw
        vm0[k, EXT] = v0
        sut[EXT] = u0 + uw
        svt[EXT] = v0 + ve
        zz = x[WZ, k, EXT] * wet_e
        mz = x[WM, k, EXT] * wet_n
        z1[k, EXT] = zz
        mm1[k, EXT] = mz
        acx[0] = acx[0] + zz
        acx[1] = acx[1] + east
        acx[2] = acx[2] + mz
        acx[3] = acx[3] + north

        t0 = SALT_COEF * x[CS, k, OWN] - HEAT_COEF * x[CT, k, OWN]
        tn = SALT_COEF * x[CS, k, 17:65] - HEAT_COEF * x[CT, k, 17:65]
        te = shifted(t0, SALT_COEF * strip(CS, k, OWN) - HEAT_COEF * strip(CT, k, OWN), 1)
        dpe = acc[4] + (te - t0)
        dpn = acc[5] + (tn - t0)
        acc[4] = dpe
        acc[5] = dpn
        own = slice(8, 56)
        drag = jnp.where(bl[...] - 1 == k, 1.0 - DRAG_COEF, 1.0)
        uo, vo = u0[own], v0[own]
        vu = (0.25 * CORIOLIS) * cor[own] * (svt[OWN] + svt[15:63])
        uv = (0.25 * CORIOLIS) * cor[own] * (sut[OWN] + sut[17:65])
        zn = uo * drag + east[own] * (vu - (PRESS_COEF / LEVELS) * dpe)
        mn = vo * drag - north[own] * (uv + (PRESS_COEF / LEVELS) * dpn)
        acc[0] = acc[0] + uo
        acc[1] = acc[1] + vo
        acc[2] = acc[2] + zn
        acc[3] = acc[3] + mn
        return 0

    tmp3[72:80] = pad
    lax.fori_loop(0, LEVELS, forward_level, 0)

    for copy in up2:
        copy.wait_recv()
    for e in range(1, outer):
        got = slot2[e - 1]
        above = above + jnp.where(lax.rem(go - e + outer, outer) > go, got, 0.0)
    above = jnp.sum(above, axis=0, keepdims=True)

    def over(num, count):
        return num / jnp.maximum(count, 1.0)

    own = slice(8, 56)
    cu, cv = acx[1, own], acx[3, own]
    surf = [
        acc[0] / LEVELS, acc[1] / LEVELS,
        (acc[2] - acc[0]) / (LEVELS * SUBCYCLES), (acc[3] - acc[1]) / (LEVELS * SUBCYCLES),
        cu, cv,
        LEVELS * over(acx[0, own], cu) + (sfx[0:48] + above),
        LEVELS * over(acx[2, own], cv),
    ]
    for n in range(2):
        pack = None
        for s in range(4):
            value = surf[4 * n + s]
            sa[SF_U + 4 * n + s, MINE] = value
            turned = roll(value, (32 * s + 16) % LANES)
            pack = turned if s == 0 else jnp.where(lax.shift_right_logical(lane, 5) == s, turned, pack)
        c2[n] = pack
    phase2 = exchange(c2, pw2, pe2, 3, 11)

    def advect_level(k, _):
        wet_rim = strip(WET, k, OWN)
        wet = x[WET, k, OWN]
        u_rim, wu = strip(WU, k, OWN), x[WU, k, OWN]
        u0, u_w = um0[k, OWN], umw[k, OWN]
        u_ww = shifted(wu, u_rim, -2) * shifted(wet, wet_rim, -1)
        u_e = shifted(wu, u_rim, 1) * shifted(wet, wet_rim, 2)
        we0, we_w = we[k, OWN], wet * shifted(wet, wet_rim, -1)
        v0, v_s, v_ss, v_n = vm0[k, OWN], vm0[k, 15:63], vm0[k, 14:62], vm0[k, 17:65]
        wn0, wn_s = wn[k, OWN], wn[k, 15:63]
        grad_u = jnp.zeros((ROWS, LANES), F32)
        grad_v = jnp.zeros((ROWS, LANES), F32)
        for c, a, out in ((CT, AT, out_t), (CS, AS, out_s)):
            a0, a_rim = x[a, k, OWN], strip(a, k, OWN)
            c0, c_rim = x[c, k, OWN], strip(c, k, OWN)
            a_e, a_ee = shifted(a0, a_rim, 1), shifted(a0, a_rim, 2)
            a_w, a_ww = shifted(a0, a_rim, -1), shifted(a0, a_rim, -2)
            d0, d_w, d_ww, d_e = a_e - a0, a0 - a_w, a_w - a_ww, a_ee - a_e
            c_e, c_ee, c_w = shifted(c0, c_rim, 1), shifted(c0, c_rim, 2), shifted(c0, c_rim, -1)
            grad_u = grad_u + d0 * ((ADVECT * 7.0 / 12.0) * (c0 + c_e) - (ADVECT / 12.0) * (c_w + c_ee))
            grad = a0 + (ADVECT * 7.0 / 12.0) * (u0 * d0 + u_w * d_w) - (ADVECT / 12.0) * (u_e * d_e + u_ww * d_ww)
            grad = grad + DIFFUSION * (we0 * d0 - we_w * d_w)
            a_n, a_nn, a_s, a_ss = x[a, k, 17:65], x[a, k, 18:66], x[a, k, 15:63], x[a, k, 14:62]
            d0, d_s, d_ss, d_n = a_n - a0, a0 - a_s, a_s - a_ss, a_nn - a_n
            c_n, c_nn, c_s = x[c, k, 17:65], x[c, k, 18:66], x[c, k, 15:63]
            grad_v = grad_v + d0 * ((ADVECT * 7.0 / 12.0) * (c0 + c_n) - (ADVECT / 12.0) * (c_s + c_nn))
            grad = grad + (ADVECT * 7.0 / 12.0) * (v0 * d0 + v_s * d_s) - (ADVECT / 12.0) * (v_n * d_n + v_ss * d_ss)
            grad = grad + DIFFUSION * (wn0 * d0 - wn_s * d_s)
            out[k] = grad
        out_u[k] = grad_u
        out_v[k] = grad_v
        wet_x = x[WET, k, EXT]
        rim_x = strip(WET, k, EXT)
        wet_ex = shifted(wet_x, rim_x, 1)
        tmp3[EXT] = wet_ex
        wet_en = tmp3[9:73]
        east_w = wet_x * shifted(wet_x, rim_x, -1)
        north_e = wet_ex * wet_en
        z_w = shifted(x[WZ, k, EXT], strip(WZ, k, EXT), -1) * wet_x
        m_e = shifted(x[WM, k, EXT], strip(WM, k, EXT), 1) * wet_en
        wew[k, EXT] = east_w
        wne[k, EXT] = north_e
        z1w[k, EXT] = z_w
        mm1e[k, EXT] = m_e
        acx[4] = acx[4] + z_w
        acx[5] = acx[5] + east_w
        acx[6] = acx[6] + m_e
        acx[7] = acx[7] + north_e
        return 0

    lax.fori_loop(0, LEVELS, advect_level, 0)

    for copy in phase2:
        copy.wait_recv()

    rim_lane = (lane80 < HALO) | (lane80 >= LANES - HALO)
    for n in range(2):
        m2[n] = jnp.where(inside, jnp.where(coarse, pw2[n], pe2[n]), 0.0)
    for f in range(11):
        source, s = (m1[2], f + 1) if f < 3 else (m2[(f - 3) // 4], (f - 3) % 4)
        sb[f] = jnp.where(rim_lane, roll(source, (LANES - 16 - 32 * s) % LANES), 0.0)

    def part(f, p):
        return jnp.where(inside, sa[f, BODY], 0.0) if p == 0 else sb[f]

    for p in range(2):
        st[0, p, BODY] = part(SF_H, p)
        st[1, p, BODY] = part(SF_U, p)
        st[2, p, BODY] = part(SF_V, p)
        wt2[p] = part(SF_WT, p)
        for d in range(2):
            count = part(SF_CU + d, p)
            opened = jnp.minimum(count, 1.0)
            ou2[d, p] = opened
            cd2[d, p] = (SLOPE_COEF / LEVELS) * count
            ff2[d, p] = opened * part(SF_FU + d, p)
            fg[d, p] = jnp.zeros((80, LANES), F32)

    BOTH = (0, 1)

    def sub_step(n, _):
        u = [st[1, p, BODY] for p in BOTH]
        v = [st[2, p, BODY] for p in BOTH]
        u_w = pair_west(*u)
        h = [
            wt2[p] * (st[0, p, BODY] - DIVERGENCE * ((u[p] - u_w[p]) + (v[p] - st[2, p, 7:87])))
            for p in BOTH
        ]
        for p in BOTH:
            st[0, p, BODY] = h[p]
        h_e = pair_east(*h)
        for p in BOTH:
            for d, old, far in ((0, u[p], h_e[p]), (1, v[p], st[0, p, 9:89])):
                slope = far - h[p]
                bend = jnp.tanh(0.5 * (h[p] + far))
                depth = cd2[d, p]
                level = depth * (1.0 + THICK_COEF * bend)
                tilt = depth * (0.5 * THICK_COEF) * (1.0 - bend * bend) * slope
                ga[n, d, p] = level - tilt
                gb[n, d, p] = level + tilt
                st[1 + d, p, BODY] = (1.0 - FRICTION) * ou2[d, p] * old + ff2[d, p] - level * slope
        return 0

    lax.fori_loop(0, SUBCYCLES, sub_step, 0)

    for p in BOTH:
        st[0, p, BODY] = part(SF_HADJ, p)
        st[1, p, BODY] = part(SF_SU, p)
        st[2, p, BODY] = part(SF_SV, p)

    def back_step(i, _):
        n = SUBCYCLES - 1 - i
        u = [ou2[0, p] * st[1, p, BODY] for p in BOTH]
        v = [ou2[1, p] * st[2, p, BODY] for p in BOTH]
        for p in BOTH:
            fg[0, p] = fg[0, p] + u[p]
            fg[1, p] = fg[1, p] + v[p]
            tmpb[p, BODY] = gb[n, 1, p] * v[p]
        b_w = pair_west(*[gb[n, 0, p] * u[p] for p in BOTH])
        h = [
            wt2[p] * (st[0, p, BODY] + (ga[n, 0, p] * u[p] - b_w[p]) + (ga[n, 1, p] * v[p] - tmpb[p, 7:87]))
            for p in BOTH
        ]
        for p in BOTH:
            st[0, p, BODY] = h[p]
        h_e = pair_east(*h)
        for p in BOTH:
            st[1, p, BODY] = (1.0 - FRICTION) * u[p] - DIVERGENCE * (h[p] - h_e[p])
            st[2, p, BODY] = (1.0 - FRICTION) * v[p] - DIVERGENCE * (h[p] - st[0, p, 9:89])
        return 0

    lax.fori_loop(0, SUBCYCLES, back_step, 0)

    out_h[...] = st[0, 0, MINE]
    window = slice(8, 72)
    force = 1.0 / (LEVELS * SUBCYCLES)
    fu, fv = fg[0, 0], fg[1, 0]
    fu_w = pair_west(fu, fg[0, 1])[0]
    fv_e = pair_east(fv, fg[1, 1])[0]
    gg[0] = force * fu[window] - over(acx[0], acx[1])
    gg[1] = force * fu_w[window] - over(acx[4], acx[5])
    gg[2] = force * fv[window] - over(acx[2], acx[3])
    gg[3] = force * fv_e[window] - over(acx[6], acx[7])
    acc[0] = (st[1, 0, MINE] - fu[16:64] / SUBCYCLES) / LEVELS
    acc[1] = (st[2, 0, MINE] - fv[16:64] / SUBCYCLES) / LEVELS

    turn = (0.25 * CORIOLIS) * cor

    def momentum_level(i, press):
        k = LEVELS - 1 - i
        z = z1[k, ZR] + we[k, ZR] * gg[0, 8:64]
        z_w = z1w[k, ZR] + wew[k, ZR] * gg[1, 8:64]
        m = mm1[k, MR] + wn[k, MR] * gg[2, 0:56]
        m_e = mm1e[k, MR] + wne[k, MR] * gg[3, 0:56]
        sut[ZR] = turn[8:64] * (z + z_w)
        svt[MR] = turn[0:56] * (m + m_e)
        tmp3[MR] = m
        z0, m0 = z[0:48], m[8:56]
        press = press + (PRESS_COEF / LEVELS) * ((z0 - z_w[0:48]) + (m0 - tmp3[15:63]))
        drag = jnp.where(bl[...] - 1 == k, 1.0 - DRAG_COEF, 1.0)
        wet = x[WET, k, OWN]
        out_t[k] = wet * (out_t[k] - HEAT_COEF * press)
        out_s[k] = wet * (out_s[k] + SALT_COEF * press)
        out_u[k] = we[k, OWN] * (out_u[k] + z0 * drag - (svt[OWN] + svt[15:63]) + acc[0])
        out_v[k] = wn[k, OWN] * (out_v[k] + m0 * drag + (sut[OWN] + sut[17:65]) + acc[1])
        return press

    lax.fori_loop(0, LEVELS, momentum_level, jnp.zeros((ROWS, LANES), F32))

    for copy in sent:
        copy.wait_send()


def solution(mesh):
    nlon, nlat = mesh.shape["lon"], mesh.shape["lat"]
    inner = next(n for n in (8, 4, 2, 1) if nlat % n == 0 and n * n <= 2 * nlat)
    outer = nlat // inner
    deep = P(None, "lat", "lon")
    flat = P("lat", "lon")

    def step(*args):
        vm = lambda *shape: pltpu.VMEM(shape, F32)
        cube = jax.ShapeDtypeStruct((LEVELS, ROWS, LANES), F32)
        plane = jax.ShapeDtypeStruct((ROWS, LANES), F32)
        level = vm(LEVELS, TALL, LANES)
        copies = 18 + inner - 1 + outer - 1
        scratch = dict(
            x=vm(9, LEVELS, TALL, LANES), lm=pltpu.VMEM((LEVELS, ROWS, LANES), jnp.int32),
            bl=pltpu.VMEM((ROWS, LANES), jnp.int32), stv=vm(ROWS, LANES),
            c1=vm(3, ROWS, LANES), pw1=vm(3, 80, LANES), pe1=vm(3, 80, LANES), m1=vm(3, 80, LANES),
            rn=vm(9, 16, LANES), rs=vm(9, 16, LANES), got_s=vm(9, 16, LANES), got_n=vm(9, 16, LANES),
            tot=vm(8, LANES), slot1=vm(max(inner - 1, 1), 8, LANES), gsum=vm(8, LANES),
            slot2=vm(max(outer - 1, 1), 8, LANES), sfx=vm(96, LANES),
            um0=level, umw=level, vm0=level, we=level, wew=level, wn=level, z1=level, z1w=level,
            mm1=level, mm1e=level, wne=level, tmp3=vm(TALL, LANES), sut=vm(TALL, LANES), svt=vm(TALL, LANES),
            acc=vm(6, ROWS, LANES), acx=vm(8, 64, LANES), c2=vm(2, ROWS, LANES), pw2=vm(2, 80, LANES),
            pe2=vm(2, 80, LANES), m2=vm(2, 80, LANES), sa=vm(11, WIDE, LANES), sb=vm(11, 80, LANES),
            st=vm(3, 2, WIDE, LANES), ou2=vm(2, 2, 80, LANES), cd2=vm(2, 2, 80, LANES), wt2=vm(2, 80, LANES),
            ff2=vm(2, 2, 80, LANES), ga=vm(SUBCYCLES, 2, 2, 80, LANES), gb=vm(SUBCYCLES, 2, 2, 80, LANES),
            fg=vm(2, 2, 80, LANES), tmpb=vm(2, WIDE, LANES), gg=vm(4, 64, LANES),
            in_sem=pltpu.SemaphoreType.DMA((13,)), send_sem=pltpu.SemaphoreType.DMA((copies,)),
            recv_sem=pltpu.SemaphoreType.DMA((copies,)),
        )

        def body(*refs):
            kernel(nlon, nlat, inner, *refs)

        return pl.pallas_call(
            body,
            out_shape=[cube, cube, cube, cube, plane],
            in_specs=[pl.BlockSpec(memory_space=pl.ANY)] * 13,
            out_specs=[pl.BlockSpec(memory_space=pltpu.VMEM)] * 5,
            scratch_shapes=list(scratch.values()),
            compiler_params=pltpu.CompilerParams(
                collective_id=0, has_side_effects=True, vmem_limit_bytes=40 * 1024 * 1024
            ),
        )(*args)

    specs = (deep, deep, deep, deep, flat, deep, flat, deep, deep, deep, deep, flat, flat)
    return jax.shard_map(
        step, mesh=mesh, in_specs=specs, out_specs=(deep, deep, deep, deep, flat), check_vma=False
    )
```

```python
import jax
import jax.numpy as jnp
from jax import lax
from jax.experimental import pallas as pl
from jax.experimental.pallas import tpu as pltpu
from jax.sharding import PartitionSpec as P

MESH = pl.DeviceIdType.MESH
F32 = jnp.float32
SUBCYCLES = 8
LEVELS = 8
ROWS = 48
LANES = 128
HALO = 16

ADVECT = 0.25
DIFFUSION = 0.1
HEAT_COEF = 0.5
SALT_COEF = 0.4
PRESS_COEF = 0.3
CORIOLIS = 0.3
DRAG_COEF = 0.5
DIVERGENCE = 0.5
SLOPE_COEF = 0.5
FRICTION = 0.05
THICK_COEF = 0.3

CT, CS, WU, WV, WET, AT, AS, WZ, WM = range(9)
OWN = slice(16, 64)
ZR = slice(16, 72)
MR = slice(8, 64)
TALL = 80
BODY = slice(8, 88)
MINE = slice(24, 72)
WIDE = 96
SF_H, SF_HADJ, SF_WT, SF_U, SF_V, SF_FU, SF_FV, SF_CU, SF_CV, SF_SU, SF_SV = range(11)
SIDES = ((1, 0), (-1, 0), (0, 1), (0, -1), (1, 1), (-1, 1), (1, -1), (-1, -1))


def roll(x, shift):
    return pltpu.roll(x, shift, axis=x.ndim - 1)


def lanes_of(rows):
    return lax.broadcasted_iota(jnp.int32, (rows, LANES), 1)


def pair_east(a, b):
    last = lanes_of(a.shape[0]) == LANES - 1
    ra, rb = roll(a, LANES - 1), roll(b, LANES - 1)
    return jnp.where(last, rb, ra), jnp.where(last, ra, rb)


def pair_west(a, b):
    first = lanes_of(a.shape[0]) == 0
    ra, rb = roll(a, 1), roll(b, 1)
    return jnp.where(first, rb, ra), jnp.where(first, ra, rb)


def kernel(
    nlon, nlat, inner,
    tracer, salinity, zonal, merid, surface, mask, bottom, tr_adj, sa_adj, zo_adj, me_adj, su_adj, st_adj,
    out_t, out_s, out_u, out_v, out_h,
    x, lm, bl, stv, c1, pw1, pe1, m1, rn, rs, got_s, got_n, tot, slot1, gsum, slot2, sfx,
    um0, umw, vm0, we, wew, wn, z1, z1w, mm1, mm1e, wne, tmp3, sut, svt,
    acc, acx, c2, pw2, pe2, m2, sa, sb, st, ou2, cd2, wt2, ff2, ga, gb, fg, tmpb, gg,
    in_sem, send_sem, recv_sem,
):
    lon, lat = lax.axis_index("lon"), lax.axis_index("lat")
    outer = nlat // inner

    def at(dlon, dlat):
        return (lax.rem(lon + dlon + nlon, nlon), lax.rem(lat + dlat + nlat, nlat))

    loads = []
    for src, dst in (
        (mask, lm), (bottom, bl), (st_adj, stv),
        (tracer, x.at[CT, :, OWN]), (salinity, x.at[CS, :, OWN]), (zonal, x.at[WU, :, OWN]), (merid, x.at[WV, :, OWN]),
        (tr_adj, x.at[AT, :, OWN]), (sa_adj, x.at[AS, :, OWN]), (zo_adj, x.at[WZ, :, OWN]), (me_adj, x.at[WM, :, OWN]),
        (surface, sa.at[SF_H, MINE]), (su_adj, sa.at[SF_HADJ, MINE]),
    ):
        copy = pltpu.make_async_copy(src, dst, in_sem.at[len(loads)])
        copy.start()
        loads.append(copy)

    gi, go = lax.rem(lat, inner), lat // inner
    mates = [(lon, go * inner + lax.rem(gi + d, inner)) for d in range(1, inner)]
    peers = [(lon, lax.rem(go + e, outer) * inner + gi) for e in range(1, outer)]
    around = [at(*side) for side in SIDES]

    barrier = pltpu.get_barrier_semaphore()
    for where in around + mates + peers:
        pl.semaphore_signal(barrier, inc=1, device_id=where, device_id_type=MESH)

    sent = []

    def send(src, dst, where):
        n = len(sent)
        copy = pltpu.make_async_remote_copy(
            src_ref=src, dst_ref=dst, send_sem=send_sem.at[n], recv_sem=recv_sem.at[n],
            device_id=where, device_id_type=MESH,
        )
        copy.start()
        sent.append(copy)
        return copy

    for copy in loads[:3]:
        copy.wait()
    pad = jnp.zeros((8, LANES), F32)
    tile_sum = stv[0:8]
    for r in range(1, ROWS // 8):
        tile_sum = tile_sum + stv[8 * r : 8 * r + 8]
    tot[...] = tile_sum
    pl.semaphore_wait(barrier, len(around) + len(mates) + len(peers))
    up1 = [send(tot, slot1.at[d - 1], mates[d - 1]) for d in range(1, inner)]

    for copy in loads[3:]:
        copy.wait()

    lane = lanes_of(ROWS)

    def mask_level(k, _):
        bottoms = bl[...]
        wet = jnp.where((lm[k] > 0) & (k < bottoms), 1.0, 0.0).astype(F32)
        packs = [c1[0], c1[1], c1[2]]
        for f in range(9):
            if f == WET:
                value = wet
            else:
                value = x[f, k, OWN] * wet
            x[f, k, OWN] = value
            here = lax.shift_right_logical(lane, 2) == 8 * (f % 4) + k
            packs[f // 4] = jnp.where(here, roll(value, 32 * (f % 4) + 4 * k + 2), packs[f // 4])
        for n in range(3):
            c1[n] = packs[n]
        return 0

    lax.fori_loop(0, LEVELS, mask_level, 0)

    def pack_rows(f, _):
        for k in range(LEVELS):
            rs[f, 2 * k : 2 * k + 2] = x[f, k, 16:18]
            rn[f, 2 * k : 2 * k + 2] = x[f, k, 62:64]
        return 0

    lax.fori_loop(0, 9, pack_rows, 0)
    sa[SF_WT, MINE] = x[WET, 0, OWN]
    pack = c1[2]
    for s, f in ((1, SF_H), (2, SF_HADJ), (3, SF_WT)):
        here = lax.shift_right_logical(lane, 5) == s
        pack = jnp.where(here, roll(sa[f, MINE], (32 * s + 16) % LANES), pack)
    c1[2] = pack

    LOW, HIGH = slice(0, 16), slice(32, 48)

    def exchange(c, pw, pe, first, last):
        return [
            send(c, pw.at[:, 16:64], around[0]),
            send(c, pe.at[:, 16:64], around[1]),
            send(sa.at[first:last, 56:72], sa.at[first:last, 8:24], around[2]),
            send(sa.at[first:last, 24:40], sa.at[first:last, 72:88], around[3]),
            send(c.at[:, HIGH], pw.at[:, 0:16], around[4]),
            send(c.at[:, HIGH], pe.at[:, 0:16], around[5]),
            send(c.at[:, LOW], pw.at[:, 64:80], around[6]),
            send(c.at[:, LOW], pe.at[:, 64:80], around[7]),
        ]

    phase1 = [send(rn, got_s, around[2]), send(rs, got_n, around[3])]
    phase1 += exchange(c1, pw1, pe1, 0, 3)

    sfx[0:48] = stv[...]
    for r in range(6):
        sfx[48 + 8 * r : 56 + 8 * r] = pad
    for step in (1, 2, 4, 8, 16, 32):
        moved = sfx[0:48] + sfx[step : step + 48]
        sfx[0:48] = moved
    for n in range(3):
        for p in range(2):
            st[n, p, 0:8] = pad
            st[n, p, 88:96] = pad
    for p in range(2):
        tmpb[p, 0:8] = pad
        tmpb[p, 88:96] = pad
    acc[...] = jnp.zeros_like(acc)
    acx[...] = jnp.zeros_like(acx)

    for copy in up1:
        copy.wait_recv()
    group = tot[...]
    above = jnp.zeros((8, LANES), F32)
    for d in range(1, inner):
        got = slot1[d - 1]
        group = group + got
        above = above + jnp.where(lax.rem(gi - d + inner, inner) > gi, got, 0.0)
    gsum[...] = group
    up2 = [send(gsum, slot2.at[e - 1], peers[e - 1]) for e in range(1, outer)]

    for copy in phase1:
        copy.wait_recv()
    south_here, north_here = lat > 0, lat < nlat - 1

    def unpack_rows(f, _):
        for k in range(LEVELS):
            x[f, k, 14:16] = jnp.where(south_here, got_s[f, 2 * k : 2 * k + 2], 0.0)
            x[f, k, 64:66] = jnp.where(north_here, got_n[f, 2 * k : 2 * k + 2], 0.0)
        return 0

    lax.fori_loop(0, 9, unpack_rows, 0)
    lane80 = lanes_of(80)
    rows80 = lax.broadcasted_iota(jnp.int32, (80, LANES), 0)
    inside = ((rows80 >= 16) | south_here) & ((rows80 < 64) | north_here)
    fine = (lane80 & 3) < 2
    coarse = (lane80 & 31) < 16
    for n in range(3):
        from_west = fine if n < 2 else jnp.where(lane80 < 32, fine.astype(jnp.int32), coarse.astype(jnp.int32)) > 0
        m1[n] = jnp.where(inside, jnp.where(from_west, pw1[n], pe1[n]), 0.0)

    def strip(f, k, rows):
        return roll(m1[f // 4, rows], 126 - 32 * (f % 4) - 4 * k)

    def shifted(value, rim, offset):
        ids = lanes_of(value.shape[0])
        if offset > 0:
            return roll(jnp.where(ids < offset, rim, value), LANES - offset)
        return roll(jnp.where(ids >= LANES + offset, rim, value), -offset)

    row_ids = lax.broadcasted_iota(jnp.int32, (64, LANES), 0) + (lat * ROWS - 8)
    cor = -(1.0 + row_ids.astype(F32) / (ROWS * nlat))

    EXT = slice(8, 72)

    def forward_level(k, _):
        wet = x[WET, k, EXT]
        wet_e = shifted(wet, strip(WET, k, EXT), 1)
        tmp3[EXT] = wet_e
        wet_n = x[WET, k, 9:73]
        east, north = wet * wet_e, wet * wet_n
        we[k, EXT] = east
        wn[k, EXT] = north
        wu, wv = x[WU, k, EXT], x[WV, k, EXT]
        u0 = wu * wet_e
        v0 = wv * wet_n
        uw = shifted(wu, strip(WU, k, EXT), -1) * wet
        ve = shifted(wv, strip(WV, k, EXT), 1) * tmp3[9:73]
        um0[k, EXT] = u0
        umw[k, EXT] = uw
        vm0[k, EXT] = v0
        sut[EXT] = u0 + uw
        svt[EXT] = v0 + ve
        zz = x[WZ, k, EXT] * wet_e
        mz = x[WM, k, EXT] * wet_n
        z1[k, EXT] = zz
        mm1[k, EXT] = mz
        acx[0] = acx[0] + zz
        acx[1] = acx[1] + east
        acx[2] = acx[2] + mz
        acx[3] = acx[3] + north

        t0 = SALT_COEF * x[CS, k, OWN] - HEAT_COEF * x[CT, k, OWN]
        tn = SALT_COEF * x[CS, k, 17:65] - HEAT_COEF * x[CT, k, 17:65]
        te = shifted(t0, SALT_COEF * strip(CS, k, OWN) - HEAT_COEF * strip(CT, k, OWN), 1)
        dpe = acc[4] + (te - t0)
        dpn = acc[5] + (tn - t0)
        acc[4] = dpe
        acc[5] = dpn
        own = slice(8, 56)
        drag = jnp.where(bl[...] - 1 == k, 1.0 - DRAG_COEF, 1.0)
        uo, vo = u0[own], v0[own]
        vu = (0.25 * CORIOLIS) * cor[own] * (svt[OWN] + svt[15:63])
        uv = (0.25 * CORIOLIS) * cor[own] * (sut[OWN] + sut[17:65])
        zn = uo * drag + east[own] * (vu - (PRESS_COEF / LEVELS) * dpe)
        mn = vo * drag - north[own] * (uv + (PRESS_COEF / LEVELS) * dpn)
        acc[0] = acc[0] + uo
        acc[1] = acc[1] + vo
        acc[2] = acc[2] + zn
        acc[3] = acc[3] + mn
        return 0

    tmp3[72:80] = pad
    lax.fori_loop(0, LEVELS, forward_level, 0)

    for copy in up2:
        copy.wait_recv()
    for e in range(1, outer):
        got = slot2[e - 1]
        above = above + jnp.where(lax.rem(go - e + outer, outer) > go, got, 0.0)
    above = jnp.sum(above, axis=0, keepdims=True)

    def over(num, count):
        return num / jnp.maximum(count, 1.0)

    own = slice(8, 56)
    cu, cv = acx[1, own], acx[3, own]
    surf = [
        acc[0] / LEVELS, acc[1] / LEVELS,
        (acc[2] - acc[0]) / (LEVELS * SUBCYCLES), (acc[3] - acc[1]) / (LEVELS * SUBCYCLES),
        cu, cv,
        LEVELS * over(acx[0, own], cu) + (sfx[0:48] + above),
        LEVELS * over(acx[2, own], cv),
    ]
    for n in range(2):
        pack = None
        for s in range(4):
            value = surf[4 * n + s]
            sa[SF_U + 4 * n + s, MINE] = value
            turned = roll(value, (32 * s + 16) % LANES)
            pack = turned if s == 0 else jnp.where(lax.shift_right_logical(lane, 5) == s, turned, pack)
        c2[n] = pack
    phase2 = exchange(c2, pw2, pe2, 3, 11)

    def advect_level(k, _):
        wet_rim = strip(WET, k, OWN)
        wet = x[WET, k, OWN]
        u_rim, wu = strip(WU, k, OWN), x[WU, k, OWN]
        u0, u_w = um0[k, OWN], umw[k, OWN]
        u_ww = shifted(wu, u_rim, -2) * shifted(wet, wet_rim, -1)
        u_e = shifted(wu, u_rim, 1) * shifted(wet, wet_rim, 2)
        we0, we_w = we[k, OWN], wet * shifted(wet, wet_rim, -1)
        v0, v_s, v_ss, v_n = vm0[k, OWN], vm0[k, 15:63], vm0[k, 14:62], vm0[k, 17:65]
        wn0, wn_s = wn[k, OWN], wn[k, 15:63]
        grad_u = jnp.zeros((ROWS, LANES), F32)
        grad_v = jnp.zeros((ROWS, LANES), F32)
        for c, a, out in ((CT, AT, out_t), (CS, AS, out_s)):
            a0, a_rim = x[a, k, OWN], strip(a, k, OWN)
            c0, c_rim = x[c, k, OWN], strip(c, k, OWN)
            a_e, a_ee = shifted(a0, a_rim, 1), shifted(a0, a_rim, 2)
            a_w, a_ww = shifted(a0, a_rim, -1), shifted(a0, a_rim, -2)
            d0, d_w, d_ww, d_e = a_e - a0, a0 - a_w, a_w - a_ww, a_ee - a_e
            c_e, c_ee, c_w = shifted(c0, c_rim, 1), shifted(c0, c_rim, 2), shifted(c0, c_rim, -1)
            grad_u = grad_u + d0 * ((ADVECT * 7.0 / 12.0) * (c0 + c_e) - (ADVECT / 12.0) * (c_w + c_ee))
            grad = a0 + (ADVECT * 7.0 / 12.0) * (u0 * d0 + u_w * d_w) - (ADVECT / 12.0) * (u_e * d_e + u_ww * d_ww)
            grad = grad + DIFFUSION * (we0 * d0 - we_w * d_w)
            a_n, a_nn, a_s, a_ss = x[a, k, 17:65], x[a, k, 18:66], x[a, k, 15:63], x[a, k, 14:62]
            d0, d_s, d_ss, d_n = a_n - a0, a0 - a_s, a_s - a_ss, a_nn - a_n
            c_n, c_nn, c_s = x[c, k, 17:65], x[c, k, 18:66], x[c, k, 15:63]
            grad_v = grad_v + d0 * ((ADVECT * 7.0 / 12.0) * (c0 + c_n) - (ADVECT / 12.0) * (c_s + c_nn))
            grad = grad + (ADVECT * 7.0 / 12.0) * (v0 * d0 + v_s * d_s) - (ADVECT / 12.0) * (v_n * d_n + v_ss * d_ss)
            grad = grad + DIFFUSION * (wn0 * d0 - wn_s * d_s)
            out[k] = grad
        out_u[k] = grad_u
        out_v[k] = grad_v
        wet_x = x[WET, k, EXT]
        rim_x = strip(WET, k, EXT)
        wet_ex = shifted(wet_x, rim_x, 1)
        tmp3[EXT] = wet_ex
        wet_en = tmp3[9:73]
        east_w = wet_x * shifted(wet_x, rim_x, -1)
        north_e = wet_ex * wet_en
        z_w = shifted(x[WZ, k, EXT], strip(WZ, k, EXT), -1) * wet_x
        m_e = shifted(x[WM, k, EXT], strip(WM, k, EXT), 1) * wet_en
        wew[k, EXT] = east_w
        wne[k, EXT] = north_e
        z1w[k, EXT] = z_w
        mm1e[k, EXT] = m_e
        acx[4] = acx[4] + z_w
        acx[5] = acx[5] + east_w
        acx[6] = acx[6] + m_e
        acx[7] = acx[7] + north_e
        return 0

    lax.fori_loop(0, LEVELS, advect_level, 0)

    for copy in phase2:
        copy.wait_recv()

    rim_lane = (lane80 < HALO) | (lane80 >= LANES - HALO)
    for n in range(2):
        m2[n] = jnp.where(inside, jnp.where(coarse, pw2[n], pe2[n]), 0.0)
    for f in range(11):
        source, s = (m1[2], f + 1) if f < 3 else (m2[(f - 3) // 4], (f - 3) % 4)
        sb[f] = jnp.where(rim_lane, roll(source, (LANES - 16 - 32 * s) % LANES), 0.0)

    def part(f, p):
        return jnp.where(inside, sa[f, BODY], 0.0) if p == 0 else sb[f]

    for p in range(2):
        st[0, p, BODY] = part(SF_H, p)
        st[1, p, BODY] = part(SF_U, p)
        st[2, p, BODY] = part(SF_V, p)
        wt2[p] = part(SF_WT, p)
        for d in range(2):
            count = part(SF_CU + d, p)
            opened = jnp.minimum(count, 1.0)
            ou2[d, p] = opened
            cd2[d, p] = (SLOPE_COEF / LEVELS) * count
            ff2[d, p] = opened * part(SF_FU + d, p)
            fg[d, p] = jnp.zeros((80, LANES), F32)

    BOTH = (0, 1)

    def sub_step(n, _):
        u = [st[1, p, BODY] for p in BOTH]
        v = [st[2, p, BODY] for p in BOTH]
        u_w = pair_west(*u)
        h = [
            wt2[p] * (st[0, p, BODY] - DIVERGENCE * ((u[p] - u_w[p]) + (v[p] - st[2, p, 7:87])))
            for p in BOTH
        ]
        for p in BOTH:
            st[0, p, BODY] = h[p]
        h_e = pair_east(*h)
        for p in BOTH:
            for d, old, far in ((0, u[p], h_e[p]), (1, v[p], st[0, p, 9:89])):
                slope = far - h[p]
                bend = jnp.tanh(0.5 * (h[p] + far))
                depth = cd2[d, p]
                level = depth * (1.0 + THICK_COEF * bend)
                tilt = depth * (0.5 * THICK_COEF) * (1.0 - bend * bend) * slope
                ga[n, d, p] = level - tilt
                gb[n, d, p] = level + tilt
                st[1 + d, p, BODY] = (1.0 - FRICTION) * ou2[d, p] * old + ff2[d, p] - level * slope
        return 0

    lax.fori_loop(0, SUBCYCLES, sub_step, 0)

    for p in BOTH:
        st[0, p, BODY] = part(SF_HADJ, p)
        st[1, p, BODY] = part(SF_SU, p)
        st[2, p, BODY] = part(SF_SV, p)

    def back_step(i, _):
        n = SUBCYCLES - 1 - i
        u = [ou2[0, p] * st[1, p, BODY] for p in BOTH]
        v = [ou2[1, p] * st[2, p, BODY] for p in BOTH]
        for p in BOTH:
            fg[0, p] = fg[0, p] + u[p]
            fg[1, p] = fg[1, p] + v[p]
            tmpb[p, BODY] = gb[n, 1, p] * v[p]
        b_w = pair_west(*[gb[n, 0, p] * u[p] for p in BOTH])
        h = [
            wt2[p] * (st[0, p, BODY] + (ga[n, 0, p] * u[p] - b_w[p]) + (ga[n, 1, p] * v[p] - tmpb[p, 7:87]))
            for p in BOTH
        ]
        for p in BOTH:
            st[0, p, BODY] = h[p]
        h_e = pair_east(*h)
        for p in BOTH:
            st[1, p, BODY] = (1.0 - FRICTION) * u[p] - DIVERGENCE * (h[p] - h_e[p])
            st[2, p, BODY] = (1.0 - FRICTION) * v[p] - DIVERGENCE * (h[p] - st[0, p, 9:89])
        return 0

    lax.fori_loop(0, SUBCYCLES, back_step, 0)

    out_h[...] = st[0, 0, MINE]
    window = slice(8, 72)
    force = 1.0 / (LEVELS * SUBCYCLES)
    fu, fv = fg[0, 0], fg[1, 0]
    fu_w = pair_west(fu, fg[0, 1])[0]
    fv_e = pair_east(fv, fg[1, 1])[0]
    gg[0] = force * fu[window] - over(acx[0], acx[1])
    gg[1] = force * fu_w[window] - over(acx[4], acx[5])
    gg[2] = force * fv[window] - over(acx[2], acx[3])
    gg[3] = force * fv_e[window] - over(acx[6], acx[7])
    acc[0] = (st[1, 0, MINE] - fu[16:64] / SUBCYCLES) / LEVELS
    acc[1] = (st[2, 0, MINE] - fv[16:64] / SUBCYCLES) / LEVELS

    turn = (0.25 * CORIOLIS) * cor

    def momentum_level(i, press):
        k = LEVELS - 1 - i
        z = z1[k, ZR] + we[k, ZR] * gg[0, 8:64]
        z_w = z1w[k, ZR] + wew[k, ZR] * gg[1, 8:64]
        m = mm1[k, MR] + wn[k, MR] * gg[2, 0:56]
        m_e = mm1e[k, MR] + wne[k, MR] * gg[3, 0:56]
        sut[ZR] = turn[8:64] * (z + z_w)
        svt[MR] = turn[0:56] * (m + m_e)
        tmp3[MR] = m
        z0, m0 = z[0:48], m[8:56]
        press = press + (PRESS_COEF / LEVELS) * ((z0 - z_w[0:48]) + (m0 - tmp3[15:63]))
        drag = jnp.where(bl[...] - 1 == k, 1.0 - DRAG_COEF, 1.0)
        wet = x[WET, k, OWN]
        out_t[k] = wet * (out_t[k] - HEAT_COEF * press)
        out_s[k] = wet * (out_s[k] + SALT_COEF * press)
        out_u[k] = we[k, OWN] * (out_u[k] + z0 * drag - (svt[OWN] + svt[15:63]) + acc[0])
        out_v[k] = wn[k, OWN] * (out_v[k] + m0 * drag + (sut[OWN] + sut[17:65]) + acc[1])
        return press

    lax.fori_loop(0, LEVELS, momentum_level, jnp.zeros((ROWS, LANES), F32))

    for copy in sent:
        copy.wait_send()


def store_kernel(*refs):
    sources, targets, sem = refs[:5], refs[5:10], refs[10]
    copies = [pltpu.make_async_copy(a, b, sem.at[n]) for n, (a, b) in enumerate(zip(sources, targets))]
    for copy in copies:
        copy.start()
    for copy in copies:
        copy.wait()


def solution(mesh):
    nlon, nlat = mesh.shape["lon"], mesh.shape["lat"]
    inner = next(n for n in (8, 4, 2, 1) if nlat % n == 0 and n * n <= 2 * nlat)
    outer = nlat // inner
    deep = P(None, "lat", "lon")
    flat = P("lat", "lon")

    def step(*args):
        vm = lambda *shape: pltpu.VMEM(shape, F32)
        cube = jax.ShapeDtypeStruct((LEVELS, ROWS, LANES), F32)
        plane = jax.ShapeDtypeStruct((ROWS, LANES), F32)
        level = vm(LEVELS, TALL, LANES)
        copies = 18 + inner - 1 + outer - 1
        scratch = dict(
            x=vm(9, LEVELS, TALL, LANES), lm=pltpu.VMEM((LEVELS, ROWS, LANES), jnp.int32),
            bl=pltpu.VMEM((ROWS, LANES), jnp.int32), stv=vm(ROWS, LANES),
            c1=vm(3, ROWS, LANES), pw1=vm(3, 80, LANES), pe1=vm(3, 80, LANES), m1=vm(3, 80, LANES),
            rn=vm(9, 16, LANES), rs=vm(9, 16, LANES), got_s=vm(9, 16, LANES), got_n=vm(9, 16, LANES),
            tot=vm(8, LANES), slot1=vm(max(inner - 1, 1), 8, LANES), gsum=vm(8, LANES),
            slot2=vm(max(outer - 1, 1), 8, LANES), sfx=vm(96, LANES),
            um0=level, umw=level, vm0=level, we=level, wew=level, wn=level, z1=level, z1w=level,
            mm1=level, mm1e=level, wne=level, tmp3=vm(TALL, LANES), sut=vm(TALL, LANES), svt=vm(TALL, LANES),
            acc=vm(6, ROWS, LANES), acx=vm(8, 64, LANES), c2=vm(2, ROWS, LANES), pw2=vm(2, 80, LANES),
            pe2=vm(2, 80, LANES), m2=vm(2, 80, LANES), sa=vm(11, WIDE, LANES), sb=vm(11, 80, LANES),
            st=vm(3, 2, WIDE, LANES), ou2=vm(2, 2, 80, LANES), cd2=vm(2, 2, 80, LANES), wt2=vm(2, 80, LANES),
            ff2=vm(2, 2, 80, LANES), ga=vm(SUBCYCLES, 2, 2, 80, LANES), gb=vm(SUBCYCLES, 2, 2, 80, LANES),
            fg=vm(2, 2, 80, LANES), tmpb=vm(2, WIDE, LANES), gg=vm(4, 64, LANES),
            in_sem=pltpu.SemaphoreType.DMA((13,)), send_sem=pltpu.SemaphoreType.DMA((copies,)),
            recv_sem=pltpu.SemaphoreType.DMA((copies,)),
        )

        def body(*refs):
            kernel(nlon, nlat, inner, *refs)

        parts = pl.pallas_call(
            body,
            out_shape=[cube, cube, cube, cube, plane],
            in_specs=[pl.BlockSpec(memory_space=pltpu.HBM)] * 13,
            out_specs=[pl.BlockSpec(memory_space=pltpu.VMEM)] * 5,
            scratch_shapes=list(scratch.values()),
            compiler_params=pltpu.CompilerParams(
                collective_id=0, has_side_effects=True, vmem_limit_bytes=40 * 1024 * 1024
            ),
        )(*(pltpu.with_memory_space_constraint(a, pltpu.HBM) for a in args))
        return pl.pallas_call(
            store_kernel,
            out_shape=[cube, cube, cube, cube, plane],
            in_specs=[pl.BlockSpec(memory_space=pltpu.VMEM)] * 5,
            out_specs=[pl.BlockSpec(memory_space=pltpu.HBM)] * 5,
            scratch_shapes=[pltpu.SemaphoreType.DMA((5,))],
        )(*parts)

    specs = (deep, deep, deep, deep, flat, deep, flat, deep, deep, deep, deep, flat, flat)
    return jax.shard_map(
        step, mesh=mesh, in_specs=specs, out_specs=(deep, deep, deep, deep, flat), check_vma=False
    )
```

```python
import jax
import jax.numpy as jnp
from jax import lax
from jax.experimental import pallas as pl
from jax.experimental.pallas import tpu as pltpu
from jax.sharding import PartitionSpec as P

MESH = pl.DeviceIdType.MESH
F32 = jnp.float32
SUBCYCLES = 8
LEVELS = 8
ROWS = 48
LANES = 128
HALO = 16

ADVECT = 0.25
DIFFUSION = 0.1
HEAT_COEF = 0.5
SALT_COEF = 0.4
PRESS_COEF = 0.3
CORIOLIS = 0.3
DRAG_COEF = 0.5
DIVERGENCE = 0.5
SLOPE_COEF = 0.5
FRICTION = 0.05
THICK_COEF = 0.3

CT, CS, WU, WV, WET, AT, AS, WZ, WM = range(9)
PACK = ((0, 0), (0, 1), (0, 2), (0, 3), (1, 0), (2, 0), (2, 1), (2, 2), (2, 3))
OWN = slice(16, 64)
ZR = slice(16, 72)
MR = slice(8, 64)
TALL = 80
BODY = slice(8, 88)
MINE = slice(24, 72)
WIDE = 96
SF_H, SF_HADJ, SF_WT, SF_U, SF_V, SF_FU, SF_FV, SF_CU, SF_CV, SF_SU, SF_SV = range(11)
SIDES = ((1, 0), (-1, 0), (0, 1), (0, -1), (1, 1), (-1, 1), (1, -1), (-1, -1))


def roll(x, shift):
    return pltpu.roll(x, shift, axis=x.ndim - 1)


def lanes_of(rows):
    return lax.broadcasted_iota(jnp.int32, (rows, LANES), 1)


def pair_east(a, b):
    last = lanes_of(a.shape[0]) == LANES - 1
    ra, rb = roll(a, LANES - 1), roll(b, LANES - 1)
    return jnp.where(last, rb, ra), jnp.where(last, ra, rb)


def pair_west(a, b):
    first = lanes_of(a.shape[0]) == 0
    ra, rb = roll(a, 1), roll(b, 1)
    return jnp.where(first, rb, ra), jnp.where(first, ra, rb)


def kernel(
    nlon, nlat, inner,
    tracer, salinity, zonal, merid, surface, mask, bottom, tr_adj, sa_adj, zo_adj, me_adj, su_adj, st_adj,
    out_t, out_s, out_u, out_v, out_h,
    x, lm, bl, stv, c1, ce1, cw1, pw1, pe1, cl, pwl, pel, m1, mr, rn, rs, got_s, got_n,
    tot, tot_w, tot_e, two, slot1, gsum, slot2, sfx,
    um0, umw, vm0, we, wew, wn, z1, z1w, mm1, mm1e, wne, tmp3, sut, svt,
    acc, acx, ce2, cw2, pw2, pe2, m2, sa, sb, st, ou2, cd2, wt2, ff2, ga, gb, fg, tmpb, gg,
    in_sem, send_sem, recv_sem,
):
    lon, lat = lax.axis_index("lon"), lax.axis_index("lat")
    south_here, north_here = lat > 0, lat < nlat - 1
    outer = nlat // inner
    gi, go = lax.rem(lat, inner), lat // inner

    def at(dlon, dlat):
        return (lax.rem(lon + dlon + nlon, nlon), lax.rem(lat + dlat + nlat, nlat))

    def when(condition, action):
        if condition is None:
            action()
        else:
            pl.when(condition)(action)

    around = [at(*side) for side in SIDES]
    exists = [{0: None, 1: north_here, -1: south_here}[side[1]] for side in SIDES]
    from_it = [{0: None, 1: south_here, -1: north_here}[side[1]] for side in SIDES]

    def signal(sem, where, condition):
        when(condition, lambda: pl.semaphore_signal(sem, inc=1, device_id=where, device_id_type=MESH))

    barrier = pltpu.get_barrier_semaphore()
    for where, condition in zip(around, exists):
        signal(barrier, where, condition)
    mates = [(lon, go * inner + lax.rem(gi + d, inner)) for d in range(1, inner)]
    peers = [(lon, lax.rem(go + e, outer) * inner + gi) for e in range(1, outer)]
    for where in mates + peers:
        signal(barrier, where, None)

    loads = []
    for src, dst in (
        (st_adj, stv), (mask, lm), (bottom, bl),
        (tracer, x.at[CT, :, OWN]), (salinity, x.at[CS, :, OWN]), (zonal, x.at[WU, :, OWN]), (merid, x.at[WV, :, OWN]),
        (surface, sa.at[SF_H, MINE]), (su_adj, sa.at[SF_HADJ, MINE]),
        (tr_adj, x.at[AT, :, OWN]), (sa_adj, x.at[AS, :, OWN]), (zo_adj, x.at[WZ, :, OWN]), (me_adj, x.at[WM, :, OWN]),
    ):
        copy = pltpu.make_async_copy(src, dst, in_sem.at[len(loads)])
        copy.start()
        loads.append(copy)

    sent = []

    def send(src, dst, where, to=None, by=None):
        n = len(sent)
        copy = pltpu.make_async_remote_copy(
            src_ref=src, dst_ref=dst, send_sem=send_sem.at[n], recv_sem=recv_sem.at[n],
            device_id=where, device_id_type=MESH,
        )
        when(to, copy.start)
        sent.append((copy, to))
        return copy, by

    def arrive(copies):
        for copy, by in copies:
            when(by, copy.wait_recv)

    pad = jnp.zeros((8, LANES), F32)
    loads[0].wait()
    tile_sum = stv[0:8]
    for r in range(1, ROWS // 8):
        tile_sum = tile_sum + stv[8 * r : 8 * r + 8]
    tot[...] = tile_sum
    for copy in loads[1:9]:
        copy.wait()

    lane = lanes_of(ROWS)
    EARLY, LATE = (CT, CS, WU, WV, WET), (AT, AS, WZ, WM)

    def mask_fields(fields):
        def mask_level(k, _):
            if WET in fields:
                wet = jnp.where((lm[k] > 0) & (k < bl[...]), 1.0, 0.0).astype(F32)
            else:
                wet = x[WET, k, OWN]
            packs = {PACK[f][0]: c1[PACK[f][0]] for f in fields}
            for f in fields:
                n, s = PACK[f]
                value = wet if f == WET else x[f, k, OWN] * wet
                x[f, k, OWN] = value
                here = lax.shift_right_logical(lane, 2) == 8 * s + k
                packs[n] = jnp.where(here, roll(value, 32 * s + 4 * k + 2), packs[n])
            for n, value in packs.items():
                c1[n] = value
            return 0

        lax.fori_loop(0, LEVELS, mask_level, 0)

        def pack_rows(f, _):
            for k in range(LEVELS):
                rs[f, 2 * k : 2 * k + 2] = x[f, k, 16:18]
                rn[f, 2 * k : 2 * k + 2] = x[f, k, 62:64]
            return 0

        lax.fori_loop(fields[0], fields[-1] + 1, pack_rows, 0)

    c1[1] = jnp.zeros((ROWS, LANES), F32)
    mask_fields(EARLY)
    fine, coarse = (lane & 3) < 2, (lane & 31) < 16
    ce1[...] = jnp.where(fine, c1[0], roll(c1[1], 2))
    cw1[...] = jnp.where(fine, roll(c1[1], LANES - 2), c1[0])
    pl.semaphore_wait(barrier, 2 + len(mates) + len(peers) + jnp.where(south_here, 3, 0) + jnp.where(north_here, 3, 0))

    def send_all(table):
        return [send(src, dst, around[n], exists[n], from_it[n]) for n, src, dst in table]

    def rows_table(first, last):
        here = slice(first, last)
        return [(2, rn.at[here], got_s.at[here]), (3, rs.at[here], got_n.at[here])]

    def planes_table(first, last):
        here = slice(first, last)
        return [(2, sa.at[here, 56:72], sa.at[here, 8:24]), (3, sa.at[here, 24:40], sa.at[here, 72:88])]

    LOW, HIGH = slice(0, 16), slice(32, 48)
    phase1 = send_all(
        [
            (5, cw1.at[40:48], pe1.at[8:16]),
            (6, ce1.at[0:8], pw1.at[64:72]),
            (7, cw1.at[0:8], pe1.at[64:72]),
            (0, ce1, pw1.at[16:64]),
            (1, cw1, pe1.at[16:64]),
        ]
        + rows_table(0, 5)
    )
    level0 = [send(tot, tot_w, around[0]), send(tot, tot_e, around[1])]

    for copy in loads[9:]:
        copy.wait()
    mask_fields(LATE)
    sa[SF_WT, MINE] = x[WET, 0, OWN]
    pack = roll(sa[SF_H, MINE], 16)
    for s, f in ((1, SF_HADJ), (2, SF_WT)):
        here = lax.shift_right_logical(lane, 5) == s
        pack = jnp.where(here, roll(sa[f, MINE], 32 * s + 16), pack)
    cl[0] = c1[2]
    cl[1] = pack
    late1 = send_all(
        rows_table(5, 9)
        + [
            (0, cl, pwl.at[:, 16:64]),
            (1, cl, pel.at[:, 16:64]),
            (4, cl.at[:, HIGH], pwl.at[:, 0:16]),
            (5, cl.at[:, HIGH], pel.at[:, 0:16]),
            (6, cl.at[:, LOW], pwl.at[:, 64:80]),
            (7, cl.at[:, LOW], pel.at[:, 64:80]),
        ]
        + planes_table(0, 3)
    )

    sfx[0:48] = stv[...]
    for r in range(6):
        sfx[48 + 8 * r : 56 + 8 * r] = pad
    for step in (1, 2, 4, 8, 16, 32):
        moved = sfx[0:48] + sfx[step : step + 48]
        sfx[0:48] = moved
    for n in range(3):
        for p in range(2):
            st[n, p, 0:8] = pad
            st[n, p, 88:96] = pad
    for p in range(2):
        tmpb[p, 0:8] = pad
        tmpb[p, 88:96] = pad
    acc[...] = jnp.zeros_like(acc)
    acx[...] = jnp.zeros_like(acx)

    arrive(phase1)
    arrive(level0)
    two[0] = tot[...]
    two[1] = jnp.where(lanes_of(8) < LANES // 2, tot_e[...], tot_w[...])
    up1 = [send(two, slot1.at[d - 1], mates[d - 1]) for d in range(1, inner)]
    up1 += send_all([(3, two, slot1.at[inner - 1])])

    def unpack_rows(f, _):
        for k in range(LEVELS):
            x[f, k, 14:16] = jnp.where(south_here, got_s[f, 2 * k : 2 * k + 2], 0.0)
            x[f, k, 64:66] = jnp.where(north_here, got_n[f, 2 * k : 2 * k + 2], 0.0)
        return 0

    lax.fori_loop(0, 5, unpack_rows, 0)
    lane80 = lanes_of(80)
    rows80 = lax.broadcasted_iota(jnp.int32, (80, LANES), 0)
    inside = ((rows80 >= 16) | south_here) & ((rows80 < 64) | north_here)
    fine = (lane80 & 3) < 2
    coarse = (lane80 & 31) < 16

    rim_w, rim_e = pw1[...], pe1[...]
    m1[0] = jnp.where(inside, jnp.where(fine, rim_w, rim_e), 0.0)
    m1[1] = jnp.where(inside, jnp.where(fine, roll(rim_w, LANES - 2), roll(rim_e, 2)), 0.0)

    def strip(f, k, rows):
        n, s = PACK[f]
        return roll(m1[n, rows], 126 - 32 * s - 4 * k)

    def shifted(value, rim, offset):
        ids = lanes_of(value.shape[0])
        if offset > 0:
            return roll(jnp.where(ids < offset, rim, value), LANES - offset)
        return roll(jnp.where(ids >= LANES + offset, rim, value), -offset)

    row_ids = lax.broadcasted_iota(jnp.int32, (64, LANES), 0) + (lat * ROWS - 8)
    cor = -(1.0 + row_ids.astype(F32) / (ROWS * nlat))

    EXT = slice(8, 72)

    def forward_level(k, _):
        wet = x[WET, k, EXT]
        wet_e = shifted(wet, strip(WET, k, EXT), 1)
        tmp3[EXT] = wet_e
        wet_n = x[WET, k, 9:73]
        east, north = wet * wet_e, wet * wet_n
        we[k, EXT] = east
        wn[k, EXT] = north
        wu, wv = x[WU, k, EXT], x[WV, k, EXT]
        u0 = wu * wet_e
        v0 = wv * wet_n
        uw = shifted(wu, strip(WU, k, EXT), -1) * wet
        ve = shifted(wv, strip(WV, k, EXT), 1) * tmp3[9:73]
        um0[k, EXT] = u0
        umw[k, EXT] = uw
        vm0[k, EXT] = v0
        sut[EXT] = u0 + uw
        svt[EXT] = v0 + ve
        acc[6] = acc[6] + x[WZ, k, OWN] * wet_e[8:56]
        acc[7] = acc[7] + x[WM, k, OWN] * wet_n[8:56]
        acx[1] = acx[1] + east
        acx[3] = acx[3] + north

        t0 = SALT_COEF * x[CS, k, OWN] - HEAT_COEF * x[CT, k, OWN]
        tn = SALT_COEF * x[CS, k, 17:65] - HEAT_COEF * x[CT, k, 17:65]
        te = shifted(t0, SALT_COEF * strip(CS, k, OWN) - HEAT_COEF * strip(CT, k, OWN), 1)
        dpe = acc[4] + (te - t0)
        dpn = acc[5] + (tn - t0)
        acc[4] = dpe
        acc[5] = dpn
        own = slice(8, 56)
        drag = jnp.where(bl[...] - 1 == k, 1.0 - DRAG_COEF, 1.0)
        uo, vo = u0[own], v0[own]
        vu = (0.25 * CORIOLIS) * cor[own] * (svt[OWN] + svt[15:63])
        uv = (0.25 * CORIOLIS) * cor[own] * (sut[OWN] + sut[17:65])
        zn = uo * drag + east[own] * (vu - (PRESS_COEF / LEVELS) * dpe)
        mn = vo * drag - north[own] * (uv + (PRESS_COEF / LEVELS) * dpn)
        acc[0] = acc[0] + uo
        acc[1] = acc[1] + vo
        acc[2] = acc[2] + zn
        acc[3] = acc[3] + mn
        return 0

    tmp3[72:80] = pad
    lax.fori_loop(0, LEVELS, forward_level, 0)

    def over(num, count):
        return num / jnp.maximum(count, 1.0)

    own = slice(8, 56)
    cu, cv = acx[1, own], acx[3, own]
    surf = [
        acc[0] / LEVELS, acc[1] / LEVELS,
        (acc[2] - acc[0]) / (LEVELS * SUBCYCLES), (acc[3] - acc[1]) / (LEVELS * SUBCYCLES),
        cu, cv,
        LEVELS * over(acc[6], cu) + sfx[0:48],
        LEVELS * over(acc[7], cv),
    ]
    packs = []
    for n in range(2):
        pack = None
        for s in range(4):
            value = surf[4 * n + s]
            sa[SF_U + 4 * n + s, MINE] = value
            turned = roll(value, (32 * s + 16) % LANES)
            pack = turned if s == 0 else jnp.where(lax.shift_right_logical(lane, 5) == s, turned, pack)
        packs.append(pack)
    own_coarse = (lane & 31) < 16
    ce2[...] = jnp.where(own_coarse, packs[0], roll(packs[1], 16))
    cw2[...] = jnp.where(own_coarse, roll(packs[1], LANES - 16), packs[0])
    phase2 = send_all(
        [
            (4, ce2.at[HIGH], pw2.at[0:16]),
            (5, cw2.at[HIGH], pe2.at[0:16]),
            (6, ce2.at[LOW], pw2.at[64:80]),
            (7, cw2.at[LOW], pe2.at[64:80]),
            (0, ce2, pw2.at[16:64]),
            (1, cw2, pe2.at[16:64]),
        ]
        + planes_table(3, 11)
    )
    arrive(late1)
    lax.fori_loop(5, 9, unpack_rows, 0)
    m1[2] = jnp.where(inside, jnp.where(fine, pwl[0], pel[0]), 0.0)
    mr[...] = jnp.where(inside, jnp.where(coarse, pwl[1], pel[1]), 0.0)

    def advect_level(k, _):
        wet_rim = strip(WET, k, OWN)
        wet = x[WET, k, OWN]
        u_rim, wu = strip(WU, k, OWN), x[WU, k, OWN]
        u0, u_w = um0[k, OWN], umw[k, OWN]
        u_ww = shifted(wu, u_rim, -2) * shifted(wet, wet_rim, -1)
        u_e = shifted(wu, u_rim, 1) * shifted(wet, wet_rim, 2)
        we0, we_w = we[k, OWN], wet * shifted(wet, wet_rim, -1)
        v0, v_s, v_ss, v_n = vm0[k, OWN], vm0[k, 15:63], vm0[k, 14:62], vm0[k, 17:65]
        wn0, wn_s = wn[k, OWN], wn[k, 15:63]
        grad_u = jnp.zeros((ROWS, LANES), F32)
        grad_v = jnp.zeros((ROWS, LANES), F32)
        for c, a, out in ((CT, AT, out_t), (CS, AS, out_s)):
            a0, a_rim = x[a, k, OWN], strip(a, k, OWN)
            c0, c_rim = x[c, k, OWN], strip(c, k, OWN)
            a_e, a_ee = shifted(a0, a_rim, 1), shifted(a0, a_rim, 2)
            a_w, a_ww = shifted(a0, a_rim, -1), shifted(a0, a_rim, -2)
            d0, d_w, d_ww, d_e = a_e - a0, a0 - a_w, a_w - a_ww, a_ee - a_e
            c_e, c_ee, c_w = shifted(c0, c_rim, 1), shifted(c0, c_rim, 2), shifted(c0, c_rim, -1)
            grad_u = grad_u + d0 * ((ADVECT * 7.0 / 12.0) * (c0 + c_e) - (ADVECT / 12.0) * (c_w + c_ee))
            grad = a0 + (ADVECT * 7.0 / 12.0) * (u0 * d0 + u_w * d_w) - (ADVECT / 12.0) * (u_e * d_e + u_ww * d_ww)
            grad = grad + DIFFUSION * (we0 * d0 - we_w * d_w)
            a_n, a_nn, a_s, a_ss = x[a, k, 17:65], x[a, k, 18:66], x[a, k, 15:63], x[a, k, 14:62]
            d0, d_s, d_ss, d_n = a_n - a0, a0 - a_s, a_s - a_ss, a_nn - a_n
            c_n, c_nn, c_s = x[c, k, 17:65], x[c, k, 18:66], x[c, k, 15:63]
            grad_v = grad_v + d0 * ((ADVECT * 7.0 / 12.0) * (c0 + c_n) - (ADVECT / 12.0) * (c_s + c_nn))
            grad = grad + (ADVECT * 7.0 / 12.0) * (v0 * d0 + v_s * d_s) - (ADVECT / 12.0) * (v_n * d_n + v_ss * d_ss)
            grad = grad + DIFFUSION * (wn0 * d0 - wn_s * d_s)
            out[k] = grad
        out_u[k] = grad_u
        out_v[k] = grad_v
        wet_x = x[WET, k, EXT]
        rim_x = strip(WET, k, EXT)
        wet_ex = shifted(wet_x, rim_x, 1)
        tmp3[EXT] = wet_ex
        wet_en = tmp3[9:73]
        east_w = wet_x * shifted(wet_x, rim_x, -1)
        north_e = wet_ex * wet_en
        z_w = shifted(x[WZ, k, EXT], strip(WZ, k, EXT), -1) * wet_x
        m_e = shifted(x[WM, k, EXT], strip(WM, k, EXT), 1) * wet_en
        wew[k, EXT] = east_w
        wne[k, EXT] = north_e
        z1w[k, EXT] = z_w
        mm1e[k, EXT] = m_e
        zz = x[WZ, k, EXT] * wet_ex
        mz = x[WM, k, EXT] * x[WET, k, 9:73]
        z1[k, EXT] = zz
        mm1[k, EXT] = mz
        acx[0] = acx[0] + zz
        acx[2] = acx[2] + mz
        acx[4] = acx[4] + z_w
        acx[5] = acx[5] + east_w
        acx[6] = acx[6] + m_e
        acx[7] = acx[7] + north_e
        return 0

    lax.fori_loop(0, LEVELS // 2, advect_level, 0)
    arrive(up1)
    group = two[...]
    above = jnp.zeros((2, 8, LANES), F32)
    for d in range(1, inner):
        got = slot1[d - 1]
        group = group + got
        above = above + jnp.where(lax.rem(gi - d + inner, inner) > gi, got, 0.0)
    gsum[...] = group
    up2 = [send(gsum, slot2.at[e - 1], peers[e - 1]) for e in range(1, outer)]
    lax.fori_loop(LEVELS // 2, LEVELS, advect_level, 0)

    arrive(phase2)

    rim_lane = (lane80 < HALO) | (lane80 >= LANES - HALO)
    rim_w, rim_e = pw2[...], pe2[...]
    m2[0] = jnp.where(inside, jnp.where(coarse, rim_w, rim_e), 0.0)
    m2[1] = jnp.where(inside, jnp.where(coarse, roll(rim_w, LANES - 16), roll(rim_e, 16)), 0.0)
    for f in range(11):
        source, s = (mr[...], f) if f < 3 else (m2[(f - 3) // 4], (f - 3) % 4)
        sb[f] = jnp.where(rim_lane, roll(source, (LANES - 16 - 32 * s) % LANES), 0.0)

    def part(f, p):
        return jnp.where(inside, sa[f, BODY], 0.0) if p == 0 else sb[f]

    for p in range(2):
        st[0, p, BODY] = part(SF_H, p)
        st[1, p, BODY] = part(SF_U, p)
        st[2, p, BODY] = part(SF_V, p)
        wt2[p] = part(SF_WT, p)
        for d in range(2):
            count = part(SF_CU + d, p)
            opened = jnp.minimum(count, 1.0)
            ou2[d, p] = opened
            cd2[d, p] = (SLOPE_COEF / LEVELS) * count
            ff2[d, p] = opened * part(SF_FU + d, p)
            fg[d, p] = jnp.zeros((80, LANES), F32)

    BOTH = (0, 1)

    def sub_step(n, _):
        u = [st[1, p, BODY] for p in BOTH]
        v = [st[2, p, BODY] for p in BOTH]
        u_w = pair_west(*u)
        h = [
            wt2[p] * (st[0, p, BODY] - DIVERGENCE * ((u[p] - u_w[p]) + (v[p] - st[2, p, 7:87])))
            for p in BOTH
        ]
        for p in BOTH:
            st[0, p, BODY] = h[p]
        h_e = pair_east(*h)
        for p in BOTH:
            for d, old, far in ((0, u[p], h_e[p]), (1, v[p], st[0, p, 9:89])):
                slope = far - h[p]
                bend = jnp.tanh(0.5 * (h[p] + far))
                depth = cd2[d, p]
                level = depth * (1.0 + THICK_COEF * bend)
                tilt = depth * (0.5 * THICK_COEF) * (1.0 - bend * bend) * slope
                ga[n, d, p] = level - tilt
                gb[n, d, p] = level + tilt
                st[1 + d, p, BODY] = (1.0 - FRICTION) * ou2[d, p] * old + ff2[d, p] - level * slope
        return 0

    lax.fori_loop(0, SUBCYCLES, sub_step, 0)

    arrive(up2)
    for e in range(1, outer):
        got = slot2[e - 1]
        above = above + jnp.where(lax.rem(go - e + outer, outer) > go, got, 0.0)
    for p in BOTH:
        st[0, p, BODY] = part(SF_HADJ, p)
        mine = jnp.sum(two[p], axis=0, keepdims=True)
        north = jnp.sum(jnp.where(north_here, slot1[inner - 1, p], 0.0), axis=0, keepdims=True)
        beyond = jnp.sum(above[p], axis=0, keepdims=True)
        suffix = jnp.where(rows80 < 16, beyond + mine, jnp.where(rows80 < 64, beyond, beyond - north))
        st[1, p, BODY] = part(SF_SU, p) + suffix
        st[2, p, BODY] = part(SF_SV, p)

    def back_step(i, _):
        n = SUBCYCLES - 1 - i
        u = [ou2[0, p] * st[1, p, BODY] for p in BOTH]
        v = [ou2[1, p] * st[2, p, BODY] for p in BOTH]
        for p in BOTH:
            fg[0, p] = fg[0, p] + u[p]
            fg[1, p] = fg[1, p] + v[p]
            tmpb[p, BODY] = gb[n, 1, p] * v[p]
        b_w = pair_west(*[gb[n, 0, p] * u[p] for p in BOTH])
        h = [
            wt2[p] * (st[0, p, BODY] + (ga[n, 0, p] * u[p] - b_w[p]) + (ga[n, 1, p] * v[p] - tmpb[p, 7:87]))
            for p in BOTH
        ]
        for p in BOTH:
            st[0, p, BODY] = h[p]
        h_e = pair_east(*h)
        for p in BOTH:
            st[1, p, BODY] = (1.0 - FRICTION) * u[p] - DIVERGENCE * (h[p] - h_e[p])
            st[2, p, BODY] = (1.0 - FRICTION) * v[p] - DIVERGENCE * (h[p] - st[0, p, 9:89])
        return 0

    lax.fori_loop(0, SUBCYCLES, back_step, 0)

    out_h[...] = st[0, 0, MINE]
    window = slice(8, 72)
    force = 1.0 / (LEVELS * SUBCYCLES)
    fu, fv = fg[0, 0], fg[1, 0]
    fu_w = pair_west(fu, fg[0, 1])[0]
    fv_e = pair_east(fv, fg[1, 1])[0]
    gg[0] = force * fu[window] - over(acx[0], acx[1])
    gg[1] = force * fu_w[window] - over(acx[4], acx[5])
    gg[2] = force * fv[window] - over(acx[2], acx[3])
    gg[3] = force * fv_e[window] - over(acx[6], acx[7])
    acc[0] = (st[1, 0, MINE] - fu[16:64] / SUBCYCLES) / LEVELS
    acc[1] = (st[2, 0, MINE] - fv[16:64] / SUBCYCLES) / LEVELS

    turn = (0.25 * CORIOLIS) * cor

    def momentum_level(i, press):
        k = LEVELS - 1 - i
        z = z1[k, ZR] + we[k, ZR] * gg[0, 8:64]
        z_w = z1w[k, ZR] + wew[k, ZR] * gg[1, 8:64]
        m = mm1[k, MR] + wn[k, MR] * gg[2, 0:56]
        m_e = mm1e[k, MR] + wne[k, MR] * gg[3, 0:56]
        sut[ZR] = turn[8:64] * (z + z_w)
        svt[MR] = turn[0:56] * (m + m_e)
        tmp3[MR] = m
        z0, m0 = z[0:48], m[8:56]
        press = press + (PRESS_COEF / LEVELS) * ((z0 - z_w[0:48]) + (m0 - tmp3[15:63]))
        drag = jnp.where(bl[...] - 1 == k, 1.0 - DRAG_COEF, 1.0)
        wet = x[WET, k, OWN]
        out_t[k] = wet * (out_t[k] - HEAT_COEF * press)
        out_s[k] = wet * (out_s[k] + SALT_COEF * press)
        out_u[k] = we[k, OWN] * (out_u[k] + z0 * drag - (svt[OWN] + svt[15:63]) + acc[0])
        out_v[k] = wn[k, OWN] * (out_v[k] + m0 * drag + (sut[OWN] + sut[17:65]) + acc[1])
        return press

    lax.fori_loop(0, LEVELS, momentum_level, jnp.zeros((ROWS, LANES), F32))

    for copy, to in sent:
        when(to, copy.wait_send)


def store_kernel(*refs):
    sources, targets, sem = refs[:5], refs[5:10], refs[10]
    copies = [pltpu.make_async_copy(a, b, sem.at[n]) for n, (a, b) in enumerate(zip(sources, targets))]
    for copy in copies:
        copy.start()
    for copy in copies:
        copy.wait()


def solution(mesh):
    nlon, nlat = mesh.shape["lon"], mesh.shape["lat"]
    inner = next(n for n in (8, 4, 2, 1) if nlat % n == 0 and n * n <= 2 * nlat)
    outer = nlat // inner
    deep = P(None, "lat", "lon")
    flat = P("lat", "lon")

    def step(*args):
        vm = lambda *shape: pltpu.VMEM(shape, F32)
        cube = jax.ShapeDtypeStruct((LEVELS, ROWS, LANES), F32)
        plane = jax.ShapeDtypeStruct((ROWS, LANES), F32)
        level = vm(LEVELS, TALL, LANES)
        copies = 7 + 2 + 10 + inner + 8 + outer - 1
        scratch = dict(
            x=vm(9, LEVELS, TALL, LANES), lm=pltpu.VMEM((LEVELS, ROWS, LANES), jnp.int32),
            bl=pltpu.VMEM((ROWS, LANES), jnp.int32), stv=vm(ROWS, LANES),
            c1=vm(3, ROWS, LANES), ce1=vm(ROWS, LANES), cw1=vm(ROWS, LANES), pw1=vm(80, LANES), pe1=vm(80, LANES),
            cl=vm(2, ROWS, LANES), pwl=vm(2, 80, LANES), pel=vm(2, 80, LANES), m1=vm(3, 80, LANES), mr=vm(80, LANES),
            rn=vm(9, 16, LANES), rs=vm(9, 16, LANES), got_s=vm(9, 16, LANES), got_n=vm(9, 16, LANES),
            tot=vm(8, LANES), tot_w=vm(8, LANES), tot_e=vm(8, LANES), two=vm(2, 8, LANES),
            slot1=vm(inner, 2, 8, LANES), gsum=vm(2, 8, LANES), slot2=vm(max(outer - 1, 1), 2, 8, LANES), sfx=vm(96, LANES),
            um0=level, umw=level, vm0=level, we=level, wew=level, wn=level, z1=level, z1w=level,
            mm1=level, mm1e=level, wne=level, tmp3=vm(TALL, LANES), sut=vm(TALL, LANES), svt=vm(TALL, LANES),
            acc=vm(8, ROWS, LANES), acx=vm(8, 64, LANES), ce2=vm(ROWS, LANES), cw2=vm(ROWS, LANES), pw2=vm(80, LANES),
            pe2=vm(80, LANES), m2=vm(2, 80, LANES), sa=vm(11, WIDE, LANES), sb=vm(11, 80, LANES),
            st=vm(3, 2, WIDE, LANES), ou2=vm(2, 2, 80, LANES), cd2=vm(2, 2, 80, LANES), wt2=vm(2, 80, LANES),
            ff2=vm(2, 2, 80, LANES), ga=vm(SUBCYCLES, 2, 2, 80, LANES), gb=vm(SUBCYCLES, 2, 2, 80, LANES),
            fg=vm(2, 2, 80, LANES), tmpb=vm(2, WIDE, LANES), gg=vm(4, 64, LANES),
            in_sem=pltpu.SemaphoreType.DMA((13,)), send_sem=pltpu.SemaphoreType.DMA((copies,)),
            recv_sem=pltpu.SemaphoreType.DMA((copies,)),
        )

        def body(*refs):
            kernel(nlon, nlat, inner, *refs)

        parts = pl.pallas_call(
            body,
            out_shape=[cube, cube, cube, cube, plane],
            in_specs=[pl.BlockSpec(memory_space=pltpu.HBM)] * 13,
            out_specs=[pl.BlockSpec(memory_space=pltpu.VMEM)] * 5,
            scratch_shapes=list(scratch.values()),
            compiler_params=pltpu.CompilerParams(
                collective_id=0, has_side_effects=True, vmem_limit_bytes=40 * 1024 * 1024
            ),
        )(*(pltpu.with_memory_space_constraint(a, pltpu.HBM) for a in args))
        return pl.pallas_call(
            store_kernel,
            out_shape=[cube, cube, cube, cube, plane],
            in_specs=[pl.BlockSpec(memory_space=pltpu.VMEM)] * 5,
            out_specs=[pl.BlockSpec(memory_space=pltpu.HBM)] * 5,
            scratch_shapes=[pltpu.SemaphoreType.DMA((5,))],
            compiler_params=pltpu.CompilerParams(vmem_limit_bytes=4 * 1024 * 1024),
        )(*parts)

    specs = (deep, deep, deep, deep, flat, deep, flat, deep, deep, deep, deep, flat, flat)
    return jax.shard_map(
        step, mesh=mesh, in_specs=specs, out_specs=(deep, deep, deep, deep, flat), check_vma=False
    )
```

```python
import jax
import jax.numpy as jnp
from jax import lax
from jax.experimental import pallas as pl
from jax.experimental.pallas import tpu as pltpu
from jax.sharding import PartitionSpec as P

MESH = pl.DeviceIdType.MESH
F32 = jnp.float32
SUBCYCLES = 8
LEVELS = 8
ROWS = 48
LANES = 128
HALO = 16

ADVECT = 0.25
DIFFUSION = 0.1
HEAT_COEF = 0.5
SALT_COEF = 0.4
PRESS_COEF = 0.3
CORIOLIS = 0.3
DRAG_COEF = 0.5
DIVERGENCE = 0.5
SLOPE_COEF = 0.5
FRICTION = 0.05
THICK_COEF = 0.3

CT, CS, WU, WV, WET, AT, AS, WZ, WM = range(9)
PACK = ((0, 0), (0, 1), (0, 2), (0, 3), (1, 0), (2, 0), (2, 1), (2, 2), (2, 3))
OWN = slice(16, 64)
ZR = slice(16, 72)
MR = slice(8, 64)
TALL = 80
BODY = slice(8, 88)
MINE = slice(24, 72)
WIDE = 96
SF_H, SF_HADJ, SF_WT, SF_U, SF_V, SF_FU, SF_FV, SF_CU, SF_CV, SF_SU, SF_SV = range(11)
SIDES = ((1, 0), (-1, 0), (0, 1), (0, -1), (1, 1), (-1, 1), (1, -1), (-1, -1))


def roll(x, shift):
    return pltpu.roll(x, shift, axis=x.ndim - 1)


def lanes_of(rows):
    return lax.broadcasted_iota(jnp.int32, (rows, LANES), 1)


def pair_east(a, b):
    last = lanes_of(a.shape[0]) == LANES - 1
    ra, rb = roll(a, LANES - 1), roll(b, LANES - 1)
    return jnp.where(last, rb, ra), jnp.where(last, ra, rb)


def pair_west(a, b):
    first = lanes_of(a.shape[0]) == 0
    ra, rb = roll(a, 1), roll(b, 1)
    return jnp.where(first, rb, ra), jnp.where(first, ra, rb)


def kernel(
    nlon, nlat, inner,
    tracer, salinity, zonal, merid, surface, mask, bottom, tr_adj, sa_adj, zo_adj, me_adj, su_adj, st_adj,
    out_t, out_s, out_u, out_v, out_h,
    x, lm, bl, stv, c1, ce1, cw1, pw1, pe1, cl, pwl, pel, m1, mr, rn, rs, got_s, got_n,
    tot, inn, slot1, gsum, slot2, inn_w, inn_e, sfx,
    um0, umw, vm0, we, wew, wn, z1, z1w, mm1, mm1e, wne, tmp3, sut, svt,
    acc, acx, ce2, cw2, pw2, pe2, m2, sa, sb, st, ou2, cd2, wt2, wte, ff2, ga, gb, fg, tmpb, gg,
    in_sem, send_sem, recv_sem, ready,
):
    lon, lat = lax.axis_index("lon"), lax.axis_index("lat")
    south_here, north_here = lat > 0, lat < nlat - 1
    outer = nlat // inner
    gi, go = lax.rem(lat, inner), lat // inner

    def at(dlon, dlat):
        return (lax.rem(lon + dlon + nlon, nlon), lax.rem(lat + dlat + nlat, nlat))

    def when(condition, action):
        if condition is None:
            action()
        else:
            pl.when(condition)(action)

    around = [at(*side) for side in SIDES]
    exists = [{0: None, 1: north_here, -1: south_here}[side[1]] for side in SIDES]
    from_it = [{0: None, 1: south_here, -1: north_here}[side[1]] for side in SIDES]

    def signal(sem, where, condition):
        when(condition, lambda: pl.semaphore_signal(sem, inc=1, device_id=where, device_id_type=MESH))

    barrier = pltpu.get_barrier_semaphore()
    for where, condition in zip(around, exists):
        signal(barrier, where, condition)
    chip, even = gi // 2, lax.rem(go, 2) == 0
    mates = []
    for d in range(1, inner):
        there = lax.rem(gi + d, inner)
        greets = jnp.logical_not(even) | (there // 2 >= chip)
        greeted = jnp.logical_not(even) | (there // 2 <= chip)
        mates.append(((lon, go * inner + there), greets, greeted))
    peers = []
    for e in range(1, outer):
        there = lax.rem(go + e, outer)
        same = lax.rem(there, 2) == lax.rem(go, 2)
        for c in (0, 1, -1):
            where = (lax.rem(lon + c + nlon, nlon), there * inner + gi)
            peers.append((where, same | even, same | jnp.logical_not(even)))
    greeted_by = 2 + jnp.where(south_here, 3, 0) + jnp.where(north_here, 3, 0)
    answers = [0, 0]
    for n, group in enumerate((mates, peers)):
        for where, greets, greeted in group:
            signal(barrier, where, greets)
            greeted_by = greeted_by + jnp.where(greeted, 1, 0)
            answers[n] = answers[n] + jnp.where(greeted, 0, 1)

    def answer():
        for n, group in enumerate((mates, peers)):
            for where, greets, _ in group:
                signal(ready.at[n], where, jnp.logical_not(greets))

    def wait_answers(n):
        when(answers[n] > 0, lambda: pl.semaphore_wait(ready.at[n], answers[n]))

    loads = []
    for src, dst in (
        (st_adj, stv), (mask, lm), (bottom, bl),
        (tracer, x.at[CT, :, OWN]), (salinity, x.at[CS, :, OWN]), (zonal, x.at[WU, :, OWN]), (merid, x.at[WV, :, OWN]),
        (surface, sa.at[SF_H, MINE]), (su_adj, sa.at[SF_HADJ, MINE]),
        (tr_adj, x.at[AT, :, OWN]), (sa_adj, x.at[AS, :, OWN]), (zo_adj, x.at[WZ, :, OWN]), (me_adj, x.at[WM, :, OWN]),
    ):
        copy = pltpu.make_async_copy(src, dst, in_sem.at[len(loads)])
        copy.start()
        loads.append(copy)

    sent = []

    def send(src, dst, where, to=None, by=None):
        n = len(sent)
        copy = pltpu.make_async_remote_copy(
            src_ref=src, dst_ref=dst, send_sem=send_sem.at[n], recv_sem=recv_sem.at[n],
            device_id=where, device_id_type=MESH,
        )
        if to is False:
            to = None
        else:
            when(to, copy.start)
        sent.append((copy, to))
        return copy, by

    def arrive(copies):
        for copy, by in copies:
            when(by, copy.wait_recv)

    pad = jnp.zeros((8, LANES), F32)
    loads[0].wait()
    tile_sum = stv[0:8]
    for r in range(1, ROWS // 8):
        tile_sum = tile_sum + stv[8 * r : 8 * r + 8]
    tot[...] = tile_sum
    for copy in loads[1:9]:
        copy.wait()

    lane = lanes_of(ROWS)
    EARLY, LATE = (CT, CS, WU, WV, WET), (AT, AS, WZ, WM)

    def mask_fields(fields):
        def mask_level(k, _):
            if WET in fields:
                wet = jnp.where((lm[k] > 0) & (k < bl[...]), 1.0, 0.0).astype(F32)
            else:
                wet = x[WET, k, OWN]
            packs = {PACK[f][0]: c1[PACK[f][0]] for f in fields}
            for f in fields:
                n, s = PACK[f]
                value = wet if f == WET else x[f, k, OWN] * wet
                x[f, k, OWN] = value
                here = lax.shift_right_logical(lane, 2) == 8 * s + k
                packs[n] = jnp.where(here, roll(value, 32 * s + 4 * k + 2), packs[n])
            for n, value in packs.items():
                c1[n] = value
            return 0

        lax.fori_loop(0, LEVELS, mask_level, 0)

        def pack_rows(f, _):
            for k in range(LEVELS):
                rs[f, 2 * k : 2 * k + 2] = x[f, k, 16:18]
                rn[f, 2 * k : 2 * k + 2] = x[f, k, 62:64]
            return 0

        lax.fori_loop(fields[0], fields[-1] + 1, pack_rows, 0)

    c1[1] = jnp.zeros((ROWS, LANES), F32)
    mask_fields(EARLY)
    fine, coarse = (lane & 3) < 2, (lane & 31) < 16
    ce1[...] = jnp.where(fine, c1[0], roll(c1[1], 2))
    cw1[...] = jnp.where(fine, roll(c1[1], LANES - 2), c1[0])
    pl.semaphore_wait(barrier, greeted_by)

    def send_all(table):
        return [send(src, dst, around[n], exists[n], from_it[n]) for n, src, dst in table]

    def rows_table(first, last):
        here = slice(first, last)
        return [(2, rn.at[here], got_s.at[here]), (3, rs.at[here], got_n.at[here])]

    def planes_table(first, last):
        here = slice(first, last)
        return [(2, sa.at[here, 56:72], sa.at[here, 8:24]), (3, sa.at[here, 24:40], sa.at[here, 72:88])]

    LOW, HIGH = slice(0, 16), slice(32, 48)
    phase1 = send_all(
        [
            (5, cw1.at[40:48], pe1.at[8:16]),
            (6, ce1.at[0:8], pw1.at[64:72]),
            (7, cw1.at[0:8], pe1.at[64:72]),
            (0, ce1, pw1.at[16:64]),
            (1, cw1, pe1.at[16:64]),
        ]
        + rows_table(0, 5)
    )
    answer()

    for copy in loads[9:]:
        copy.wait()
    mask_fields(LATE)
    sa[SF_WT, MINE] = x[WET, 0, OWN]
    pack = roll(sa[SF_H, MINE], 16)
    for s, f in ((1, SF_HADJ), (2, SF_WT)):
        here = lax.shift_right_logical(lane, 5) == s
        pack = jnp.where(here, roll(sa[f, MINE], 32 * s + 16), pack)
    cl[0] = c1[2]
    cl[1] = pack
    late1 = send_all(
        rows_table(5, 9)
        + [
            (0, cl, pwl.at[:, 16:64]),
            (1, cl, pel.at[:, 16:64]),
            (4, cl.at[:, HIGH], pwl.at[:, 0:16]),
            (5, cl.at[:, HIGH], pel.at[:, 0:16]),
            (6, cl.at[:, LOW], pwl.at[:, 64:80]),
            (7, cl.at[:, LOW], pel.at[:, 64:80]),
        ]
        + planes_table(0, 3)
    )

    wait_answers(0)
    up1 = [send(tot, slot1.at[n], mate[0]) for n, mate in enumerate(mates)]

    sfx[0:48] = stv[...]
    for r in range(6):
        sfx[48 + 8 * r : 56 + 8 * r] = pad
    for step in (1, 2, 4, 8, 16, 32):
        moved = sfx[0:48] + sfx[step : step + 48]
        sfx[0:48] = moved
    for n in range(3):
        for p in range(2):
            st[n, p, 0:8] = pad
            st[n, p, 88:96] = pad
    for p in range(2):
        tmpb[p, 8:16] = pad
    acc[...] = jnp.zeros_like(acc)
    acx[...] = jnp.zeros_like(acx)

    arrive(phase1)
    def unpack_rows(f, _):
        for k in range(LEVELS):
            x[f, k, 14:16] = jnp.where(south_here, got_s[f, 2 * k : 2 * k + 2], 0.0)
            x[f, k, 64:66] = jnp.where(north_here, got_n[f, 2 * k : 2 * k + 2], 0.0)
        return 0

    lax.fori_loop(0, 5, unpack_rows, 0)
    lane80 = lanes_of(80)
    rows80 = lax.broadcasted_iota(jnp.int32, (80, LANES), 0)
    inside = ((rows80 >= 16) | south_here) & ((rows80 < 64) | north_here)
    fine = (lane80 & 3) < 2
    coarse = (lane80 & 31) < 16

    rim_w, rim_e = pw1[...], pe1[...]
    m1[0] = jnp.where(inside, jnp.where(fine, rim_w, rim_e), 0.0)
    m1[1] = jnp.where(inside, jnp.where(fine, roll(rim_w, LANES - 2), roll(rim_e, 2)), 0.0)

    def strip(f, k, rows):
        n, s = PACK[f]
        return roll(m1[n, rows], 126 - 32 * s - 4 * k)

    def shifted(value, rim, offset):
        ids = lanes_of(value.shape[0])
        if offset > 0:
            return roll(jnp.where(ids < offset, rim, value), LANES - offset)
        return roll(jnp.where(ids >= LANES + offset, rim, value), -offset)

    row_ids = lax.broadcasted_iota(jnp.int32, (64, LANES), 0) + (lat * ROWS - 8)
    cor = -(1.0 + row_ids.astype(F32) / (ROWS * nlat))

    up2 = [send(inn, inn_w, around[0], False), send(inn, inn_e, around[1], False)]
    up2 += [send(gsum, slot2.at[n], where, False) for n, (where, _, _) in enumerate(peers)]

    def group_sums():
        arrive(up1)
        group = tot[...]
        above = jnp.zeros((8, LANES), F32)
        for d in range(1, inner):
            got = slot1[d - 1]
            group = group + got
            above = above + jnp.where(lax.rem(gi - d + inner, inner) > gi, got, 0.0)
        gsum[...] = group
        inn[0] = above
        inn[1] = tot[...]
        wait_answers(1)
        for copy, _ in up2:
            copy.start()

    pl.when(jnp.logical_not(even))(group_sums)
    EXT = slice(8, 72)

    def forward_level(k, _):
        wet = x[WET, k, EXT]
        wet_e = shifted(wet, strip(WET, k, EXT), 1)
        tmp3[EXT] = wet_e
        wet_n = x[WET, k, 9:73]
        east, north = wet * wet_e, wet * wet_n
        we[k, EXT] = east
        wn[k, EXT] = north
        wu, wv = x[WU, k, EXT], x[WV, k, EXT]
        u0 = wu * wet_e
        v0 = wv * wet_n
        uw = shifted(wu, strip(WU, k, EXT), -1) * wet
        ve = shifted(wv, strip(WV, k, EXT), 1) * tmp3[9:73]
        um0[k, EXT] = u0
        umw[k, EXT] = uw
        vm0[k, EXT] = v0
        sut[EXT] = u0 + uw
        svt[EXT] = v0 + ve
        acc[6] = acc[6] + x[WZ, k, OWN] * wet_e[8:56]
        acc[7] = acc[7] + x[WM, k, OWN] * wet_n[8:56]
        acx[1] = acx[1] + east
        acx[3] = acx[3] + north

        t0 = SALT_COEF * x[CS, k, OWN] - HEAT_COEF * x[CT, k, OWN]
        tn = SALT_COEF * x[CS, k, 17:65] - HEAT_COEF * x[CT, k, 17:65]
        te = shifted(t0, SALT_COEF * strip(CS, k, OWN) - HEAT_COEF * strip(CT, k, OWN), 1)
        dpe = acc[4] + (te - t0)
        dpn = acc[5] + (tn - t0)
        acc[4] = dpe
        acc[5] = dpn
        own = slice(8, 56)
        drag = jnp.where(bl[...] - 1 == k, 1.0 - DRAG_COEF, 1.0)
        uo, vo = u0[own], v0[own]
        vu = (0.25 * CORIOLIS) * cor[own] * (svt[OWN] + svt[15:63])
        uv = (0.25 * CORIOLIS) * cor[own] * (sut[OWN] + sut[17:65])
        zn = uo * drag + east[own] * (vu - (PRESS_COEF / LEVELS) * dpe)
        mn = vo * drag - north[own] * (uv + (PRESS_COEF / LEVELS) * dpn)
        acc[0] = acc[0] + uo
        acc[1] = acc[1] + vo
        acc[2] = acc[2] + zn
        acc[3] = acc[3] + mn
        return 0

    tmp3[72:80] = pad
    lax.fori_loop(0, LEVELS, forward_level, 0, unroll=2)

    def over(num, count):
        return num / jnp.maximum(count, 1.0)

    own = slice(8, 56)
    cu, cv = acx[1, own], acx[3, own]
    near = sfx[0:48] - jnp.where(row_ids[0:48] - (lat * ROWS - 8) < ROWS // 2, sfx[0:1], 0.0)
    surf = [
        acc[0] / LEVELS, acc[1] / LEVELS,
        (acc[2] - acc[0]) / (LEVELS * SUBCYCLES), (acc[3] - acc[1]) / (LEVELS * SUBCYCLES),
        cu, cv,
        LEVELS * over(acc[6], cu) + near,
        LEVELS * over(acc[7], cv),
    ]
    packs = []
    for n in range(2):
        pack = None
        for s in range(4):
            value = surf[4 * n + s]
            sa[SF_U + 4 * n + s, MINE] = value
            turned = roll(value, (32 * s + 16) % LANES)
            pack = turned if s == 0 else jnp.where(lax.shift_right_logical(lane, 5) == s, turned, pack)
        packs.append(pack)
    own_coarse = (lane & 31) < 16
    ce2[...] = jnp.where(own_coarse, packs[0], roll(packs[1], 16))
    cw2[...] = jnp.where(own_coarse, roll(packs[1], LANES - 16), packs[0])
    phase2 = send_all(
        [
            (4, ce2.at[HIGH], pw2.at[0:16]),
            (5, cw2.at[HIGH], pe2.at[0:16]),
            (6, ce2.at[LOW], pw2.at[64:80]),
            (7, cw2.at[LOW], pe2.at[64:80]),
            (0, ce2, pw2.at[16:64]),
            (1, cw2, pe2.at[16:64]),
        ]
        + planes_table(3, 11)
    )
    pl.when(even)(group_sums)
    arrive(late1)
    lax.fori_loop(5, 9, unpack_rows, 0)
    m1[2] = jnp.where(inside, jnp.where(fine, pwl[0], pel[0]), 0.0)
    mr[...] = jnp.where(inside, jnp.where(coarse, pwl[1], pel[1]), 0.0)

    def advect_level(k, _):
        wet_rim = strip(WET, k, OWN)
        wet = x[WET, k, OWN]
        u_rim, wu = strip(WU, k, OWN), x[WU, k, OWN]
        u0, u_w = um0[k, OWN], umw[k, OWN]
        u_ww = shifted(wu, u_rim, -2) * shifted(wet, wet_rim, -1)
        u_e = shifted(wu, u_rim, 1) * shifted(wet, wet_rim, 2)
        we0, we_w = we[k, OWN], wet * shifted(wet, wet_rim, -1)
        v0, v_s, v_ss, v_n = vm0[k, OWN], vm0[k, 15:63], vm0[k, 14:62], vm0[k, 17:65]
        wn0, wn_s = wn[k, OWN], wn[k, 15:63]
        grad_u = jnp.zeros((ROWS, LANES), F32)
        grad_v = jnp.zeros((ROWS, LANES), F32)
        for c, a, out in ((CT, AT, out_t), (CS, AS, out_s)):
            a0, a_rim = x[a, k, OWN], strip(a, k, OWN)
            c0, c_rim = x[c, k, OWN], strip(c, k, OWN)
            a_e, a_ee = shifted(a0, a_rim, 1), shifted(a0, a_rim, 2)
            a_w, a_ww = shifted(a0, a_rim, -1), shifted(a0, a_rim, -2)
            d0, d_w, d_ww, d_e = a_e - a0, a0 - a_w, a_w - a_ww, a_ee - a_e
            c_e, c_ee, c_w = shifted(c0, c_rim, 1), shifted(c0, c_rim, 2), shifted(c0, c_rim, -1)
            grad_u = grad_u + d0 * ((ADVECT * 7.0 / 12.0) * (c0 + c_e) - (ADVECT / 12.0) * (c_w + c_ee))
            grad = a0 + (ADVECT * 7.0 / 12.0) * (u0 * d0 + u_w * d_w) - (ADVECT / 12.0) * (u_e * d_e + u_ww * d_ww)
            grad = grad + DIFFUSION * (we0 * d0 - we_w * d_w)
            a_n, a_nn, a_s, a_ss = x[a, k, 17:65], x[a, k, 18:66], x[a, k, 15:63], x[a, k, 14:62]
            d0, d_s, d_ss, d_n = a_n - a0, a0 - a_s, a_s - a_ss, a_nn - a_n
            c_n, c_nn, c_s = x[c, k, 17:65], x[c, k, 18:66], x[c, k, 15:63]
            grad_v = grad_v + d0 * ((ADVECT * 7.0 / 12.0) * (c0 + c_n) - (ADVECT / 12.0) * (c_s + c_nn))
            grad = grad + (ADVECT * 7.0 / 12.0) * (v0 * d0 + v_s * d_s) - (ADVECT / 12.0) * (v_n * d_n + v_ss * d_ss)
            grad = grad + DIFFUSION * (wn0 * d0 - wn_s * d_s)
            out[k] = grad
        out_u[k] = grad_u
        out_v[k] = grad_v
        wet_x = x[WET, k, EXT]
        rim_x = strip(WET, k, EXT)
        wet_ex = shifted(wet_x, rim_x, 1)
        tmp3[EXT] = wet_ex
        wet_en = tmp3[9:73]
        east_w = wet_x * shifted(wet_x, rim_x, -1)
        north_e = wet_ex * wet_en
        z_w = shifted(x[WZ, k, EXT], strip(WZ, k, EXT), -1) * wet_x
        m_e = shifted(x[WM, k, EXT], strip(WM, k, EXT), 1) * wet_en
        wew[k, EXT] = east_w
        wne[k, EXT] = north_e
        z1w[k, EXT] = z_w
        mm1e[k, EXT] = m_e
        zz = x[WZ, k, EXT] * wet_ex
        mz = x[WM, k, EXT] * x[WET, k, 9:73]
        z1[k, EXT] = zz
        mm1[k, EXT] = mz
        acx[0] = acx[0] + zz
        acx[2] = acx[2] + mz
        acx[4] = acx[4] + z_w
        acx[5] = acx[5] + east_w
        acx[6] = acx[6] + m_e
        acx[7] = acx[7] + north_e
        return 0

    lax.fori_loop(0, LEVELS, advect_level, 0)

    arrive(phase2)

    rim_lane = (lane80 < HALO) | (lane80 >= LANES - HALO)
    rim_w, rim_e = pw2[...], pe2[...]
    m2[0] = jnp.where(inside, jnp.where(coarse, rim_w, rim_e), 0.0)
    m2[1] = jnp.where(inside, jnp.where(coarse, roll(rim_w, LANES - 16), roll(rim_e, 16)), 0.0)
    for f in range(11):
        source, s = (mr[...], f) if f < 3 else (m2[(f - 3) // 4], (f - 3) % 4)
        sb[f] = jnp.where(rim_lane, roll(source, (LANES - 16 - 32 * s) % LANES), 0.0)

    def part(f, p):
        return jnp.where(inside, sa[f, BODY], 0.0) if p == 0 else sb[f]

    for p in range(2):
        st[0, p, BODY] = part(SF_H, p)
        st[1, p, BODY] = part(SF_U, p)
        st[2, p, BODY] = part(SF_V, p)
        wt2[p] = part(SF_WT, p)
        for d in range(2):
            count = part(SF_CU + d, p)
            opened = jnp.minimum(count, 1.0)
            ou2[d, p] = opened
            cd2[d, p] = (SLOPE_COEF / LEVELS) * count
            ff2[d, p] = opened * part(SF_FU + d, p)
            fg[d, p] = jnp.zeros((80, LANES), F32)

    BOTH = (0, 1)
    wte[0], wte[1] = pair_east(wt2[0], wt2[1])

    def sub_step(n, lo, hi):
        mid, down, up = slice(lo + 8, hi + 8), slice(lo + 7, hi + 7), slice(lo + 9, hi + 9)
        rows = slice(lo, hi)
        u = [st[1, p, mid] for p in BOTH]
        v = [st[2, p, mid] for p in BOTH]
        rest = [st[0, p, mid] - DIVERGENCE * (v[p] - st[2, p, down]) - DIVERGENCE * u[p] for p in BOTH]
        u_w, rest_e = pair_west(*u), pair_east(*rest)
        h = [wt2[p, rows] * (rest[p] + DIVERGENCE * u_w[p]) for p in BOTH]
        h_e = [wte[p, rows] * (rest_e[p] + DIVERGENCE * u[p]) for p in BOTH]
        for p in BOTH:
            st[0, p, mid] = h[p]
        for p in BOTH:
            for d, old, far in ((0, u[p], h_e[p]), (1, v[p], st[0, p, up])):
                slope = far - h[p]
                bend = jnp.tanh(0.5 * (h[p] + far))
                depth = cd2[d, p, rows]
                level = depth * (1.0 + THICK_COEF * bend)
                tilt = depth * (0.5 * THICK_COEF) * (1.0 - bend * bend) * slope
                ga[n, d, p, rows] = level - tilt
                gb[n, d, p, rows] = level + tilt
                st[1 + d, p, mid] = (1.0 - FRICTION) * ou2[d, p, rows] * old + ff2[d, p, rows] - level * slope
        return 0

    lax.fori_loop(0, 3, lambda n, _: sub_step(n, 0, 80), 0, unroll=3)
    lax.fori_loop(3, SUBCYCLES, lambda n, _: sub_step(n, 4, 76), 0, unroll=5)

    arrive(up2)
    sums = []
    for c, source in enumerate((inn, inn_w, inn_e)):
        beyond = source[0]
        for e in range(1, outer):
            beyond = beyond + jnp.where(lax.rem(go - e + outer, outer) > go, slot2[3 * (e - 1) + c], 0.0)
        beyond = jnp.sum(beyond, axis=0, keepdims=True)
        sums.append((beyond, beyond + jnp.sum(source[1], axis=0, keepdims=True)))
    east_half = lanes_of(1) < LANES // 2
    sums = (sums[0], tuple(jnp.where(east_half, e, w) for w, e in zip(sums[1], sums[2])))
    for p in BOTH:
        st[0, p, BODY] = part(SF_HADJ, p)
        suffix = jnp.where(rows80 < HALO + ROWS // 2, sums[p][1], sums[p][0])
        st[1, p, BODY] = part(SF_SU, p) + suffix
        st[2, p, BODY] = part(SF_SV, p)

    mid, down, up, rows = slice(16, 80), slice(15, 79), slice(17, 81), slice(8, 72)

    def back_step(i, _):
        n = SUBCYCLES - 1 - i
        u = [ou2[0, p, rows] * st[1, p, mid] for p in BOTH]
        v = [ou2[1, p, rows] * st[2, p, mid] for p in BOTH]
        for p in BOTH:
            fg[0, p, rows] = fg[0, p, rows] + u[p]
            fg[1, p, rows] = fg[1, p, rows] + v[p]
            tmpb[p, mid] = gb[n, 1, p, rows] * v[p]
        b_u = [gb[n, 0, p, rows] * u[p] for p in BOTH]
        rest = [
            st[0, p, mid] + ga[n, 0, p, rows] * u[p] + (ga[n, 1, p, rows] * v[p] - tmpb[p, down]) for p in BOTH
        ]
        b_w, rest_e = pair_west(*b_u), pair_east(*rest)
        h = [wt2[p, rows] * (rest[p] - b_w[p]) for p in BOTH]
        h_e = [wte[p, rows] * (rest_e[p] - b_u[p]) for p in BOTH]
        for p in BOTH:
            st[0, p, mid] = h[p]
        for p in BOTH:
            st[1, p, mid] = (1.0 - FRICTION) * u[p] - DIVERGENCE * (h[p] - h_e[p])
            st[2, p, mid] = (1.0 - FRICTION) * v[p] - DIVERGENCE * (h[p] - st[0, p, up])
        return 0

    lax.fori_loop(0, SUBCYCLES, back_step, 0, unroll=8)

    out_h[...] = st[0, 0, MINE]
    window = slice(8, 72)
    force = 1.0 / (LEVELS * SUBCYCLES)
    fu, fv = fg[0, 0], fg[1, 0]
    fu_w = pair_west(fu, fg[0, 1])[0]
    fv_e = pair_east(fv, fg[1, 1])[0]
    gg[0] = force * fu[window] - over(acx[0], acx[1])
    gg[1] = force * fu_w[window] - over(acx[4], acx[5])
    gg[2] = force * fv[window] - over(acx[2], acx[3])
    gg[3] = force * fv_e[window] - over(acx[6], acx[7])
    acc[0] = (st[1, 0, MINE] - fu[16:64] / SUBCYCLES) / LEVELS
    acc[1] = (st[2, 0, MINE] - fv[16:64] / SUBCYCLES) / LEVELS

    turn = (0.25 * CORIOLIS) * cor

    def momentum_level(i, press):
        k = LEVELS - 1 - i
        z = z1[k, ZR] + we[k, ZR] * gg[0, 8:64]
        z_w = z1w[k, ZR] + wew[k, ZR] * gg[1, 8:64]
        m = mm1[k, MR] + wn[k, MR] * gg[2, 0:56]
        m_e = mm1e[k, MR] + wne[k, MR] * gg[3, 0:56]
        sut[ZR] = turn[8:64] * (z + z_w)
        svt[MR] = turn[0:56] * (m + m_e)
        tmp3[MR] = m
        z0, m0 = z[0:48], m[8:56]
        press = press + (PRESS_COEF / LEVELS) * ((z0 - z_w[0:48]) + (m0 - tmp3[15:63]))
        drag = jnp.where(bl[...] - 1 == k, 1.0 - DRAG_COEF, 1.0)
        wet = x[WET, k, OWN]
        out_t[k] = wet * (out_t[k] - HEAT_COEF * press)
        out_s[k] = wet * (out_s[k] + SALT_COEF * press)
        out_u[k] = we[k, OWN] * (out_u[k] + z0 * drag - (svt[OWN] + svt[15:63]) + acc[0])
        out_v[k] = wn[k, OWN] * (out_v[k] + m0 * drag + (sut[OWN] + sut[17:65]) + acc[1])
        return press

    lax.fori_loop(0, LEVELS, momentum_level, jnp.zeros((ROWS, LANES), F32))

    for copy, to in sent:
        when(to, copy.wait_send)


def store_kernel(*refs):
    sources, targets, sem = refs[:5], refs[5:10], refs[10]
    copies = [pltpu.make_async_copy(a, b, sem.at[n]) for n, (a, b) in enumerate(zip(sources, targets))]
    for copy in copies:
        copy.start()
    for copy in copies:
        copy.wait()


def solution(mesh):
    nlon, nlat = mesh.shape["lon"], mesh.shape["lat"]
    inner = next(n for n in (8, 4, 2, 1) if nlat % n == 0 and n * n <= 2 * nlat)
    outer = nlat // inner
    deep = P(None, "lat", "lon")
    flat = P("lat", "lon")

    def step(*args):
        vm = lambda *shape: pltpu.VMEM(shape, F32)
        cube = jax.ShapeDtypeStruct((LEVELS, ROWS, LANES), F32)
        plane = jax.ShapeDtypeStruct((ROWS, LANES), F32)
        level = vm(LEVELS, TALL, LANES)
        copies = 7 + 10 + inner - 1 + 8 + 2 + 3 * (outer - 1)
        scratch = dict(
            x=vm(9, LEVELS, TALL, LANES), lm=pltpu.VMEM((LEVELS, ROWS, LANES), jnp.int32),
            bl=pltpu.VMEM((ROWS, LANES), jnp.int32), stv=vm(ROWS, LANES),
            c1=vm(3, ROWS, LANES), ce1=vm(ROWS, LANES), cw1=vm(ROWS, LANES), pw1=vm(80, LANES), pe1=vm(80, LANES),
            cl=vm(2, ROWS, LANES), pwl=vm(2, 80, LANES), pel=vm(2, 80, LANES), m1=vm(3, 80, LANES), mr=vm(80, LANES),
            rn=vm(9, 16, LANES), rs=vm(9, 16, LANES), got_s=vm(9, 16, LANES), got_n=vm(9, 16, LANES),
            tot=vm(8, LANES), inn=vm(2, 8, LANES), slot1=vm(max(inner - 1, 1), 8, LANES), gsum=vm(8, LANES),
            slot2=vm(max(3 * (outer - 1), 1), 8, LANES), inn_w=vm(2, 8, LANES), inn_e=vm(2, 8, LANES), sfx=vm(96, LANES),
            um0=level, umw=level, vm0=level, we=level, wew=level, wn=level, z1=level, z1w=level,
            mm1=level, mm1e=level, wne=level, tmp3=vm(TALL, LANES), sut=vm(TALL, LANES), svt=vm(TALL, LANES),
            acc=vm(8, ROWS, LANES), acx=vm(8, 64, LANES), ce2=vm(ROWS, LANES), cw2=vm(ROWS, LANES), pw2=vm(80, LANES),
            pe2=vm(80, LANES), m2=vm(2, 80, LANES), sa=vm(11, WIDE, LANES), sb=vm(11, 80, LANES),
            st=vm(3, 2, WIDE, LANES), ou2=vm(2, 2, 80, LANES), cd2=vm(2, 2, 80, LANES), wt2=vm(2, 80, LANES), wte=vm(2, 80, LANES),
            ff2=vm(2, 2, 80, LANES), ga=vm(SUBCYCLES, 2, 2, 80, LANES), gb=vm(SUBCYCLES, 2, 2, 80, LANES),
            fg=vm(2, 2, 80, LANES), tmpb=vm(2, WIDE, LANES), gg=vm(4, 64, LANES),
            in_sem=pltpu.SemaphoreType.DMA((13,)), send_sem=pltpu.SemaphoreType.DMA((copies,)),
            recv_sem=pltpu.SemaphoreType.DMA((copies,)),
            ready=pltpu.SemaphoreType.REGULAR((2,)),
        )

        def body(*refs):
            kernel(nlon, nlat, inner, *refs)

        parts = pl.pallas_call(
            body,
            out_shape=[cube, cube, cube, cube, plane],
            in_specs=[pl.BlockSpec(memory_space=pltpu.HBM)] * 13,
            out_specs=[pl.BlockSpec(memory_space=pltpu.VMEM)] * 5,
            scratch_shapes=list(scratch.values()),
            compiler_params=pltpu.CompilerParams(
                collective_id=0, has_side_effects=True, vmem_limit_bytes=40 * 1024 * 1024
            ),
        )(*(pltpu.with_memory_space_constraint(a, pltpu.HBM) for a in args))
        return pl.pallas_call(
            store_kernel,
            out_shape=[cube, cube, cube, cube, plane],
            in_specs=[pl.BlockSpec(memory_space=pltpu.VMEM)] * 5,
            out_specs=[pl.BlockSpec(memory_space=pltpu.HBM)] * 5,
            scratch_shapes=[pltpu.SemaphoreType.DMA((5,))],
            compiler_params=pltpu.CompilerParams(vmem_limit_bytes=4 * 1024 * 1024),
        )(*parts)

    specs = (deep, deep, deep, deep, flat, deep, flat, deep, deep, deep, deep, flat, flat)
    return jax.shard_map(
        step, mesh=mesh, in_specs=specs, out_specs=(deep, deep, deep, deep, flat), check_vma=False
    )
```

```python
import jax
import jax.numpy as jnp
from jax import lax
from jax.experimental import pallas as pl
from jax.experimental.pallas import tpu as pltpu
from jax.sharding import PartitionSpec as P

MESH = pl.DeviceIdType.MESH
F32 = jnp.float32
SUBCYCLES = 8
LEVELS = 8
ROWS = 48
LANES = 128
HALO = 16

ADVECT = 0.25
DIFFUSION = 0.1
HEAT_COEF = 0.5
SALT_COEF = 0.4
PRESS_COEF = 0.3
CORIOLIS = 0.3
DRAG_COEF = 0.5
DIVERGENCE = 0.5
SLOPE_COEF = 0.5
FRICTION = 0.05
THICK_COEF = 0.3

CT, CS, WU, WV, WET, AT, AS, WZ, WM = range(9)
PACK = ((0, 0), (0, 1), (0, 2), (0, 3), (1, 0), (2, 0), (2, 1), (2, 2), (2, 3))
OWN = slice(16, 64)
ZR = slice(16, 72)
MR = slice(8, 64)
TALL = 80
BODY = slice(8, 88)
MINE = slice(24, 72)
WIDE = 96
SF_H, SF_HADJ, SF_WT, SF_U, SF_V, SF_FU, SF_FV, SF_CU, SF_CV, SF_SU, SF_SV = range(11)
SIDES = ((1, 0), (-1, 0), (0, 1), (0, -1), (1, 1), (-1, 1), (1, -1), (-1, -1))


def roll(x, shift):
    return pltpu.roll(x, shift, axis=x.ndim - 1)


def lanes_of(rows):
    return lax.broadcasted_iota(jnp.int32, (rows, LANES), 1)


def pair_east(a, b):
    last = lanes_of(a.shape[0]) == LANES - 1
    ra, rb = roll(a, LANES - 1), roll(b, LANES - 1)
    return jnp.where(last, rb, ra), jnp.where(last, ra, rb)


def pair_west(a, b):
    first = lanes_of(a.shape[0]) == 0
    ra, rb = roll(a, 1), roll(b, 1)
    return jnp.where(first, rb, ra), jnp.where(first, ra, rb)


def kernel(
    nlon, nlat, inner,
    tracer, salinity, zonal, merid, surface, mask, bottom, tr_adj, sa_adj, zo_adj, me_adj, su_adj, st_adj,
    out_t, out_s, out_u, out_v, out_h,
    x, lm, bl, stv, c1, ce1, cw1, pw1, pe1, cl, pwl, pel, m1, mr, rn, rs, got_s, got_n,
    tot, inn, slot1, gsum, slot2, inn_w, inn_e, sfx,
    um0, umw, vm0, we, wew, wn, z1, z1w, mm1, mm1e, wne, tmp3, sut, svt,
    acc, acx, ce2, cw2, pw2, pe2, m2, sa, sb, st, ou2, cd2, wt2, wte, ff2, ga, gb, fg, tmpb, gg,
    in_sem, send_sem, recv_sem, ready,
):
    lon, lat = lax.axis_index("lon"), lax.axis_index("lat")
    south_here, north_here = lat > 0, lat < nlat - 1
    outer = nlat // inner
    gi, go = lax.rem(lat, inner), lat // inner

    def at(dlon, dlat):
        return (lax.rem(lon + dlon + nlon, nlon), lax.rem(lat + dlat + nlat, nlat))

    def when(condition, action):
        if condition is None:
            action()
        else:
            pl.when(condition)(action)

    around = [at(*side) for side in SIDES]
    exists = [{0: None, 1: north_here, -1: south_here}[side[1]] for side in SIDES]
    from_it = [{0: None, 1: south_here, -1: north_here}[side[1]] for side in SIDES]

    def signal(sem, where, condition):
        when(condition, lambda: pl.semaphore_signal(sem, inc=1, device_id=where, device_id_type=MESH))

    barrier = pltpu.get_barrier_semaphore()
    for where, condition in zip(around, exists):
        signal(barrier, where, condition)
    chip, even = gi // 2, lax.rem(go, 2) == 0
    mates = []
    for d in range(1, inner):
        there = lax.rem(gi + d, inner)
        greets = jnp.logical_not(even) | (there // 2 >= chip)
        greeted = jnp.logical_not(even) | (there // 2 <= chip)
        mates.append(((lon, go * inner + there), greets, greeted))
    peers = []
    for e in range(1, outer):
        there = lax.rem(go + e, outer)
        down = go > there
        facing = jnp.where(lax.rem(there + go, 2) == 0, gi, inner - 1 - gi)
        hasty = jnp.where(down, go, there) % 2 < jnp.where(down, there, go) % 2
        for c in (1, -1, 0):
            where = (lax.rem(lon + c + nlon, nlon), there * inner + facing)
            peers.append((where, down == hasty, down != hasty, down, hasty))
    greeted_by = 2 + jnp.where(south_here, 3, 0) + jnp.where(north_here, 3, 0)
    answers = [0, 0]
    for where, greets, greeted in mates:
        signal(barrier, where, greets)
        greeted_by = greeted_by + jnp.where(greeted, 1, 0)
        answers[0] = answers[0] + jnp.where(greeted, 0, 1)
    for where, greets, greeted, down, hasty in peers:
        signal(barrier, where, greets)
        greeted_by = greeted_by + jnp.where(greeted, 1, 0)
        answers[1] = answers[1] + jnp.where(down & hasty, 1, 0)

    def answer():
        for where, greets, _ in mates:
            signal(ready.at[0], where, jnp.logical_not(greets))
        for where, _, _, down, hasty in peers:
            signal(ready.at[1], where, hasty & jnp.logical_not(down))

    def wait_answers(n):
        when(answers[n] > 0, lambda: pl.semaphore_wait(ready.at[n], answers[n]))

    loads = []
    for src, dst in (
        (st_adj, stv), (mask, lm), (bottom, bl),
        (tracer, x.at[CT, :, OWN]), (salinity, x.at[CS, :, OWN]), (zonal, x.at[WU, :, OWN]), (merid, x.at[WV, :, OWN]),
        (surface, sa.at[SF_H, MINE]), (su_adj, sa.at[SF_HADJ, MINE]),
        (tr_adj, x.at[AT, :, OWN]), (sa_adj, x.at[AS, :, OWN]), (zo_adj, x.at[WZ, :, OWN]), (me_adj, x.at[WM, :, OWN]),
    ):
        copy = pltpu.make_async_copy(src, dst, in_sem.at[len(loads)])
        copy.start()
        loads.append(copy)

    sent = []

    def send(src, dst, where, to=None, by=None, now=None):
        n = len(sent)
        copy = pltpu.make_async_remote_copy(
            src_ref=src, dst_ref=dst, send_sem=send_sem.at[n], recv_sem=recv_sem.at[n],
            device_id=where, device_id_type=MESH,
        )
        if now is not False:
            when(to if now is None else now, copy.start)
        sent.append((copy, to))
        return copy, by

    def arrive(copies):
        for copy, by in copies:
            when(by, copy.wait_recv)

    pad = jnp.zeros((8, LANES), F32)
    loads[0].wait()
    tile_sum = stv[0:8]
    for r in range(1, ROWS // 8):
        tile_sum = tile_sum + stv[8 * r : 8 * r + 8]
    tot[...] = tile_sum
    for copy in loads[1:9]:
        copy.wait()

    lane = lanes_of(ROWS)
    EARLY, LATE = (CT, CS, WU, WV, WET), (AT, AS, WZ, WM)

    def mask_fields(fields):
        def mask_level(k, _):
            if WET in fields:
                wet = jnp.where((lm[k] > 0) & (k < bl[...]), 1.0, 0.0).astype(F32)
            else:
                wet = x[WET, k, OWN]
            packs = {PACK[f][0]: c1[PACK[f][0]] for f in fields}
            for f in fields:
                n, s = PACK[f]
                value = wet if f == WET else x[f, k, OWN] * wet
                x[f, k, OWN] = value
                here = lax.shift_right_logical(lane, 2) == 8 * s + k
                packs[n] = jnp.where(here, roll(value, 32 * s + 4 * k + 2), packs[n])
            for n, value in packs.items():
                c1[n] = value
            return 0

        lax.fori_loop(0, LEVELS, mask_level, 0, unroll=4)

        def pack_rows(f, _):
            for k in range(LEVELS):
                rs[f, 2 * k : 2 * k + 2] = x[f, k, 16:18]
                rn[f, 2 * k : 2 * k + 2] = x[f, k, 62:64]
            return 0

        lax.fori_loop(fields[0], fields[-1] + 1, pack_rows, 0)

    c1[1] = jnp.zeros((ROWS, LANES), F32)
    mask_fields(EARLY)
    fine, coarse = (lane & 3) < 2, (lane & 31) < 16
    ce1[...] = jnp.where(fine, c1[0], roll(c1[1], 2))
    cw1[...] = jnp.where(fine, roll(c1[1], LANES - 2), c1[0])
    pl.semaphore_wait(barrier, greeted_by)

    def send_all(table):
        return [send(src, dst, around[n], exists[n], from_it[n]) for n, src, dst in table]

    def rows_table(first, last):
        here = slice(first, last)
        return [(2, rn.at[here], got_s.at[here]), (3, rs.at[here], got_n.at[here])]

    def planes_table(first, last):
        here = slice(first, last)
        return [(2, sa.at[here, 56:72], sa.at[here, 8:24]), (3, sa.at[here, 24:40], sa.at[here, 72:88])]

    LOW, HIGH = slice(0, 16), slice(32, 48)
    phase1 = send_all(
        [
            (5, cw1.at[40:48], pe1.at[8:16]),
            (6, ce1.at[0:8], pw1.at[64:72]),
            (7, cw1.at[0:8], pe1.at[64:72]),
            (0, ce1, pw1.at[16:64]),
            (1, cw1, pe1.at[16:64]),
        ]
        + rows_table(0, 5)
    )
    up1 = [send(tot, slot1.at[n], mate[0], now=False) for n, mate in enumerate(mates)]

    def member_sums():
        wait_answers(0)
        for copy, _ in up1:
            copy.start()

    pl.when(jnp.logical_not(even))(member_sums)
    answer()

    for copy in loads[9:]:
        copy.wait()
    mask_fields(LATE)
    sa[SF_WT, MINE] = x[WET, 0, OWN]
    pack = roll(sa[SF_H, MINE], 16)
    for s, f in ((1, SF_HADJ), (2, SF_WT)):
        here = lax.shift_right_logical(lane, 5) == s
        pack = jnp.where(here, roll(sa[f, MINE], 32 * s + 16), pack)
    cl[0] = c1[2]
    cl[1] = pack
    late1 = send_all(
        rows_table(5, 9)
        + [
            (0, cl, pwl.at[:, 16:64]),
            (1, cl, pel.at[:, 16:64]),
            (4, cl.at[:, HIGH], pwl.at[:, 0:16]),
            (5, cl.at[:, HIGH], pel.at[:, 0:16]),
            (6, cl.at[:, LOW], pwl.at[:, 64:80]),
            (7, cl.at[:, LOW], pel.at[:, 64:80]),
        ]
        + planes_table(0, 3)
    )

    pl.when(even)(member_sums)

    sfx[0:48] = stv[...]
    for r in range(6):
        sfx[48 + 8 * r : 56 + 8 * r] = pad
    for step in (1, 2, 4, 8, 16, 32):
        moved = sfx[0:48] + sfx[step : step + 48]
        sfx[0:48] = moved
    for n in range(3):
        for p in range(2):
            st[n, p, 0:8] = pad
            st[n, p, 88:96] = pad
    for p in range(2):
        tmpb[p, 8:16] = pad
    acc[...] = jnp.zeros_like(acc)
    acx[...] = jnp.zeros_like(acx)

    up2 = [send(inn, inn_w, around[0], now=False), send(inn, inn_e, around[1], now=False)]
    for n, (where, _, _, down, hasty) in enumerate(peers):
        come = lax.rem(go - n // 3 - 1 + outer, outer) > go
        up2.append(send(gsum, slot2.at[n], where, down, come, False))

    def group_sums():
        arrive(up1)
        group = tot[...]
        above = jnp.zeros((8, LANES), F32)
        for d in range(1, inner):
            got = slot1[d - 1]
            group = group + got
            above = above + jnp.where(lax.rem(gi - d + inner, inner) > gi, got, 0.0)
        gsum[...] = group
        inn[0] = above
        inn[1] = tot[...]
        for copy, _ in up2[:2]:
            copy.start()
        for (copy, _), (_, _, _, down, hasty) in zip(up2[2:], peers):
            when(down & jnp.logical_not(hasty), copy.start)

    pl.when(jnp.logical_not(even))(group_sums)
    arrive(phase1)
    def unpack_rows(f, _):
        for k in range(LEVELS):
            x[f, k, 14:16] = jnp.where(south_here, got_s[f, 2 * k : 2 * k + 2], 0.0)
            x[f, k, 64:66] = jnp.where(north_here, got_n[f, 2 * k : 2 * k + 2], 0.0)
        return 0

    lax.fori_loop(0, 5, unpack_rows, 0)
    lane80 = lanes_of(80)
    rows80 = lax.broadcasted_iota(jnp.int32, (80, LANES), 0)
    inside = ((rows80 >= 16) | south_here) & ((rows80 < 64) | north_here)
    fine = (lane80 & 3) < 2
    coarse = (lane80 & 31) < 16

    rim_w, rim_e = pw1[...], pe1[...]
    m1[0] = jnp.where(inside, jnp.where(fine, rim_w, rim_e), 0.0)
    m1[1] = jnp.where(inside, jnp.where(fine, roll(rim_w, LANES - 2), roll(rim_e, 2)), 0.0)

    def strip(f, k, rows):
        n, s = PACK[f]
        return roll(m1[n, rows], 126 - 32 * s - 4 * k)

    def shifted(value, rim, offset):
        ids = lanes_of(value.shape[0])
        if offset > 0:
            return roll(jnp.where(ids < offset, rim, value), LANES - offset)
        return roll(jnp.where(ids >= LANES + offset, rim, value), -offset)

    row_ids = lax.broadcasted_iota(jnp.int32, (64, LANES), 0) + (lat * ROWS - 8)
    cor = -(1.0 + row_ids.astype(F32) / (ROWS * nlat))

    EXT = slice(8, 72)

    def forward_level(k, _):
        wet = x[WET, k, EXT]
        wet_e = shifted(wet, strip(WET, k, EXT), 1)
        tmp3[EXT] = wet_e
        wet_n = x[WET, k, 9:73]
        east, north = wet * wet_e, wet * wet_n
        we[k, EXT] = east
        wn[k, EXT] = north
        wu, wv = x[WU, k, EXT], x[WV, k, EXT]
        u0 = wu * wet_e
        v0 = wv * wet_n
        uw = shifted(wu, strip(WU, k, EXT), -1) * wet
        ve = shifted(wv, strip(WV, k, EXT), 1) * tmp3[9:73]
        um0[k, EXT] = u0
        umw[k, EXT] = uw
        vm0[k, EXT] = v0
        sut[EXT] = u0 + uw
        svt[EXT] = v0 + ve
        acc[6] = acc[6] + x[WZ, k, OWN] * wet_e[8:56]
        acc[7] = acc[7] + x[WM, k, OWN] * wet_n[8:56]
        acx[1] = acx[1] + east
        acx[3] = acx[3] + north

        t0 = SALT_COEF * x[CS, k, OWN] - HEAT_COEF * x[CT, k, OWN]
        tn = SALT_COEF * x[CS, k, 17:65] - HEAT_COEF * x[CT, k, 17:65]
        te = shifted(t0, SALT_COEF * strip(CS, k, OWN) - HEAT_COEF * strip(CT, k, OWN), 1)
        dpe = acc[4] + (te - t0)
        dpn = acc[5] + (tn - t0)
        acc[4] = dpe
        acc[5] = dpn
        own = slice(8, 56)
        drag = jnp.where(bl[...] - 1 == k, 1.0 - DRAG_COEF, 1.0)
        uo, vo = u0[own], v0[own]
        vu = (0.25 * CORIOLIS) * cor[own] * (svt[OWN] + svt[15:63])
        uv = (0.25 * CORIOLIS) * cor[own] * (sut[OWN] + sut[17:65])
        zn = uo * drag + east[own] * (vu - (PRESS_COEF / LEVELS) * dpe)
        mn = vo * drag - north[own] * (uv + (PRESS_COEF / LEVELS) * dpn)
        acc[0] = acc[0] + uo
        acc[1] = acc[1] + vo
        acc[2] = acc[2] + zn
        acc[3] = acc[3] + mn
        return 0

    tmp3[72:80] = pad
    lax.fori_loop(0, LEVELS, forward_level, 0, unroll=2)

    def over(num, count):
        return num / jnp.maximum(count, 1.0)

    own = slice(8, 56)
    cu, cv = acx[1, own], acx[3, own]
    near = sfx[0:48] - jnp.where(row_ids[0:48] - (lat * ROWS - 8) < ROWS // 2, sfx[0:1], 0.0)
    surf = [
        acc[0] / LEVELS, acc[1] / LEVELS,
        (acc[2] - acc[0]) / (LEVELS * SUBCYCLES), (acc[3] - acc[1]) / (LEVELS * SUBCYCLES),
        cu, cv,
        LEVELS * over(acc[6], cu) + near,
        LEVELS * over(acc[7], cv),
    ]
    packs = []
    for n in range(2):
        pack = None
        for s in range(4):
            value = surf[4 * n + s]
            sa[SF_U + 4 * n + s, MINE] = value
            turned = roll(value, (32 * s + 16) % LANES)
            pack = turned if s == 0 else jnp.where(lax.shift_right_logical(lane, 5) == s, turned, pack)
        packs.append(pack)
    own_coarse = (lane & 31) < 16
    ce2[...] = jnp.where(own_coarse, packs[0], roll(packs[1], 16))
    cw2[...] = jnp.where(own_coarse, roll(packs[1], LANES - 16), packs[0])
    phase2 = send_all(
        [
            (4, ce2.at[HIGH], pw2.at[0:16]),
            (5, cw2.at[HIGH], pe2.at[0:16]),
            (6, ce2.at[LOW], pw2.at[64:80]),
            (7, cw2.at[LOW], pe2.at[64:80]),
            (0, ce2, pw2.at[16:64]),
            (1, cw2, pe2.at[16:64]),
        ]
        + planes_table(3, 11)
    )
    pl.when(even)(group_sums)
    wait_answers(1)
    for copy, (_, _, _, down, hasty) in zip(up2[2:], peers):
        when(down & hasty, copy[0].start)
    arrive(late1)
    lax.fori_loop(5, 9, unpack_rows, 0)
    m1[2] = jnp.where(inside, jnp.where(fine, pwl[0], pel[0]), 0.0)
    mr[...] = jnp.where(inside, jnp.where(coarse, pwl[1], pel[1]), 0.0)

    def advect_level(k, _):
        wet_rim = strip(WET, k, OWN)
        wet = x[WET, k, OWN]
        u_rim, wu = strip(WU, k, OWN), x[WU, k, OWN]
        u0, u_w = um0[k, OWN], umw[k, OWN]
        u_ww = shifted(wu, u_rim, -2) * shifted(wet, wet_rim, -1)
        u_e = shifted(wu, u_rim, 1) * shifted(wet, wet_rim, 2)
        we0, we_w = we[k, OWN], wet * shifted(wet, wet_rim, -1)
        v0, v_s, v_ss, v_n = vm0[k, OWN], vm0[k, 15:63], vm0[k, 14:62], vm0[k, 17:65]
        wn0, wn_s = wn[k, OWN], wn[k, 15:63]
        grad_u = jnp.zeros((ROWS, LANES), F32)
        grad_v = jnp.zeros((ROWS, LANES), F32)
        for c, a, out in ((CT, AT, out_t), (CS, AS, out_s)):
            a0, a_rim = x[a, k, OWN], strip(a, k, OWN)
            c0, c_rim = x[c, k, OWN], strip(c, k, OWN)
            a_e, a_ee = shifted(a0, a_rim, 1), shifted(a0, a_rim, 2)
            a_w, a_ww = shifted(a0, a_rim, -1), shifted(a0, a_rim, -2)
            d0, d_w, d_ww, d_e = a_e - a0, a0 - a_w, a_w - a_ww, a_ee - a_e
            c_e, c_ee, c_w = shifted(c0, c_rim, 1), shifted(c0, c_rim, 2), shifted(c0, c_rim, -1)
            grad_u = grad_u + d0 * ((ADVECT * 7.0 / 12.0) * (c0 + c_e) - (ADVECT / 12.0) * (c_w + c_ee))
            grad = a0 + (ADVECT * 7.0 / 12.0) * (u0 * d0 + u_w * d_w) - (ADVECT / 12.0) * (u_e * d_e + u_ww * d_ww)
            grad = grad + DIFFUSION * (we0 * d0 - we_w * d_w)
            a_n, a_nn, a_s, a_ss = x[a, k, 17:65], x[a, k, 18:66], x[a, k, 15:63], x[a, k, 14:62]
            d0, d_s, d_ss, d_n = a_n - a0, a0 - a_s, a_s - a_ss, a_nn - a_n
            c_n, c_nn, c_s = x[c, k, 17:65], x[c, k, 18:66], x[c, k, 15:63]
            grad_v = grad_v + d0 * ((ADVECT * 7.0 / 12.0) * (c0 + c_n) - (ADVECT / 12.0) * (c_s + c_nn))
            grad = grad + (ADVECT * 7.0 / 12.0) * (v0 * d0 + v_s * d_s) - (ADVECT / 12.0) * (v_n * d_n + v_ss * d_ss)
            grad = grad + DIFFUSION * (wn0 * d0 - wn_s * d_s)
            out[k] = grad
        out_u[k] = grad_u
        out_v[k] = grad_v
        wet_x = x[WET, k, EXT]
        rim_x = strip(WET, k, EXT)
        wet_ex = shifted(wet_x, rim_x, 1)
        tmp3[EXT] = wet_ex
        wet_en = tmp3[9:73]
        east_w = wet_x * shifted(wet_x, rim_x, -1)
        north_e = wet_ex * wet_en
        z_w = shifted(x[WZ, k, EXT], strip(WZ, k, EXT), -1) * wet_x
        m_e = shifted(x[WM, k, EXT], strip(WM, k, EXT), 1) * wet_en
        wew[k, EXT] = east_w
        wne[k, EXT] = north_e
        z1w[k, EXT] = z_w
        mm1e[k, EXT] = m_e
        zz = x[WZ, k, EXT] * wet_ex
        mz = x[WM, k, EXT] * x[WET, k, 9:73]
        z1[k, EXT] = zz
        mm1[k, EXT] = mz
        acx[0] = acx[0] + zz
        acx[2] = acx[2] + mz
        acx[4] = acx[4] + z_w
        acx[5] = acx[5] + east_w
        acx[6] = acx[6] + m_e
        acx[7] = acx[7] + north_e
        return 0

    lax.fori_loop(0, LEVELS, advect_level, 0)

    arrive(phase2)

    rim_lane = (lane80 < HALO) | (lane80 >= LANES - HALO)
    rim_w, rim_e = pw2[...], pe2[...]
    m2[0] = jnp.where(inside, jnp.where(coarse, rim_w, rim_e), 0.0)
    m2[1] = jnp.where(inside, jnp.where(coarse, roll(rim_w, LANES - 16), roll(rim_e, 16)), 0.0)
    for f in range(11):
        source, s = (mr[...], f) if f < 3 else (m2[(f - 3) // 4], (f - 3) % 4)
        sb[f] = jnp.where(rim_lane, roll(source, (LANES - 16 - 32 * s) % LANES), 0.0)

    def part(f, p):
        return jnp.where(inside, sa[f, BODY], 0.0) if p == 0 else sb[f]

    for p in range(2):
        st[0, p, BODY] = part(SF_H, p)
        st[1, p, BODY] = part(SF_U, p)
        st[2, p, BODY] = part(SF_V, p)
        wt2[p] = part(SF_WT, p)
        for d in range(2):
            count = part(SF_CU + d, p)
            opened = jnp.minimum(count, 1.0)
            ou2[d, p] = opened
            cd2[d, p] = (SLOPE_COEF / LEVELS) * count
            ff2[d, p] = opened * part(SF_FU + d, p)
            fg[d, p] = jnp.zeros((80, LANES), F32)

    BOTH = (0, 1)
    wte[0], wte[1] = pair_east(wt2[0], wt2[1])

    def sub_step(n, lo, hi):
        mid, down, up = slice(lo + 8, hi + 8), slice(lo + 7, hi + 7), slice(lo + 9, hi + 9)
        rows = slice(lo, hi)
        u = [st[1, p, mid] for p in BOTH]
        v = [st[2, p, mid] for p in BOTH]
        rest = [st[0, p, mid] - DIVERGENCE * (v[p] - st[2, p, down]) - DIVERGENCE * u[p] for p in BOTH]
        u_w, rest_e = pair_west(*u), pair_east(*rest)
        h = [wt2[p, rows] * (rest[p] + DIVERGENCE * u_w[p]) for p in BOTH]
        h_e = [wte[p, rows] * (rest_e[p] + DIVERGENCE * u[p]) for p in BOTH]
        for p in BOTH:
            st[0, p, mid] = h[p]
        for p in BOTH:
            for d, old, far in ((0, u[p], h_e[p]), (1, v[p], st[0, p, up])):
                slope = far - h[p]
                bend = jnp.tanh(0.5 * (h[p] + far))
                depth = cd2[d, p, rows]
                level = depth * (1.0 + THICK_COEF * bend)
                tilt = depth * (0.5 * THICK_COEF) * (1.0 - bend * bend) * slope
                ga[n, d, p, rows] = level - tilt
                gb[n, d, p, rows] = level + tilt
                st[1 + d, p, mid] = (1.0 - FRICTION) * ou2[d, p, rows] * old + ff2[d, p, rows] - level * slope
        return 0

    lax.fori_loop(0, 3, lambda n, _: sub_step(n, 0, 80), 0, unroll=3)
    lax.fori_loop(3, SUBCYCLES, lambda n, _: sub_step(n, 4, 76), 0, unroll=5)

    arrive(up2)
    sums = []
    for c, source in enumerate((inn_w, inn_e, inn)):
        beyond = source[0]
        for e in range(1, outer):
            beyond = beyond + jnp.where(lax.rem(go - e + outer, outer) > go, slot2[3 * (e - 1) + c], 0.0)
        beyond = jnp.sum(beyond, axis=0, keepdims=True)
        sums.append((beyond, beyond + jnp.sum(source[1], axis=0, keepdims=True)))
    east_half = lanes_of(1) < LANES // 2
    sums = (sums[2], tuple(jnp.where(east_half, e, w) for w, e in zip(sums[0], sums[1])))
    for p in BOTH:
        st[0, p, BODY] = part(SF_HADJ, p)
        suffix = jnp.where(rows80 < HALO + ROWS // 2, sums[p][1], sums[p][0])
        st[1, p, BODY] = part(SF_SU, p) + suffix
        st[2, p, BODY] = part(SF_SV, p)

    mid, down, up, rows = slice(16, 80), slice(15, 79), slice(17, 81), slice(8, 72)

    def back_step(i, _):
        n = SUBCYCLES - 1 - i
        u = [ou2[0, p, rows] * st[1, p, mid] for p in BOTH]
        v = [ou2[1, p, rows] * st[2, p, mid] for p in BOTH]
        for p in BOTH:
            fg[0, p, rows] = fg[0, p, rows] + u[p]
            fg[1, p, rows] = fg[1, p, rows] + v[p]
            tmpb[p, mid] = gb[n, 1, p, rows] * v[p]
        b_u = [gb[n, 0, p, rows] * u[p] for p in BOTH]
        rest = [
            st[0, p, mid] + ga[n, 0, p, rows] * u[p] + (ga[n, 1, p, rows] * v[p] - tmpb[p, down]) for p in BOTH
        ]
        b_w, rest_e = pair_west(*b_u), pair_east(*rest)
        h = [wt2[p, rows] * (rest[p] - b_w[p]) for p in BOTH]
        h_e = [wte[p, rows] * (rest_e[p] - b_u[p]) for p in BOTH]
        for p in BOTH:
            st[0, p, mid] = h[p]
        for p in BOTH:
            st[1, p, mid] = (1.0 - FRICTION) * u[p] - DIVERGENCE * (h[p] - h_e[p])
            st[2, p, mid] = (1.0 - FRICTION) * v[p] - DIVERGENCE * (h[p] - st[0, p, up])
        return 0

    lax.fori_loop(0, SUBCYCLES, back_step, 0, unroll=8)

    out_h[...] = st[0, 0, MINE]
    window = slice(8, 72)
    force = 1.0 / (LEVELS * SUBCYCLES)
    fu, fv = fg[0, 0], fg[1, 0]
    fu_w = pair_west(fu, fg[0, 1])[0]
    fv_e = pair_east(fv, fg[1, 1])[0]
    gg[0] = force * fu[window] - over(acx[0], acx[1])
    gg[1] = force * fu_w[window] - over(acx[4], acx[5])
    gg[2] = force * fv[window] - over(acx[2], acx[3])
    gg[3] = force * fv_e[window] - over(acx[6], acx[7])
    acc[0] = (st[1, 0, MINE] - fu[16:64] / SUBCYCLES) / LEVELS
    acc[1] = (st[2, 0, MINE] - fv[16:64] / SUBCYCLES) / LEVELS

    turn = (0.25 * CORIOLIS) * cor

    def momentum_level(i, press):
        k = LEVELS - 1 - i
        z = z1[k, ZR] + we[k, ZR] * gg[0, 8:64]
        z_w = z1w[k, ZR] + wew[k, ZR] * gg[1, 8:64]
        m = mm1[k, MR] + wn[k, MR] * gg[2, 0:56]
        m_e = mm1e[k, MR] + wne[k, MR] * gg[3, 0:56]
        sut[ZR] = turn[8:64] * (z + z_w)
        svt[MR] = turn[0:56] * (m + m_e)
        tmp3[MR] = m
        z0, m0 = z[0:48], m[8:56]
        press = press + (PRESS_COEF / LEVELS) * ((z0 - z_w[0:48]) + (m0 - tmp3[15:63]))
        drag = jnp.where(bl[...] - 1 == k, 1.0 - DRAG_COEF, 1.0)
        wet = x[WET, k, OWN]
        out_t[k] = wet * (out_t[k] - HEAT_COEF * press)
        out_s[k] = wet * (out_s[k] + SALT_COEF * press)
        out_u[k] = we[k, OWN] * (out_u[k] + z0 * drag - (svt[OWN] + svt[15:63]) + acc[0])
        out_v[k] = wn[k, OWN] * (out_v[k] + m0 * drag + (sut[OWN] + sut[17:65]) + acc[1])
        return press

    lax.fori_loop(0, LEVELS, momentum_level, jnp.zeros((ROWS, LANES), F32))

    for copy, to in sent:
        when(to, copy.wait_send)


def store_kernel(*refs):
    sources, targets, sem = refs[:5], refs[5:10], refs[10]
    copies = [pltpu.make_async_copy(a, b, sem.at[n]) for n, (a, b) in enumerate(zip(sources, targets))]
    for copy in copies:
        copy.start()
    for copy in copies:
        copy.wait()


def solution(mesh):
    nlon, nlat = mesh.shape["lon"], mesh.shape["lat"]
    inner = next(n for n in (8, 4, 2, 1) if nlat % n == 0 and n * n <= 2 * nlat)
    outer = nlat // inner
    deep = P(None, "lat", "lon")
    flat = P("lat", "lon")

    def step(*args):
        vm = lambda *shape: pltpu.VMEM(shape, F32)
        cube = jax.ShapeDtypeStruct((LEVELS, ROWS, LANES), F32)
        plane = jax.ShapeDtypeStruct((ROWS, LANES), F32)
        level = vm(LEVELS, TALL, LANES)
        copies = 7 + 10 + inner - 1 + 8 + 2 + 3 * (outer - 1)
        scratch = dict(
            x=vm(9, LEVELS, TALL, LANES), lm=pltpu.VMEM((LEVELS, ROWS, LANES), jnp.int32),
            bl=pltpu.VMEM((ROWS, LANES), jnp.int32), stv=vm(ROWS, LANES),
            c1=vm(3, ROWS, LANES), ce1=vm(ROWS, LANES), cw1=vm(ROWS, LANES), pw1=vm(80, LANES), pe1=vm(80, LANES),
            cl=vm(2, ROWS, LANES), pwl=vm(2, 80, LANES), pel=vm(2, 80, LANES), m1=vm(3, 80, LANES), mr=vm(80, LANES),
            rn=vm(9, 16, LANES), rs=vm(9, 16, LANES), got_s=vm(9, 16, LANES), got_n=vm(9, 16, LANES),
            tot=vm(8, LANES), inn=vm(2, 8, LANES), slot1=vm(max(inner - 1, 1), 8, LANES), gsum=vm(8, LANES),
            slot2=vm(max(3 * (outer - 1), 1), 8, LANES), inn_w=vm(2, 8, LANES), inn_e=vm(2, 8, LANES), sfx=vm(96, LANES),
            um0=level, umw=level, vm0=level, we=level, wew=level, wn=level, z1=level, z1w=level,
            mm1=level, mm1e=level, wne=level, tmp3=vm(TALL, LANES), sut=vm(TALL, LANES), svt=vm(TALL, LANES),
            acc=vm(8, ROWS, LANES), acx=vm(8, 64, LANES), ce2=vm(ROWS, LANES), cw2=vm(ROWS, LANES), pw2=vm(80, LANES),
            pe2=vm(80, LANES), m2=vm(2, 80, LANES), sa=vm(11, WIDE, LANES), sb=vm(11, 80, LANES),
            st=vm(3, 2, WIDE, LANES), ou2=vm(2, 2, 80, LANES), cd2=vm(2, 2, 80, LANES), wt2=vm(2, 80, LANES), wte=vm(2, 80, LANES),
            ff2=vm(2, 2, 80, LANES), ga=vm(SUBCYCLES, 2, 2, 80, LANES), gb=vm(SUBCYCLES, 2, 2, 80, LANES),
            fg=vm(2, 2, 80, LANES), tmpb=vm(2, WIDE, LANES), gg=vm(4, 64, LANES),
            in_sem=pltpu.SemaphoreType.DMA((13,)), send_sem=pltpu.SemaphoreType.DMA((copies,)),
            recv_sem=pltpu.SemaphoreType.DMA((copies,)),
            ready=pltpu.SemaphoreType.REGULAR((2,)),
        )

        def body(*refs):
            kernel(nlon, nlat, inner, *refs)

        parts = pl.pallas_call(
            body,
            out_shape=[cube, cube, cube, cube, plane],
            in_specs=[pl.BlockSpec(memory_space=pltpu.HBM)] * 13,
            out_specs=[pl.BlockSpec(memory_space=pltpu.VMEM)] * 5,
            scratch_shapes=list(scratch.values()),
            compiler_params=pltpu.CompilerParams(
                collective_id=0, has_side_effects=True, vmem_limit_bytes=40 * 1024 * 1024
            ),
        )(*(pltpu.with_memory_space_constraint(a, pltpu.HBM) for a in args))
        return pl.pallas_call(
            store_kernel,
            out_shape=[cube, cube, cube, cube, plane],
            in_specs=[pl.BlockSpec(memory_space=pltpu.VMEM)] * 5,
            out_specs=[pl.BlockSpec(memory_space=pltpu.HBM)] * 5,
            scratch_shapes=[pltpu.SemaphoreType.DMA((5,))],
            compiler_params=pltpu.CompilerParams(vmem_limit_bytes=4 * 1024 * 1024),
        )(*parts)

    specs = (deep, deep, deep, deep, flat, deep, flat, deep, deep, deep, deep, flat, flat)
    return jax.shard_map(
        step, mesh=mesh, in_specs=specs, out_specs=(deep, deep, deep, deep, flat), check_vma=False
    )
```

```python
import jax
import jax.numpy as jnp
from jax import lax
from jax.experimental import pallas as pl
from jax.experimental.pallas import tpu as pltpu
from jax.sharding import PartitionSpec as P

MESH = pl.DeviceIdType.MESH
F32 = jnp.float32
SUBCYCLES = 8
LEVELS = 8
ROWS = 48
LANES = 128
HALO = 16

ADVECT = 0.25
DIFFUSION = 0.1
HEAT_COEF = 0.5
SALT_COEF = 0.4
PRESS_COEF = 0.3
CORIOLIS = 0.3
DRAG_COEF = 0.5
DIVERGENCE = 0.5
SLOPE_COEF = 0.5
FRICTION = 0.05
THICK_COEF = 0.3

CT, CS, WU, WV, WET, AT, AS, WZ, WM = range(9)
PACK = ((0, 0), (0, 1), (0, 2), (0, 3), (1, 0), (2, 0), (2, 1), (2, 2), (2, 3))
OWN = slice(16, 64)
ZR = slice(16, 72)
MR = slice(8, 64)
TALL = 80
BODY = slice(8, 88)
MINE = slice(24, 72)
WIDE = 96
SF_H, SF_HADJ, SF_WT, SF_U, SF_V, SF_FU, SF_FV, SF_CU, SF_CV, SF_SU, SF_SV = range(11)
SIDES = ((1, 0), (-1, 0), (0, 1), (0, -1), (1, 1), (-1, 1), (1, -1), (-1, -1))


def roll(x, shift):
    return pltpu.roll(x, shift, axis=x.ndim - 1)


def lanes_of(rows):
    return lax.broadcasted_iota(jnp.int32, (rows, LANES), 1)


def pair_east(a, b):
    last = lanes_of(a.shape[0]) == LANES - 1
    ra, rb = roll(a, LANES - 1), roll(b, LANES - 1)
    return jnp.where(last, rb, ra), jnp.where(last, ra, rb)


def pair_west(a, b):
    first = lanes_of(a.shape[0]) == 0
    ra, rb = roll(a, 1), roll(b, 1)
    return jnp.where(first, rb, ra), jnp.where(first, ra, rb)


def kernel(
    nlon, nlat, inner,
    tracer, salinity, zonal, merid, surface, mask, bottom, tr_adj, sa_adj, zo_adj, me_adj, su_adj, st_adj,
    out_t, out_s, out_u, out_v, out_h,
    x, lm, bl, stv, c1, ce1, cw1, pw1, pe1, cl, pwl, pel, m1, mr, rn, rs, got_s, got_n,
    tot, inn, slot1, gsum, slot2, inn_w, inn_e, sfx,
    um0, umw, vm0, we, wew, wn, z1, z1w, mm1, mm1e, wne, tmp3, sut, svt,
    acc, acx, ce2, cw2, pw2, pe2, m2, sa, sb, st, ou2, cd2, wt2, wte, ff2, ga, gb, fg, tmpb, gg,
    in_sem, send_sem, recv_sem, ready,
):
    lon, lat = lax.axis_index("lon"), lax.axis_index("lat")
    south_here, north_here = lat > 0, lat < nlat - 1
    outer = nlat // inner
    gi, go = lax.rem(lat, inner), lat // inner

    def at(dlon, dlat):
        return (lax.rem(lon + dlon + nlon, nlon), lax.rem(lat + dlat + nlat, nlat))

    def when(condition, action):
        if condition is None:
            action()
        else:
            pl.when(condition)(action)

    around = [at(*side) for side in SIDES]
    exists = [{0: None, 1: north_here, -1: south_here}[side[1]] for side in SIDES]
    from_it = [{0: None, 1: south_here, -1: north_here}[side[1]] for side in SIDES]

    def signal(sem, where, condition):
        when(condition, lambda: pl.semaphore_signal(sem, inc=1, device_id=where, device_id_type=MESH))

    barrier = pltpu.get_barrier_semaphore()
    for where, condition in zip(around, exists):
        signal(barrier, where, condition)
    chip, even = gi // 2, lax.rem(go, 2) == 0
    mates = []
    for d in range(1, inner):
        there = lax.rem(gi + d, inner)
        greets = jnp.logical_not(even) | (there // 2 >= chip)
        greeted = jnp.logical_not(even) | (there // 2 <= chip)
        mates.append(((lon, go * inner + there), greets, greeted))
    peers = []
    for e in range(1, outer):
        there = lax.rem(go + e, outer)
        down = go > there
        facing = jnp.where(lax.rem(there + go, 2) == 0, gi, inner - 1 - gi)
        hasty = jnp.where(down, go, there) % 2 < jnp.where(down, there, go) % 2
        for c in (1, -1, 0):
            where = (lax.rem(lon + c + nlon, nlon), there * inner + facing)
            peers.append((where, down == hasty, down != hasty, down, hasty))
    greeted_by = 2 + jnp.where(south_here, 3, 0) + jnp.where(north_here, 3, 0)
    answers = [0, 0]
    for where, greets, greeted in mates:
        signal(barrier, where, greets)
        greeted_by = greeted_by + jnp.where(greeted, 1, 0)
        answers[0] = answers[0] + jnp.where(greeted, 0, 1)
    for where, greets, greeted, down, hasty in peers:
        signal(barrier, where, greets)
        greeted_by = greeted_by + jnp.where(greeted, 1, 0)
        answers[1] = answers[1] + jnp.where(down & hasty, 1, 0)

    def answer():
        for where, greets, _ in mates:
            signal(ready.at[0], where, jnp.logical_not(greets))
        for where, _, _, down, hasty in peers:
            signal(ready.at[1], where, hasty & jnp.logical_not(down))

    def wait_answers(n):
        when(answers[n] > 0, lambda: pl.semaphore_wait(ready.at[n], answers[n]))

    loads = []
    for src, dst in (
        (st_adj, stv), (mask, lm), (bottom, bl),
        (tracer, x.at[CT, :, OWN]), (salinity, x.at[CS, :, OWN]), (zonal, x.at[WU, :, OWN]), (merid, x.at[WV, :, OWN]),
        (surface, sa.at[SF_H, MINE]), (su_adj, sa.at[SF_HADJ, MINE]),
        (tr_adj, x.at[AT, :, OWN]), (sa_adj, x.at[AS, :, OWN]), (zo_adj, x.at[WZ, :, OWN]), (me_adj, x.at[WM, :, OWN]),
    ):
        copy = pltpu.make_async_copy(src, dst, in_sem.at[len(loads)])
        copy.start()
        loads.append(copy)

    sent = []

    def send(src, dst, where, to=None, by=None, now=None):
        n = len(sent)
        copy = pltpu.make_async_remote_copy(
            src_ref=src, dst_ref=dst, send_sem=send_sem.at[n], recv_sem=recv_sem.at[n],
            device_id=where, device_id_type=MESH,
        )
        if now is not False:
            when(to if now is None else now, copy.start)
        sent.append((copy, to))
        return copy, by

    def arrive(copies):
        for copy, by in copies:
            when(by, copy.wait_recv)

    pad = jnp.zeros((8, LANES), F32)
    loads[0].wait()
    tile_sum = stv[0:8]
    for r in range(1, ROWS // 8):
        tile_sum = tile_sum + stv[8 * r : 8 * r + 8]
    tot[...] = tile_sum
    for copy in loads[1:9]:
        copy.wait()

    lane = lanes_of(ROWS)
    EARLY, LATE = (CT, CS, WU, WV, WET), (AT, AS, WZ, WM)

    def mask_fields(fields):
        def mask_level(k, _):
            if WET in fields:
                wet = jnp.where((lm[k] > 0) & (k < bl[...]), 1.0, 0.0).astype(F32)
            else:
                wet = x[WET, k, OWN]
            packs = {PACK[f][0]: c1[PACK[f][0]] for f in fields}
            for f in fields:
                n, s = PACK[f]
                value = wet if f == WET else x[f, k, OWN] * wet
                x[f, k, OWN] = value
                here = lax.shift_right_logical(lane, 2) == 8 * s + k
                packs[n] = jnp.where(here, roll(value, 32 * s + 4 * k + 2), packs[n])
            for n, value in packs.items():
                c1[n] = value
            return 0

        lax.fori_loop(0, LEVELS, mask_level, 0, unroll=4)

        def pack_rows(f, _):
            for k in range(LEVELS):
                rs[f, 2 * k : 2 * k + 2] = x[f, k, 16:18]
                rn[f, 2 * k : 2 * k + 2] = x[f, k, 62:64]
            return 0

        lax.fori_loop(fields[0], fields[-1] + 1, pack_rows, 0)

    c1[1] = jnp.zeros((ROWS, LANES), F32)
    mask_fields(EARLY)
    fine, coarse = (lane & 3) < 2, (lane & 31) < 16
    ce1[...] = jnp.where(fine, c1[0], roll(c1[1], 2))
    cw1[...] = jnp.where(fine, roll(c1[1], LANES - 2), c1[0])
    pl.semaphore_wait(barrier, greeted_by)

    def send_all(table):
        return [send(src, dst, around[n], exists[n], from_it[n]) for n, src, dst in table]

    def rows_table(first, last):
        here = slice(first, last)
        return [(2, rn.at[here], got_s.at[here]), (3, rs.at[here], got_n.at[here])]

    def planes_table(first, last):
        here = slice(first, last)
        return [(2, sa.at[here, 56:72], sa.at[here, 8:24]), (3, sa.at[here, 24:40], sa.at[here, 72:88])]

    LOW, HIGH = slice(0, 16), slice(32, 48)
    phase1 = send_all(
        [
            (5, cw1.at[40:48], pe1.at[8:16]),
            (6, ce1.at[0:8], pw1.at[64:72]),
            (7, cw1.at[0:8], pe1.at[64:72]),
            (0, ce1, pw1.at[16:64]),
            (1, cw1, pe1.at[16:64]),
        ]
        + rows_table(0, 5)
    )
    up1 = [send(tot, slot1.at[n], mate[0], now=False) for n, mate in enumerate(mates)]

    def member_sums():
        wait_answers(0)
        for copy, _ in up1:
            copy.start()

    pl.when(jnp.logical_not(even))(member_sums)
    answer()

    for copy in loads[9:]:
        copy.wait()
    mask_fields(LATE)
    sa[SF_WT, MINE] = x[WET, 0, OWN]
    pack = roll(sa[SF_H, MINE], 16)
    for s, f in ((1, SF_HADJ), (2, SF_WT)):
        here = lax.shift_right_logical(lane, 5) == s
        pack = jnp.where(here, roll(sa[f, MINE], 32 * s + 16), pack)
    cl[0] = c1[2]
    cl[1] = pack
    late1 = send_all(
        rows_table(5, 9)
        + [
            (0, cl, pwl.at[:, 16:64]),
            (1, cl, pel.at[:, 16:64]),
            (4, cl.at[:, HIGH], pwl.at[:, 0:16]),
            (5, cl.at[:, HIGH], pel.at[:, 0:16]),
            (6, cl.at[:, LOW], pwl.at[:, 64:80]),
            (7, cl.at[:, LOW], pel.at[:, 64:80]),
        ]
        + planes_table(0, 3)
    )

    pl.when(even)(member_sums)

    sfx[0:48] = stv[...]
    for r in range(6):
        sfx[48 + 8 * r : 56 + 8 * r] = pad
    for step in (1, 2, 4, 8, 16, 32):
        moved = sfx[0:48] + sfx[step : step + 48]
        sfx[0:48] = moved
    for n in range(3):
        for p in range(2):
            st[n, p, 0:8] = pad
            st[n, p, 88:96] = pad
    for p in range(2):
        tmpb[p, 8:16] = pad
    acc[...] = jnp.zeros_like(acc)
    acx[...] = jnp.zeros_like(acx)

    up2 = [send(inn, inn_w, around[0], now=False), send(inn, inn_e, around[1], now=False)]
    for n, (where, _, _, down, hasty) in enumerate(peers):
        come = lax.rem(go - n // 3 - 1 + outer, outer) > go
        up2.append(send(gsum, slot2.at[n], where, down, come, False))

    def group_sums():
        arrive(up1)
        group = tot[...]
        above = jnp.zeros((8, LANES), F32)
        for d in range(1, inner):
            got = slot1[d - 1]
            group = group + got
            above = above + jnp.where(lax.rem(gi - d + inner, inner) > gi, got, 0.0)
        gsum[...] = group
        inn[0] = above
        inn[1] = tot[...]
        for copy, _ in up2[:2]:
            copy.start()
        for (copy, _), (_, _, _, down, hasty) in zip(up2[2:], peers):
            when(down & jnp.logical_not(hasty), copy.start)

    pl.when(jnp.logical_not(even))(group_sums)
    arrive(phase1)
    def unpack_rows(f, _):
        for k in range(LEVELS):
            x[f, k, 14:16] = jnp.where(south_here, got_s[f, 2 * k : 2 * k + 2], 0.0)
            x[f, k, 64:66] = jnp.where(north_here, got_n[f, 2 * k : 2 * k + 2], 0.0)
        return 0

    lax.fori_loop(0, 5, unpack_rows, 0)
    lane80 = lanes_of(80)
    rows80 = lax.broadcasted_iota(jnp.int32, (80, LANES), 0)
    inside = ((rows80 >= 16) | south_here) & ((rows80 < 64) | north_here)
    fine = (lane80 & 3) < 2
    coarse = (lane80 & 31) < 16

    rim_w, rim_e = pw1[...], pe1[...]
    m1[0] = jnp.where(inside, jnp.where(fine, rim_w, rim_e), 0.0)
    m1[1] = jnp.where(inside, jnp.where(fine, roll(rim_w, LANES - 2), roll(rim_e, 2)), 0.0)

    def strip(f, k, rows):
        n, s = PACK[f]
        return roll(m1[n, rows], 126 - 32 * s - 4 * k)

    def shifted(value, rim, offset):
        ids = lanes_of(value.shape[0])
        if offset > 0:
            return roll(jnp.where(ids < offset, rim, value), LANES - offset)
        return roll(jnp.where(ids >= LANES + offset, rim, value), -offset)

    row_ids = lax.broadcasted_iota(jnp.int32, (64, LANES), 0) + (lat * ROWS - 8)
    cor = -(1.0 + row_ids.astype(F32) / (ROWS * nlat))

    m2[0] = SALT_COEF * roll(m1[0], LANES - 32) - HEAT_COEF * m1[0]

    EXT = slice(8, 72)

    def forward_level(k, _):
        wet = x[WET, k, EXT]
        wet_e = shifted(wet, strip(WET, k, EXT), 1)
        tmp3[EXT] = wet_e
        wet_n = x[WET, k, 9:73]
        east, north = wet * wet_e, wet * wet_n
        we[k, EXT] = east
        wn[k, EXT] = north
        wu, wv = x[WU, k, EXT], x[WV, k, EXT]
        u0 = wu * wet_e
        v0 = wv * wet_n
        uw = shifted(wu[8:64], strip(WU, k, ZR), -1) * wet[8:64]
        ve = shifted(wv[0:56], strip(WV, k, MR), 1) * tmp3[9:65]
        um0[k, EXT] = u0
        umw[k, ZR] = uw
        vm0[k, EXT] = v0
        sut[ZR] = u0[8:64] + uw
        svt[MR] = v0[0:56] + ve
        acc[6] = acc[6] + x[WZ, k, OWN] * wet_e[8:56]
        acc[7] = acc[7] + x[WM, k, OWN] * wet_n[8:56]
        acx[1] = acx[1] + east
        acx[3] = acx[3] + north

        t0 = SALT_COEF * x[CS, k, OWN] - HEAT_COEF * x[CT, k, OWN]
        tn = SALT_COEF * x[CS, k, 17:65] - HEAT_COEF * x[CT, k, 17:65]
        te = shifted(t0, roll(m2[0, OWN], 126 - 4 * k), 1)
        dpe = acc[4] + (te - t0)
        dpn = acc[5] + (tn - t0)
        acc[4] = dpe
        acc[5] = dpn
        own = slice(8, 56)
        drag = jnp.where(bl[...] - 1 == k, 1.0 - DRAG_COEF, 1.0)
        uo, vo = u0[own], v0[own]
        vu = (0.25 * CORIOLIS) * cor[own] * (svt[OWN] + svt[15:63])
        uv = (0.25 * CORIOLIS) * cor[own] * (sut[OWN] + sut[17:65])
        zn = uo * drag + east[own] * (vu - (PRESS_COEF / LEVELS) * dpe)
        mn = vo * drag - north[own] * (uv + (PRESS_COEF / LEVELS) * dpn)
        acc[0] = acc[0] + uo
        acc[1] = acc[1] + vo
        acc[2] = acc[2] + zn
        acc[3] = acc[3] + mn
        return 0

    tmp3[72:80] = pad
    lax.fori_loop(0, LEVELS, forward_level, 0, unroll=2)

    def over(num, count):
        return num / jnp.maximum(count, 1.0)

    own = slice(8, 56)
    cu, cv = acx[1, own], acx[3, own]
    near = sfx[0:48] - jnp.where(row_ids[0:48] - (lat * ROWS - 8) < ROWS // 2, sfx[0:1], 0.0)
    surf = [
        acc[0] / LEVELS, acc[1] / LEVELS,
        (acc[2] - acc[0]) / (LEVELS * SUBCYCLES), (acc[3] - acc[1]) / (LEVELS * SUBCYCLES),
        cu, cv,
        LEVELS * over(acc[6], cu) + near,
        LEVELS * over(acc[7], cv),
    ]
    packs = []
    for n in range(2):
        pack = None
        for s in range(4):
            value = surf[4 * n + s]
            sa[SF_U + 4 * n + s, MINE] = value
            turned = roll(value, (32 * s + 16) % LANES)
            pack = turned if s == 0 else jnp.where(lax.shift_right_logical(lane, 5) == s, turned, pack)
        packs.append(pack)
    own_coarse = (lane & 31) < 16
    ce2[...] = jnp.where(own_coarse, packs[0], roll(packs[1], 16))
    cw2[...] = jnp.where(own_coarse, roll(packs[1], LANES - 16), packs[0])
    phase2 = send_all(
        [
            (4, ce2.at[HIGH], pw2.at[0:16]),
            (5, cw2.at[HIGH], pe2.at[0:16]),
            (6, ce2.at[LOW], pw2.at[64:80]),
            (7, cw2.at[LOW], pe2.at[64:80]),
            (0, ce2, pw2.at[16:64]),
            (1, cw2, pe2.at[16:64]),
        ]
        + planes_table(3, 11)
    )
    pl.when(even)(group_sums)
    wait_answers(1)
    for copy, (_, _, _, down, hasty) in zip(up2[2:], peers):
        when(down & hasty, copy[0].start)
    arrive(late1)
    lax.fori_loop(5, 9, unpack_rows, 0)
    m1[2] = jnp.where(inside, jnp.where(fine, pwl[0], pel[0]), 0.0)
    mr[...] = jnp.where(inside, jnp.where(coarse, pwl[1], pel[1]), 0.0)

    def advect_level(k, _):
        wet_rim = strip(WET, k, OWN)
        wet = x[WET, k, OWN]
        u_rim, wu = strip(WU, k, OWN), x[WU, k, OWN]
        u0, u_w = um0[k, OWN], umw[k, OWN]
        u_ww = shifted(wu, u_rim, -2) * shifted(wet, wet_rim, -1)
        u_e = shifted(wu, u_rim, 1) * shifted(wet, wet_rim, 2)
        we0, we_w = we[k, OWN], wet * shifted(wet, wet_rim, -1)
        v0, v_s, v_ss, v_n = vm0[k, OWN], vm0[k, 15:63], vm0[k, 14:62], vm0[k, 17:65]
        wn0, wn_s = wn[k, OWN], wn[k, 15:63]
        grad_u = jnp.zeros((ROWS, LANES), F32)
        grad_v = jnp.zeros((ROWS, LANES), F32)
        for c, a, out in ((CT, AT, out_t), (CS, AS, out_s)):
            a0, a_rim = x[a, k, OWN], strip(a, k, OWN)
            c0, c_rim = x[c, k, OWN], strip(c, k, OWN)
            a_e, a_ee = shifted(a0, a_rim, 1), shifted(a0, a_rim, 2)
            a_w, a_ww = shifted(a0, a_rim, -1), shifted(a0, a_rim, -2)
            d0, d_w, d_ww, d_e = a_e - a0, a0 - a_w, a_w - a_ww, a_ee - a_e
            c_e, c_ee, c_w = shifted(c0, c_rim, 1), shifted(c0, c_rim, 2), shifted(c0, c_rim, -1)
            grad_u = grad_u + d0 * ((ADVECT * 7.0 / 12.0) * (c0 + c_e) - (ADVECT / 12.0) * (c_w + c_ee))
            grad = a0 + (ADVECT * 7.0 / 12.0) * (u0 * d0 + u_w * d_w) - (ADVECT / 12.0) * (u_e * d_e + u_ww * d_ww)
            grad = grad + DIFFUSION * (we0 * d0 - we_w * d_w)
            a_n, a_nn, a_s, a_ss = x[a, k, 17:65], x[a, k, 18:66], x[a, k, 15:63], x[a, k, 14:62]
            d0, d_s, d_ss, d_n = a_n - a0, a0 - a_s, a_s - a_ss, a_nn - a_n
            c_n, c_nn, c_s = x[c, k, 17:65], x[c, k, 18:66], x[c, k, 15:63]
            grad_v = grad_v + d0 * ((ADVECT * 7.0 / 12.0) * (c0 + c_n) - (ADVECT / 12.0) * (c_s + c_nn))
            grad = grad + (ADVECT * 7.0 / 12.0) * (v0 * d0 + v_s * d_s) - (ADVECT / 12.0) * (v_n * d_n + v_ss * d_ss)
            grad = grad + DIFFUSION * (wn0 * d0 - wn_s * d_s)
            out[k] = grad
        out_u[k] = grad_u
        out_v[k] = grad_v
        wet_x = x[WET, k, EXT]
        rim_x = strip(WET, k, EXT)
        wet_ex = shifted(wet_x, rim_x, 1)
        tmp3[EXT] = wet_ex
        wet_en = tmp3[9:73]
        east_w = wet_x * shifted(wet_x, rim_x, -1)
        north_e = wet_ex * wet_en
        z_w = shifted(x[WZ, k, EXT], strip(WZ, k, EXT), -1) * wet_x
        m_e = shifted(x[WM, k, EXT], strip(WM, k, EXT), 1) * wet_en
        wew[k, EXT] = east_w
        wne[k, EXT] = north_e
        z1w[k, EXT] = z_w
        mm1e[k, EXT] = m_e
        zz = x[WZ, k, EXT] * wet_ex
        mz = x[WM, k, EXT] * x[WET, k, 9:73]
        z1[k, EXT] = zz
        mm1[k, EXT] = mz
        acx[0] = acx[0] + zz
        acx[2] = acx[2] + mz
        acx[4] = acx[4] + z_w
        acx[5] = acx[5] + east_w
        acx[6] = acx[6] + m_e
        acx[7] = acx[7] + north_e
        return 0

    lax.fori_loop(0, LEVELS, advect_level, 0)

    for copy, to in sent:
        when(to, copy.wait_send)
    arrive(phase2)

    rim_lane = (lane80 < HALO) | (lane80 >= LANES - HALO)
    rim_w, rim_e = pw2[...], pe2[...]
    m2[0] = jnp.where(inside, jnp.where(coarse, rim_w, rim_e), 0.0)
    m2[1] = jnp.where(inside, jnp.where(coarse, roll(rim_w, LANES - 16), roll(rim_e, 16)), 0.0)
    for f in range(11):
        source, s = (mr[...], f) if f < 3 else (m2[(f - 3) // 4], (f - 3) % 4)
        sb[f] = jnp.where(rim_lane, roll(source, (LANES - 16 - 32 * s) % LANES), 0.0)

    def part(f, p):
        return jnp.where(inside, sa[f, BODY], 0.0) if p == 0 else sb[f]

    for p in range(2):
        st[0, p, BODY] = part(SF_H, p)
        st[1, p, BODY] = part(SF_U, p)
        st[2, p, BODY] = part(SF_V, p)
        wt2[p] = part(SF_WT, p)
        for d in range(2):
            count = part(SF_CU + d, p)
            opened = jnp.minimum(count, 1.0)
            ou2[d, p] = opened
            cd2[d, p] = (SLOPE_COEF / LEVELS) * count
            ff2[d, p] = opened * part(SF_FU + d, p)
            fg[d, p] = jnp.zeros((80, LANES), F32)

    BOTH = (0, 1)
    wte[0], wte[1] = pair_east(wt2[0], wt2[1])

    def sub_step(n, lo, hi):
        mid, down, up = slice(lo + 8, hi + 8), slice(lo + 7, hi + 7), slice(lo + 9, hi + 9)
        rows = slice(lo, hi)
        u = [st[1, p, mid] for p in BOTH]
        v = [st[2, p, mid] for p in BOTH]
        rest = [st[0, p, mid] - DIVERGENCE * (v[p] - st[2, p, down]) - DIVERGENCE * u[p] for p in BOTH]
        u_w, rest_e = pair_west(*u), pair_east(*rest)
        h = [wt2[p, rows] * (rest[p] + DIVERGENCE * u_w[p]) for p in BOTH]
        h_e = [wte[p, rows] * (rest_e[p] + DIVERGENCE * u[p]) for p in BOTH]
        for p in BOTH:
            st[0, p, mid] = h[p]
        for p in BOTH:
            for d, old, far in ((0, u[p], h_e[p]), (1, v[p], st[0, p, up])):
                slope = far - h[p]
                bend = jnp.tanh(0.5 * (h[p] + far))
                depth = cd2[d, p, rows]
                level = depth * (1.0 + THICK_COEF * bend)
                tilt = depth * (0.5 * THICK_COEF) * (1.0 - bend * bend) * slope
                ga[n, d, p, rows] = level - tilt
                gb[n, d, p, rows] = level + tilt
                st[1 + d, p, mid] = (1.0 - FRICTION) * ou2[d, p, rows] * old + ff2[d, p, rows] - level * slope
        return 0

    lax.fori_loop(0, 3, lambda n, _: sub_step(n, 0, 80), 0, unroll=3)
    lax.fori_loop(3, SUBCYCLES, lambda n, _: sub_step(n, 4, 76), 0, unroll=5)

    arrive(up2)
    sums = []
    for c, source in enumerate((inn_w, inn_e, inn)):
        beyond = source[0]
        for e in range(1, outer):
            beyond = beyond + jnp.where(lax.rem(go - e + outer, outer) > go, slot2[3 * (e - 1) + c], 0.0)
        beyond = jnp.sum(beyond, axis=0, keepdims=True)
        sums.append((beyond, beyond + jnp.sum(source[1], axis=0, keepdims=True)))
    east_half = lanes_of(1) < LANES // 2
    sums = (sums[2], tuple(jnp.where(east_half, e, w) for w, e in zip(sums[0], sums[1])))
    for p in BOTH:
        st[0, p, BODY] = part(SF_HADJ, p)
        suffix = jnp.where(rows80 < HALO + ROWS // 2, sums[p][1], sums[p][0])
        st[1, p, BODY] = part(SF_SU, p) + suffix
        st[2, p, BODY] = part(SF_SV, p)

    mid, down, up, rows = slice(16, 80), slice(15, 79), slice(17, 81), slice(8, 72)

    def back_step(i, _):
        n = SUBCYCLES - 1 - i
        u = [ou2[0, p, rows] * st[1, p, mid] for p in BOTH]
        v = [ou2[1, p, rows] * st[2, p, mid] for p in BOTH]
        for p in BOTH:
            fg[0, p, rows] = fg[0, p, rows] + u[p]
            fg[1, p, rows] = fg[1, p, rows] + v[p]
            tmpb[p, mid] = gb[n, 1, p, rows] * v[p]
        b_u = [gb[n, 0, p, rows] * u[p] for p in BOTH]
        rest = [
            st[0, p, mid] + ga[n, 0, p, rows] * u[p] + (ga[n, 1, p, rows] * v[p] - tmpb[p, down]) for p in BOTH
        ]
        b_w, rest_e = pair_west(*b_u), pair_east(*rest)
        h = [wt2[p, rows] * (rest[p] - b_w[p]) for p in BOTH]
        h_e = [wte[p, rows] * (rest_e[p] - b_u[p]) for p in BOTH]
        for p in BOTH:
            st[0, p, mid] = h[p]
        for p in BOTH:
            st[1, p, mid] = (1.0 - FRICTION) * u[p] - DIVERGENCE * (h[p] - h_e[p])
            st[2, p, mid] = (1.0 - FRICTION) * v[p] - DIVERGENCE * (h[p] - st[0, p, up])
        return 0

    lax.fori_loop(0, SUBCYCLES, back_step, 0, unroll=8)

    out_h[...] = st[0, 0, MINE]
    window = slice(8, 72)
    force = 1.0 / (LEVELS * SUBCYCLES)
    fu, fv = fg[0, 0], fg[1, 0]
    fu_w = pair_west(fu, fg[0, 1])[0]
    fv_e = pair_east(fv, fg[1, 1])[0]
    gg[0] = force * fu[window] - over(acx[0], acx[1])
    gg[1] = force * fu_w[window] - over(acx[4], acx[5])
    gg[2] = force * fv[window] - over(acx[2], acx[3])
    gg[3] = force * fv_e[window] - over(acx[6], acx[7])
    acc[0] = (st[1, 0, MINE] - fu[16:64] / SUBCYCLES) / LEVELS
    acc[1] = (st[2, 0, MINE] - fv[16:64] / SUBCYCLES) / LEVELS

    turn = (0.25 * CORIOLIS) * cor

    def momentum_level(i, press):
        k = LEVELS - 1 - i
        z = z1[k, ZR] + we[k, ZR] * gg[0, 8:64]
        z_w = z1w[k, ZR] + wew[k, ZR] * gg[1, 8:64]
        m = mm1[k, MR] + wn[k, MR] * gg[2, 0:56]
        m_e = mm1e[k, MR] + wne[k, MR] * gg[3, 0:56]
        sut[ZR] = turn[8:64] * (z + z_w)
        svt[MR] = turn[0:56] * (m + m_e)
        tmp3[MR] = m
        z0, m0 = z[0:48], m[8:56]
        press = press + (PRESS_COEF / LEVELS) * ((z0 - z_w[0:48]) + (m0 - tmp3[15:63]))
        drag = jnp.where(bl[...] - 1 == k, 1.0 - DRAG_COEF, 1.0)
        wet = x[WET, k, OWN]
        out_t[k] = wet * (out_t[k] - HEAT_COEF * press)
        out_s[k] = wet * (out_s[k] + SALT_COEF * press)
        out_u[k] = we[k, OWN] * (out_u[k] + z0 * drag - (svt[OWN] + svt[15:63]) + acc[0])
        out_v[k] = wn[k, OWN] * (out_v[k] + m0 * drag + (sut[OWN] + sut[17:65]) + acc[1])
        return press

    lax.fori_loop(0, LEVELS, momentum_level, jnp.zeros((ROWS, LANES), F32))


def store_kernel(*refs):
    sources, targets, sem = refs[:5], refs[5:10], refs[10]
    copies = [pltpu.make_async_copy(a, b, sem.at[n]) for n, (a, b) in enumerate(zip(sources, targets))]
    for copy in copies:
        copy.start()
    for copy in copies:
        copy.wait()


def solution(mesh):
    nlon, nlat = mesh.shape["lon"], mesh.shape["lat"]
    inner = next(n for n in (8, 4, 2, 1) if nlat % n == 0 and n * n <= 2 * nlat)
    outer = nlat // inner
    deep = P(None, "lat", "lon")
    flat = P("lat", "lon")

    def step(*args):
        vm = lambda *shape: pltpu.VMEM(shape, F32)
        cube = jax.ShapeDtypeStruct((LEVELS, ROWS, LANES), F32)
        plane = jax.ShapeDtypeStruct((ROWS, LANES), F32)
        level = vm(LEVELS, TALL, LANES)
        copies = 7 + 10 + inner - 1 + 8 + 2 + 3 * (outer - 1)
        scratch = dict(
            x=vm(9, LEVELS, TALL, LANES), lm=pltpu.VMEM((LEVELS, ROWS, LANES), jnp.int32),
            bl=pltpu.VMEM((ROWS, LANES), jnp.int32), stv=vm(ROWS, LANES),
            c1=vm(3, ROWS, LANES), ce1=vm(ROWS, LANES), cw1=vm(ROWS, LANES), pw1=vm(80, LANES), pe1=vm(80, LANES),
            cl=vm(2, ROWS, LANES), pwl=vm(2, 80, LANES), pel=vm(2, 80, LANES), m1=vm(3, 80, LANES), mr=vm(80, LANES),
            rn=vm(9, 16, LANES), rs=vm(9, 16, LANES), got_s=vm(9, 16, LANES), got_n=vm(9, 16, LANES),
            tot=vm(8, LANES), inn=vm(2, 8, LANES), slot1=vm(max(inner - 1, 1), 8, LANES), gsum=vm(8, LANES),
            slot2=vm(max(3 * (outer - 1), 1), 8, LANES), inn_w=vm(2, 8, LANES), inn_e=vm(2, 8, LANES), sfx=vm(96, LANES),
            um0=level, umw=level, vm0=level, we=level, wew=level, wn=level, z1=level, z1w=level,
            mm1=level, mm1e=level, wne=level, tmp3=vm(TALL, LANES), sut=vm(TALL, LANES), svt=vm(TALL, LANES),
            acc=vm(8, ROWS, LANES), acx=vm(8, 64, LANES), ce2=vm(ROWS, LANES), cw2=vm(ROWS, LANES), pw2=vm(80, LANES),
            pe2=vm(80, LANES), m2=vm(2, 80, LANES), sa=vm(11, WIDE, LANES), sb=vm(11, 80, LANES),
            st=vm(3, 2, WIDE, LANES), ou2=vm(2, 2, 80, LANES), cd2=vm(2, 2, 80, LANES), wt2=vm(2, 80, LANES), wte=vm(2, 80, LANES),
            ff2=vm(2, 2, 80, LANES), ga=vm(SUBCYCLES, 2, 2, 80, LANES), gb=vm(SUBCYCLES, 2, 2, 80, LANES),
            fg=vm(2, 2, 80, LANES), tmpb=vm(2, WIDE, LANES), gg=vm(4, 64, LANES),
            in_sem=pltpu.SemaphoreType.DMA((13,)), send_sem=pltpu.SemaphoreType.DMA((copies,)),
            recv_sem=pltpu.SemaphoreType.DMA((copies,)),
            ready=pltpu.SemaphoreType.REGULAR((2,)),
        )

        def body(*refs):
            kernel(nlon, nlat, inner, *refs)

        parts = pl.pallas_call(
            body,
            out_shape=[cube, cube, cube, cube, plane],
            in_specs=[pl.BlockSpec(memory_space=pltpu.HBM)] * 13,
            out_specs=[pl.BlockSpec(memory_space=pltpu.VMEM)] * 5,
            scratch_shapes=list(scratch.values()),
            compiler_params=pltpu.CompilerParams(
                collective_id=0, has_side_effects=True, vmem_limit_bytes=40 * 1024 * 1024
            ),
        )(*(pltpu.with_memory_space_constraint(a, pltpu.HBM) for a in args))
        return pl.pallas_call(
            store_kernel,
            out_shape=[cube, cube, cube, cube, plane],
            in_specs=[pl.BlockSpec(memory_space=pltpu.VMEM)] * 5,
            out_specs=[pl.BlockSpec(memory_space=pltpu.HBM)] * 5,
            scratch_shapes=[pltpu.SemaphoreType.DMA((5,))],
            compiler_params=pltpu.CompilerParams(vmem_limit_bytes=4 * 1024 * 1024),
        )(*parts)

    specs = (deep, deep, deep, deep, flat, deep, flat, deep, deep, deep, deep, flat, flat)
    return jax.shard_map(
        step, mesh=mesh, in_specs=specs, out_specs=(deep, deep, deep, deep, flat), check_vma=False
    )
```

```python
import jax
import jax.numpy as jnp
from jax import lax
from jax.experimental import pallas as pl
from jax.experimental.pallas import tpu as pltpu
from jax.sharding import PartitionSpec as P

MESH = pl.DeviceIdType.MESH
F32 = jnp.float32
SUBCYCLES = 8
LEVELS = 8
ROWS = 48
LANES = 128
HALO = 16

ADVECT = 0.25
DIFFUSION = 0.1
HEAT_COEF = 0.5
SALT_COEF = 0.4
PRESS_COEF = 0.3
CORIOLIS = 0.3
DRAG_COEF = 0.5
DIVERGENCE = 0.5
SLOPE_COEF = 0.5
FRICTION = 0.05
THICK_COEF = 0.3

CT, CS, WU, WV, WET, AT, AS, WZ, WM = range(9)
PACK = ((0, 0), (0, 1), (0, 2), (0, 3), (1, 0), (2, 0), (2, 1), (2, 2), (2, 3))
OWN = slice(16, 64)
ZR = slice(16, 72)
MR = slice(8, 64)
TALL = 80
BODY = slice(8, 88)
MINE = slice(24, 72)
WIDE = 96
SF_H, SF_HADJ, SF_WT, SF_U, SF_V, SF_FU, SF_FV, SF_CU, SF_CV, SF_SU, SF_SV = range(11)
SIDES = ((1, 0), (-1, 0), (0, 1), (0, -1), (1, 1), (-1, 1), (1, -1), (-1, -1))


def roll(x, shift):
    return pltpu.roll(x, shift, axis=x.ndim - 1)


def lanes_of(rows):
    return lax.broadcasted_iota(jnp.int32, (rows, LANES), 1)


def pair_east(a, b):
    last = lanes_of(a.shape[0]) == LANES - 1
    ra, rb = roll(a, LANES - 1), roll(b, LANES - 1)
    return jnp.where(last, rb, ra), jnp.where(last, ra, rb)


def pair_west(a, b):
    first = lanes_of(a.shape[0]) == 0
    ra, rb = roll(a, 1), roll(b, 1)
    return jnp.where(first, rb, ra), jnp.where(first, ra, rb)


def kernel(
    nlon, nlat, inner,
    tracer, salinity, zonal, merid, surface, mask, bottom, tr_adj, sa_adj, zo_adj, me_adj, su_adj, st_adj,
    out_t, out_s, out_u, out_v, out_h,
    x, lm, bl, stv, c1, ce1, cw1, pw1, pe1, cl, pwl, pel, m1, mr, rn, rs, got_s, got_n,
    tot, inn, slot1, gsum, slot2, inn_w, inn_e, sfx,
    um0, umw, vm0, we, wew, wn, z1, z1w, mm1, mm1e, wne, tmp3, sut, svt,
    acc, acx, ce2, cw2, pw2, pe2, m2, sa, sb, st, ou2, cd2, wt2, wte, ff2, ga, gb, fg, tmpb, gg,
    in_sem, send_sem, recv_sem, ready,
):
    lon, lat = lax.axis_index("lon"), lax.axis_index("lat")
    south_here, north_here = lat > 0, lat < nlat - 1
    outer = nlat // inner
    gi, go = lax.rem(lat, inner), lat // inner

    def at(dlon, dlat):
        return (lax.rem(lon + dlon + nlon, nlon), lax.rem(lat + dlat + nlat, nlat))

    def when(condition, action):
        if condition is None:
            action()
        else:
            pl.when(condition)(action)

    around = [at(*side) for side in SIDES]
    exists = [{0: None, 1: north_here, -1: south_here}[side[1]] for side in SIDES]
    from_it = [{0: None, 1: south_here, -1: north_here}[side[1]] for side in SIDES]

    def signal(sem, where, condition):
        when(condition, lambda: pl.semaphore_signal(sem, inc=1, device_id=where, device_id_type=MESH))

    barrier = pltpu.get_barrier_semaphore()
    for where, condition in zip(around, exists):
        signal(barrier, where, condition)
    chip, even = gi // 2, lax.rem(go, 2) == 0
    mates = []
    for d in range(1, inner):
        there = lax.rem(gi + d, inner)
        greets = jnp.logical_not(even) | (there // 2 >= chip)
        greeted = jnp.logical_not(even) | (there // 2 <= chip)
        mates.append(((lon, go * inner + there), greets, greeted))
    peers = []
    for e in range(1, outer):
        there = lax.rem(go + e, outer)
        down = go > there
        facing = jnp.where(lax.rem(there + go, 2) == 0, gi, inner - 1 - gi)
        hasty = jnp.where(down, go, there) % 2 < jnp.where(down, there, go) % 2
        for c in (1, -1, 0):
            where = (lax.rem(lon + c + nlon, nlon), there * inner + facing)
            peers.append((where, down == hasty, down != hasty, down, hasty))
    greeted_by = 2 + jnp.where(south_here, 3, 0) + jnp.where(north_here, 3, 0)
    answers = [0, 0]
    for where, greets, greeted in mates:
        signal(barrier, where, greets)
        greeted_by = greeted_by + jnp.where(greeted, 1, 0)
        answers[0] = answers[0] + jnp.where(greeted, 0, 1)
    for where, greets, greeted, down, hasty in peers:
        signal(barrier, where, greets)
        greeted_by = greeted_by + jnp.where(greeted, 1, 0)
        answers[1] = answers[1] + jnp.where(down & hasty, 1, 0)

    def answer():
        for where, greets, _ in mates:
            signal(ready.at[0], where, jnp.logical_not(greets))
        for where, _, _, down, hasty in peers:
            signal(ready.at[1], where, hasty & jnp.logical_not(down))

    def wait_answers(n):
        when(answers[n] > 0, lambda: pl.semaphore_wait(ready.at[n], answers[n]))

    loads = []
    for src, dst in (
        (st_adj, stv), (mask, lm), (bottom, bl),
        (tracer, x.at[CT, :, OWN]), (salinity, x.at[CS, :, OWN]), (zonal, x.at[WU, :, OWN]), (merid, x.at[WV, :, OWN]),
        (surface, sa.at[SF_H, MINE]), (su_adj, sa.at[SF_HADJ, MINE]),
        (tr_adj, x.at[AT, :, OWN]), (sa_adj, x.at[AS, :, OWN]), (zo_adj, x.at[WZ, :, OWN]), (me_adj, x.at[WM, :, OWN]),
    ):
        copy = pltpu.make_async_copy(src, dst, in_sem.at[len(loads)])
        copy.start()
        loads.append(copy)

    sent = []

    def send(src, dst, where, to=None, by=None, now=None):
        n = len(sent)
        copy = pltpu.make_async_remote_copy(
            src_ref=src, dst_ref=dst, send_sem=send_sem.at[n], recv_sem=recv_sem.at[n],
            device_id=where, device_id_type=MESH,
        )
        if now is not False:
            when(to if now is None else now, copy.start)
        sent.append((copy, to))
        return copy, by

    def arrive(copies):
        for copy, by in copies:
            when(by, copy.wait_recv)

    pad = jnp.zeros((8, LANES), F32)
    loads[0].wait()
    tile_sum = stv[0:8]
    for r in range(1, ROWS // 8):
        tile_sum = tile_sum + stv[8 * r : 8 * r + 8]
    tot[...] = tile_sum
    for copy in loads[1:9]:
        copy.wait()

    lane = lanes_of(ROWS)
    EARLY, LATE = (CT, CS, WU, WV, WET), (AT, AS, WZ, WM)

    def mask_fields(fields):
        def mask_level(k, _):
            if WET in fields:
                wet = jnp.where((lm[k] > 0) & (k < bl[...]), 1.0, 0.0).astype(F32)
            else:
                wet = x[WET, k, OWN]
            packs = {PACK[f][0]: c1[PACK[f][0]] for f in fields}
            for f in fields:
                n, s = PACK[f]
                value = wet if f == WET else x[f, k, OWN] * wet
                x[f, k, OWN] = value
                here = lax.shift_right_logical(lane, 2) == 8 * s + k
                packs[n] = jnp.where(here, roll(value, 32 * s + 4 * k + 2), packs[n])
            for n, value in packs.items():
                c1[n] = value
            return 0

        lax.fori_loop(0, LEVELS, mask_level, 0, unroll=4)

        def pack_rows(f, _):
            for k in range(LEVELS):
                rs[f, 2 * k : 2 * k + 2] = x[f, k, 16:18]
                rn[f, 2 * k : 2 * k + 2] = x[f, k, 62:64]
            return 0

        lax.fori_loop(fields[0], fields[-1] + 1, pack_rows, 0)

    c1[1] = jnp.zeros((ROWS, LANES), F32)
    mask_fields(EARLY)
    fine, coarse = (lane & 3) < 2, (lane & 31) < 16
    ce1[...] = jnp.where(fine, c1[0], roll(c1[1], 2))
    cw1[...] = jnp.where(fine, roll(c1[1], LANES - 2), c1[0])
    pl.semaphore_wait(barrier, greeted_by)

    def send_all(table):
        return [send(src, dst, around[n], exists[n], from_it[n]) for n, src, dst in table]

    def rows_table(first, last):
        here = slice(first, last)
        return [(2, rn.at[here], got_s.at[here]), (3, rs.at[here], got_n.at[here])]

    def planes_table(first, last):
        here = slice(first, last)
        return [(2, sa.at[here, 56:72], sa.at[here, 8:24]), (3, sa.at[here, 24:40], sa.at[here, 72:88])]

    LOW, HIGH = slice(0, 16), slice(32, 48)
    phase1 = send_all(
        [
            (5, cw1.at[40:48], pe1.at[8:16]),
            (6, ce1.at[0:8], pw1.at[64:72]),
            (7, cw1.at[0:8], pe1.at[64:72]),
            (0, ce1, pw1.at[16:64]),
            (1, cw1, pe1.at[16:64]),
        ]
        + rows_table(0, 5)
    )
    up1 = [send(tot, slot1.at[n], mate[0], now=False) for n, mate in enumerate(mates)]

    def member_sums():
        wait_answers(0)
        for copy, _ in up1:
            copy.start()

    pl.when(jnp.logical_not(even))(member_sums)
    answer()

    for copy in loads[9:]:
        copy.wait()
    mask_fields(LATE)
    sa[SF_WT, MINE] = x[WET, 0, OWN]
    pack = roll(sa[SF_H, MINE], 16)
    for s, f in ((1, SF_HADJ), (2, SF_WT)):
        here = lax.shift_right_logical(lane, 5) == s
        pack = jnp.where(here, roll(sa[f, MINE], 32 * s + 16), pack)
    cl[0] = c1[2]
    cl[1] = pack
    late1 = send_all(
        rows_table(5, 9)
        + [
            (0, cl, pwl.at[:, 16:64]),
            (1, cl, pel.at[:, 16:64]),
            (4, cl.at[:, HIGH], pwl.at[:, 0:16]),
            (5, cl.at[:, HIGH], pel.at[:, 0:16]),
            (6, cl.at[:, LOW], pwl.at[:, 64:80]),
            (7, cl.at[:, LOW], pel.at[:, 64:80]),
        ]
        + planes_table(0, 3)
    )

    pl.when(even)(member_sums)

    sfx[0:48] = stv[...]
    for r in range(6):
        sfx[48 + 8 * r : 56 + 8 * r] = pad
    for step in (1, 2, 4, 8, 16, 32):
        moved = sfx[0:48] + sfx[step : step + 48]
        sfx[0:48] = moved
    for n in range(3):
        for p in range(2):
            st[n, p, 0:8] = pad
            st[n, p, 88:96] = pad
    for p in range(2):
        tmpb[p, 8:16] = pad
    acc[...] = jnp.zeros_like(acc)
    acx[...] = jnp.zeros_like(acx)

    up2 = [send(inn, inn_w, around[0], now=False), send(inn, inn_e, around[1], now=False)]
    for n, (where, _, _, down, hasty) in enumerate(peers):
        come = lax.rem(go - n // 3 - 1 + outer, outer) > go
        up2.append(send(gsum, slot2.at[n], where, down, come, False))

    def group_sums():
        arrive(up1)
        group = tot[...]
        above = jnp.zeros((8, LANES), F32)
        for d in range(1, inner):
            got = slot1[d - 1]
            group = group + got
            above = above + jnp.where(lax.rem(gi - d + inner, inner) > gi, got, 0.0)
        gsum[...] = group
        inn[0] = above
        inn[1] = tot[...]
        for copy, _ in up2[:2]:
            copy.start()
        for (copy, _), (_, _, _, down, hasty) in zip(up2[2:], peers):
            when(down & jnp.logical_not(hasty), copy.start)

    pl.when(jnp.logical_not(even))(group_sums)
    arrive(phase1)
    def unpack_rows(f, _):
        for k in range(LEVELS):
            x[f, k, 14:16] = jnp.where(south_here, got_s[f, 2 * k : 2 * k + 2], 0.0)
            x[f, k, 64:66] = jnp.where(north_here, got_n[f, 2 * k : 2 * k + 2], 0.0)
        return 0

    lax.fori_loop(0, 5, unpack_rows, 0)
    lane80 = lanes_of(80)
    rows80 = lax.broadcasted_iota(jnp.int32, (80, LANES), 0)
    inside = ((rows80 >= 16) | south_here) & ((rows80 < 64) | north_here)
    fine = (lane80 & 3) < 2
    coarse = (lane80 & 31) < 16

    rim_w, rim_e = pw1[...], pe1[...]
    m1[0] = jnp.where(inside, jnp.where(fine, rim_w, rim_e), 0.0)
    m1[1] = jnp.where(inside, jnp.where(fine, roll(rim_w, LANES - 2), roll(rim_e, 2)), 0.0)

    def strip(f, k, rows):
        n, s = PACK[f]
        return roll(m1[n, rows], 126 - 32 * s - 4 * k)

    def shifted(value, rim, offset):
        ids = lanes_of(value.shape[0])
        if offset > 0:
            return roll(jnp.where(ids < offset, rim, value), LANES - offset)
        return roll(jnp.where(ids >= LANES + offset, rim, value), -offset)

    row_ids = lax.broadcasted_iota(jnp.int32, (64, LANES), 0) + (lat * ROWS - 8)
    cor = -(1.0 + row_ids.astype(F32) / (ROWS * nlat))

    m2[0] = SALT_COEF * roll(m1[0], LANES - 32) - HEAT_COEF * m1[0]

    EXT = slice(8, 72)

    def forward_level(k, _):
        wet = x[WET, k, EXT]
        wet_e = shifted(wet, strip(WET, k, EXT), 1)
        tmp3[EXT] = wet_e
        wet_n = x[WET, k, 9:73]
        east, north = wet * wet_e, wet * wet_n
        we[k, EXT] = east
        wn[k, EXT] = north
        wu, wv = x[WU, k, EXT], x[WV, k, EXT]
        u0 = wu * wet_e
        v0 = wv * wet_n
        uw = shifted(wu[8:64], strip(WU, k, ZR), -1) * wet[8:64]
        ve = shifted(wv[0:56], strip(WV, k, MR), 1) * tmp3[9:65]
        um0[k, EXT] = u0
        umw[k, ZR] = uw
        vm0[k, EXT] = v0
        sut[ZR] = u0[8:64] + uw
        svt[MR] = v0[0:56] + ve
        acc[6] = acc[6] + x[WZ, k, OWN] * wet_e[8:56]
        acc[7] = acc[7] + x[WM, k, OWN] * wet_n[8:56]
        acx[1] = acx[1] + east
        acx[3] = acx[3] + north

        t0 = SALT_COEF * x[CS, k, OWN] - HEAT_COEF * x[CT, k, OWN]
        tn = SALT_COEF * x[CS, k, 17:65] - HEAT_COEF * x[CT, k, 17:65]
        te = shifted(t0, roll(m2[0, OWN], 126 - 4 * k), 1)
        dpe = acc[4] + (te - t0)
        dpn = acc[5] + (tn - t0)
        acc[4] = dpe
        acc[5] = dpn
        own = slice(8, 56)
        drag = jnp.where(bl[...] - 1 == k, 1.0 - DRAG_COEF, 1.0)
        uo, vo = u0[own], v0[own]
        vu = (0.25 * CORIOLIS) * cor[own] * (svt[OWN] + svt[15:63])
        uv = (0.25 * CORIOLIS) * cor[own] * (sut[OWN] + sut[17:65])
        zn = uo * drag + east[own] * (vu - (PRESS_COEF / LEVELS) * dpe)
        mn = vo * drag - north[own] * (uv + (PRESS_COEF / LEVELS) * dpn)
        acc[0] = acc[0] + uo
        acc[1] = acc[1] + vo
        acc[2] = acc[2] + zn
        acc[3] = acc[3] + mn
        return 0

    tmp3[72:80] = pad
    lax.fori_loop(0, LEVELS, forward_level, 0, unroll=2)

    def over(num, count):
        return num / jnp.maximum(count, 1.0)

    own = slice(8, 56)
    cu, cv = acx[1, own], acx[3, own]
    near = sfx[0:48] - jnp.where(row_ids[0:48] - (lat * ROWS - 8) < ROWS // 2, sfx[0:1], 0.0)
    surf = [
        acc[0] / LEVELS, acc[1] / LEVELS,
        (acc[2] - acc[0]) / (LEVELS * SUBCYCLES), (acc[3] - acc[1]) / (LEVELS * SUBCYCLES),
        cu, cv,
        LEVELS * over(acc[6], cu) + near,
        LEVELS * over(acc[7], cv),
    ]
    packs = []
    for n in range(2):
        pack = None
        for s in range(4):
            value = surf[4 * n + s]
            sa[SF_U + 4 * n + s, MINE] = value
            turned = roll(value, (32 * s + 16) % LANES)
            pack = turned if s == 0 else jnp.where(lax.shift_right_logical(lane, 5) == s, turned, pack)
        packs.append(pack)
    own_coarse = (lane & 31) < 16
    ce2[...] = jnp.where(own_coarse, packs[0], roll(packs[1], 16))
    cw2[...] = jnp.where(own_coarse, roll(packs[1], LANES - 16), packs[0])
    phase2 = send_all(
        [
            (4, ce2.at[HIGH], pw2.at[0:16]),
            (5, cw2.at[HIGH], pe2.at[0:16]),
            (6, ce2.at[LOW], pw2.at[64:80]),
            (7, cw2.at[LOW], pe2.at[64:80]),
            (0, ce2, pw2.at[16:64]),
            (1, cw2, pe2.at[16:64]),
        ]
        + planes_table(3, 11)
    )
    pl.when(even)(group_sums)
    wait_answers(1)
    for copy, (_, _, _, down, hasty) in zip(up2[2:], peers):
        when(down & hasty, copy[0].start)
    arrive(late1)
    lax.fori_loop(5, 9, unpack_rows, 0)
    m1[2] = jnp.where(inside, jnp.where(fine, pwl[0], pel[0]), 0.0)
    mr[...] = jnp.where(inside, jnp.where(coarse, pwl[1], pel[1]), 0.0)

    def advect_level(k, _):
        wet_rim = strip(WET, k, OWN)
        wet = x[WET, k, OWN]
        u_rim, wu = strip(WU, k, OWN), x[WU, k, OWN]
        u0, u_w = um0[k, OWN], umw[k, OWN]
        u_ww = shifted(wu, u_rim, -2) * shifted(wet, wet_rim, -1)
        u_e = shifted(wu, u_rim, 1) * shifted(wet, wet_rim, 2)
        we0, we_w = we[k, OWN], wet * shifted(wet, wet_rim, -1)
        v0, v_s, v_ss, v_n = vm0[k, OWN], vm0[k, 15:63], vm0[k, 14:62], vm0[k, 17:65]
        wn0, wn_s = wn[k, OWN], wn[k, 15:63]
        grad_u = jnp.zeros((ROWS, LANES), F32)
        grad_v = jnp.zeros((ROWS, LANES), F32)
        for c, a, out in ((CT, AT, out_t), (CS, AS, out_s)):
            a0, a_rim = x[a, k, OWN], strip(a, k, OWN)
            c0, c_rim = x[c, k, OWN], strip(c, k, OWN)
            a_e, a_ee = shifted(a0, a_rim, 1), shifted(a0, a_rim, 2)
            a_w, a_ww = shifted(a0, a_rim, -1), shifted(a0, a_rim, -2)
            d0, d_w, d_ww, d_e = a_e - a0, a0 - a_w, a_w - a_ww, a_ee - a_e
            c_e, c_ee, c_w = shifted(c0, c_rim, 1), shifted(c0, c_rim, 2), shifted(c0, c_rim, -1)
            grad_u = grad_u + d0 * ((ADVECT * 7.0 / 12.0) * (c0 + c_e) - (ADVECT / 12.0) * (c_w + c_ee))
            grad = a0 + (ADVECT * 7.0 / 12.0) * (u0 * d0 + u_w * d_w) - (ADVECT / 12.0) * (u_e * d_e + u_ww * d_ww)
            grad = grad + DIFFUSION * (we0 * d0 - we_w * d_w)
            a_n, a_nn, a_s, a_ss = x[a, k, 17:65], x[a, k, 18:66], x[a, k, 15:63], x[a, k, 14:62]
            d0, d_s, d_ss, d_n = a_n - a0, a0 - a_s, a_s - a_ss, a_nn - a_n
            c_n, c_nn, c_s = x[c, k, 17:65], x[c, k, 18:66], x[c, k, 15:63]
            grad_v = grad_v + d0 * ((ADVECT * 7.0 / 12.0) * (c0 + c_n) - (ADVECT / 12.0) * (c_s + c_nn))
            grad = grad + (ADVECT * 7.0 / 12.0) * (v0 * d0 + v_s * d_s) - (ADVECT / 12.0) * (v_n * d_n + v_ss * d_ss)
            grad = grad + DIFFUSION * (wn0 * d0 - wn_s * d_s)
            out[k] = grad
        out_u[k] = grad_u
        out_v[k] = grad_v
        wet_x = x[WET, k, EXT]
        rim_x = strip(WET, k, EXT)
        wet_ex = shifted(wet_x, rim_x, 1)
        tmp3[EXT] = wet_ex
        wet_en = tmp3[9:73]
        east_w = wet_x * shifted(wet_x, rim_x, -1)
        north_e = wet_ex * wet_en
        z_w = shifted(x[WZ, k, EXT], strip(WZ, k, EXT), -1) * wet_x
        m_e = shifted(x[WM, k, EXT], strip(WM, k, EXT), 1) * wet_en
        wew[k, EXT] = east_w
        wne[k, EXT] = north_e
        z1w[k, EXT] = z_w
        mm1e[k, EXT] = m_e
        zz = x[WZ, k, EXT] * wet_ex
        mz = x[WM, k, EXT] * x[WET, k, 9:73]
        z1[k, EXT] = zz
        mm1[k, EXT] = mz
        acx[0] = acx[0] + zz
        acx[2] = acx[2] + mz
        acx[4] = acx[4] + z_w
        acx[5] = acx[5] + east_w
        acx[6] = acx[6] + m_e
        acx[7] = acx[7] + north_e
        return 0

    lax.fori_loop(0, LEVELS, advect_level, 0)

    for copy, to in sent:
        when(to, copy.wait_send)
    arrive(phase2)

    rim_lane = (lane80 < HALO) | (lane80 >= LANES - HALO)
    rim_w, rim_e = pw2[...], pe2[...]
    m2[0] = jnp.where(inside, jnp.where(coarse, rim_w, rim_e), 0.0)
    m2[1] = jnp.where(inside, jnp.where(coarse, roll(rim_w, LANES - 16), roll(rim_e, 16)), 0.0)
    for f in range(11):
        source, s = (mr[...], f) if f < 3 else (m2[(f - 3) // 4], (f - 3) % 4)
        sb[f] = jnp.where(rim_lane, roll(source, (LANES - 16 - 32 * s) % LANES), 0.0)

    def part(f, p):
        return jnp.where(inside, sa[f, BODY], 0.0) if p == 0 else sb[f]

    for p in range(2):
        st[0, p, BODY] = part(SF_H, p)
        st[1, p, BODY] = part(SF_U, p)
        st[2, p, BODY] = part(SF_V, p)
        wt2[p] = part(SF_WT, p)
        for d in range(2):
            count = part(SF_CU + d, p)
            opened = jnp.minimum(count, 1.0)
            ou2[d, p] = opened
            cd2[d, p] = (SLOPE_COEF / LEVELS) * count
            ff2[d, p] = opened * part(SF_FU + d, p)
            fg[d, p] = jnp.zeros((80, LANES), F32)

    BOTH = (0, 1)
    wte[0], wte[1] = pair_east(wt2[0], wt2[1])

    def sub_step(n, lo, hi):
        mid, down, up = slice(lo + 8, hi + 8), slice(lo + 7, hi + 7), slice(lo + 9, hi + 9)
        rows = slice(lo, hi)
        u = [st[1, p, mid] for p in BOTH]
        v = [st[2, p, mid] for p in BOTH]
        rest = [st[0, p, mid] - DIVERGENCE * (v[p] - st[2, p, down]) - DIVERGENCE * u[p] for p in BOTH]
        u_w, rest_e = pair_west(*u), pair_east(*rest)
        h = [wt2[p, rows] * (rest[p] + DIVERGENCE * u_w[p]) for p in BOTH]
        h_e = [wte[p, rows] * (rest_e[p] + DIVERGENCE * u[p]) for p in BOTH]
        for p in BOTH:
            st[0, p, mid] = h[p]
        for p in BOTH:
            for d, old, far in ((0, u[p], h_e[p]), (1, v[p], st[0, p, up])):
                slope = far - h[p]
                bend = jnp.tanh(0.5 * (h[p] + far))
                depth = cd2[d, p, rows]
                level = depth * (1.0 + THICK_COEF * bend)
                tilt = depth * (0.5 * THICK_COEF) * (1.0 - bend * bend) * slope
                ga[n, d, p, rows] = level - tilt
                gb[n, d, p, rows] = level + tilt
                st[1 + d, p, mid] = (1.0 - FRICTION) * ou2[d, p, rows] * old + ff2[d, p, rows] - level * slope
        return 0

    lax.fori_loop(0, 3, lambda n, _: sub_step(n, 0, 80), 0, unroll=3)
    lax.fori_loop(3, SUBCYCLES, lambda n, _: sub_step(n, 4, 76), 0, unroll=5)

    arrive(up2)
    sums = []
    for c, source in enumerate((inn_w, inn_e, inn)):
        beyond = source[0]
        for e in range(1, outer):
            beyond = beyond + jnp.where(lax.rem(go - e + outer, outer) > go, slot2[3 * (e - 1) + c], 0.0)
        beyond = jnp.sum(beyond, axis=0, keepdims=True)
        sums.append((beyond, beyond + jnp.sum(source[1], axis=0, keepdims=True)))
    east_half = lanes_of(1) < LANES // 2
    sums = (sums[2], tuple(jnp.where(east_half, e, w) for w, e in zip(sums[0], sums[1])))
    for p in BOTH:
        st[0, p, BODY] = part(SF_HADJ, p)
        suffix = jnp.where(rows80 < HALO + ROWS // 2, sums[p][1], sums[p][0])
        st[1, p, BODY] = part(SF_SU, p) + suffix
        st[2, p, BODY] = part(SF_SV, p)

    def back_step(i, lo, hi):
        mid, down, up, rows = slice(lo + 8, hi + 8), slice(lo + 7, hi + 7), slice(lo + 9, hi + 9), slice(lo, hi)
        n = SUBCYCLES - 1 - i
        u = [ou2[0, p, rows] * st[1, p, mid] for p in BOTH]
        v = [ou2[1, p, rows] * st[2, p, mid] for p in BOTH]
        for p in BOTH:
            fg[0, p, rows] = fg[0, p, rows] + u[p]
            fg[1, p, rows] = fg[1, p, rows] + v[p]
            tmpb[p, mid] = gb[n, 1, p, rows] * v[p]
        b_u = [gb[n, 0, p, rows] * u[p] for p in BOTH]
        rest = [
            st[0, p, mid] + ga[n, 0, p, rows] * u[p] + (ga[n, 1, p, rows] * v[p] - tmpb[p, down]) for p in BOTH
        ]
        b_w, rest_e = pair_west(*b_u), pair_east(*rest)
        h = [wt2[p, rows] * (rest[p] - b_w[p]) for p in BOTH]
        h_e = [wte[p, rows] * (rest_e[p] - b_u[p]) for p in BOTH]
        for p in BOTH:
            st[0, p, mid] = h[p]
        for p in BOTH:
            st[1, p, mid] = (1.0 - FRICTION) * u[p] - DIVERGENCE * (h[p] - h_e[p])
            st[2, p, mid] = (1.0 - FRICTION) * v[p] - DIVERGENCE * (h[p] - st[0, p, up])
        return 0

    lax.fori_loop(0, 4, lambda i, _: back_step(i, 8, 72), 0, unroll=4)
    lax.fori_loop(4, SUBCYCLES, lambda i, _: back_step(i, 12, 68), 0, unroll=4)

    out_h[...] = st[0, 0, MINE]
    window = slice(8, 72)
    force = 1.0 / (LEVELS * SUBCYCLES)
    fu, fv = fg[0, 0], fg[1, 0]
    fu_w = pair_west(fu, fg[0, 1])[0]
    fv_e = pair_east(fv, fg[1, 1])[0]
    gg[0] = force * fu[window] - over(acx[0], acx[1])
    gg[1] = force * fu_w[window] - over(acx[4], acx[5])
    gg[2] = force * fv[window] - over(acx[2], acx[3])
    gg[3] = force * fv_e[window] - over(acx[6], acx[7])
    acc[0] = (st[1, 0, MINE] - fu[16:64] / SUBCYCLES) / LEVELS
    acc[1] = (st[2, 0, MINE] - fv[16:64] / SUBCYCLES) / LEVELS

    turn = (0.25 * CORIOLIS) * cor

    def momentum_level(i, press):
        k = LEVELS - 1 - i
        z = z1[k, ZR] + we[k, ZR] * gg[0, 8:64]
        z_w = z1w[k, ZR] + wew[k, ZR] * gg[1, 8:64]
        m = mm1[k, MR] + wn[k, MR] * gg[2, 0:56]
        m_e = mm1e[k, MR] + wne[k, MR] * gg[3, 0:56]
        sut[ZR] = turn[8:64] * (z + z_w)
        svt[MR] = turn[0:56] * (m + m_e)
        tmp3[MR] = m
        z0, m0 = z[0:48], m[8:56]
        press = press + (PRESS_COEF / LEVELS) * ((z0 - z_w[0:48]) + (m0 - tmp3[15:63]))
        drag = jnp.where(bl[...] - 1 == k, 1.0 - DRAG_COEF, 1.0)
        wet = x[WET, k, OWN]
        out_t[k] = wet * (out_t[k] - HEAT_COEF * press)
        out_s[k] = wet * (out_s[k] + SALT_COEF * press)
        out_u[k] = we[k, OWN] * (out_u[k] + z0 * drag - (svt[OWN] + svt[15:63]) + acc[0])
        out_v[k] = wn[k, OWN] * (out_v[k] + m0 * drag + (sut[OWN] + sut[17:65]) + acc[1])
        return press

    lax.fori_loop(0, LEVELS, momentum_level, jnp.zeros((ROWS, LANES), F32))


def store_kernel(*refs):
    sources, targets, sem = refs[:5], refs[5:10], refs[10]
    copies = [pltpu.make_async_copy(a, b, sem.at[n]) for n, (a, b) in enumerate(zip(sources, targets))]
    for copy in copies:
        copy.start()
    for copy in copies:
        copy.wait()


def solution(mesh):
    nlon, nlat = mesh.shape["lon"], mesh.shape["lat"]
    inner = next(n for n in (8, 4, 2, 1) if nlat % n == 0 and n * n <= 2 * nlat)
    outer = nlat // inner
    deep = P(None, "lat", "lon")
    flat = P("lat", "lon")

    def step(*args):
        vm = lambda *shape: pltpu.VMEM(shape, F32)
        cube = jax.ShapeDtypeStruct((LEVELS, ROWS, LANES), F32)
        plane = jax.ShapeDtypeStruct((ROWS, LANES), F32)
        level = vm(LEVELS, TALL, LANES)
        copies = 7 + 10 + inner - 1 + 8 + 2 + 3 * (outer - 1)
        scratch = dict(
            x=vm(9, LEVELS, TALL, LANES), lm=pltpu.VMEM((LEVELS, ROWS, LANES), jnp.int32),
            bl=pltpu.VMEM((ROWS, LANES), jnp.int32), stv=vm(ROWS, LANES),
            c1=vm(3, ROWS, LANES), ce1=vm(ROWS, LANES), cw1=vm(ROWS, LANES), pw1=vm(80, LANES), pe1=vm(80, LANES),
            cl=vm(2, ROWS, LANES), pwl=vm(2, 80, LANES), pel=vm(2, 80, LANES), m1=vm(3, 80, LANES), mr=vm(80, LANES),
            rn=vm(9, 16, LANES), rs=vm(9, 16, LANES), got_s=vm(9, 16, LANES), got_n=vm(9, 16, LANES),
            tot=vm(8, LANES), inn=vm(2, 8, LANES), slot1=vm(max(inner - 1, 1), 8, LANES), gsum=vm(8, LANES),
            slot2=vm(max(3 * (outer - 1), 1), 8, LANES), inn_w=vm(2, 8, LANES), inn_e=vm(2, 8, LANES), sfx=vm(96, LANES),
            um0=level, umw=level, vm0=level, we=level, wew=level, wn=level, z1=level, z1w=level,
            mm1=level, mm1e=level, wne=level, tmp3=vm(TALL, LANES), sut=vm(TALL, LANES), svt=vm(TALL, LANES),
            acc=vm(8, ROWS, LANES), acx=vm(8, 64, LANES), ce2=vm(ROWS, LANES), cw2=vm(ROWS, LANES), pw2=vm(80, LANES),
            pe2=vm(80, LANES), m2=vm(2, 80, LANES), sa=vm(11, WIDE, LANES), sb=vm(11, 80, LANES),
            st=vm(3, 2, WIDE, LANES), ou2=vm(2, 2, 80, LANES), cd2=vm(2, 2, 80, LANES), wt2=vm(2, 80, LANES), wte=vm(2, 80, LANES),
            ff2=vm(2, 2, 80, LANES), ga=vm(SUBCYCLES, 2, 2, 80, LANES), gb=vm(SUBCYCLES, 2, 2, 80, LANES),
            fg=vm(2, 2, 80, LANES), tmpb=vm(2, WIDE, LANES), gg=vm(4, 64, LANES),
            in_sem=pltpu.SemaphoreType.DMA((13,)), send_sem=pltpu.SemaphoreType.DMA((copies,)),
            recv_sem=pltpu.SemaphoreType.DMA((copies,)),
            ready=pltpu.SemaphoreType.REGULAR((2,)),
        )

        def body(*refs):
            kernel(nlon, nlat, inner, *refs)

        parts = pl.pallas_call(
            body,
            out_shape=[cube, cube, cube, cube, plane],
            in_specs=[pl.BlockSpec(memory_space=pltpu.HBM)] * 13,
            out_specs=[pl.BlockSpec(memory_space=pltpu.VMEM)] * 5,
            scratch_shapes=list(scratch.values()),
            compiler_params=pltpu.CompilerParams(
                collective_id=0, has_side_effects=True, vmem_limit_bytes=40 * 1024 * 1024
            ),
        )(*(pltpu.with_memory_space_constraint(a, pltpu.HBM) for a in args))
        return pl.pallas_call(
            store_kernel,
            out_shape=[cube, cube, cube, cube, plane],
            in_specs=[pl.BlockSpec(memory_space=pltpu.VMEM)] * 5,
            out_specs=[pl.BlockSpec(memory_space=pltpu.HBM)] * 5,
            scratch_shapes=[pltpu.SemaphoreType.DMA((5,))],
            compiler_params=pltpu.CompilerParams(vmem_limit_bytes=4 * 1024 * 1024),
        )(*parts)

    specs = (deep, deep, deep, deep, flat, deep, flat, deep, deep, deep, deep, flat, flat)
    return jax.shard_map(
        step, mesh=mesh, in_specs=specs, out_specs=(deep, deep, deep, deep, flat), check_vma=False
    )
```
